32 devices in a mesh: seq: 8 (over z, core), hid: 4 (over y, x).
Axes of the slice: x: 2, y: 2, z: 4, core: 2. Of those that a mesh axis runs over, the one named last changes fastest.
Arguments:
- inputs: float32 [32768, 768], P(('seq', 'hid')), may hold values from -6 to 6
- mask_flags: int32 [32768], P(('seq', 'hid')), may hold values 0 or 1
- out_grad: float32 [16, 256, 1280], P('seq', 'hid'), may hold values from -6 to 6
- square: float32 [4, 1280, 1280], P(None, None, 'hid'), as said below
- square_state: float32 [3, 4, 1280, 1280], P(None, None, 'seq', 'hid'), as said below
- kv_weights: float32 [2, 768, 1280], P(None, None, 'hid'), may hold values from -0.21875 to 0.21875
- kv_state: float32 [3, 2, 768, 1280], P(None, None, 'seq', 'hid'), as said below
- latents: float32 [256, 1280], P('hid'), may hold values from -6 to 6
- latents_state: float32 [3, 256, 1280], P(None, 'hid', 'seq'), as said below
- in_params: float32 [3, 768], replicated, as said below
- in_state: float32 [3, 3, 768], replicated, as said below
- lat_params: float32 [4, 1280], replicated, as said below
- lat_state: float32 [3, 4, 1280], replicated, as said below
Outputs:
- latents_out: float32 [16, 256, 1280], P('seq', 'hid')
- inputs_grad: float32 [32768, 768], P(('seq', 'hid'))
- grad_norm: float32 [], replicated
- square_new: float32 [2, 4, 1280, 1280], P(None, None, 'seq', 'hid')
- square_moments: float32 [2, 4, 1280, 1280], P(None, None, 'seq', 'hid')
- kv_new: float32 [2, 2, 768, 1280], P(None, None, 'seq', 'hid')
- kv_moments: float32 [2, 2, 768, 1280], P(None, None, 'seq', 'hid')
- latents_new: float32 [2, 256, 1280], P(None, 'hid', 'seq')
- latents_moments: float32 [2, 256, 1280], P(None, 'hid', 'seq')
- in_new: float32 [2, 3, 768], replicated
- in_moments: float32 [2, 3, 768], replicated
- lat_new: float32 [2, 4, 1280], replicated
- lat_moments: float32 [2, 4, 1280], replicated
- in_grads_clipped: float32 [3, 768], replicated
- lat_grads_clipped: float32 [4, 1280], replicated
The draws below stay inside these ranges and needn't reach their ends.
Inputs may be any that keep to these rules, and one draw needn't show every extreme that they name: square: slot 1 is the output projection transposed, slot 3 the second feed-forward matrix transposed. `square_state`: slot 0 first moments of both signs, slot 1 positive roots of second moments, slot 2 averaged weights. `kv_state`: slot 0 first moments, slot 1 positive roots of second moments, slot 2 averaged weights. `latents_state`: slot 0 first moments, slot 1 positive roots of second moments, slot 2 averaged weights. `in_params`: gains near 1. `in_state`: slot 0 first moments, slot 1 positive roots of second moments, slot 2 averaged parameters. `lat_params`: gains near 1. `lat_state`: slot 0 first moments, slot 1 positive roots of second moments, slot 2 averaged parameters.
All inputs are finite; a program needn't handle non-finite values. No bound on the sum of `mask_flags` on one device may be relied on, other than what follows from the above.
Results may differ from the reference program's by a relative error of at most 0.015.
The reference program's roundings to bfloat16 on the way count: a program that leaves them out, or rounds other values in their place, can miss the bound.
Values may be sent and summed in bfloat16 or wider, within the bound.
No kernel may reach another device: no remote copies, remote signals or barrier semaphores. Data moves between devices by JAX's collectives and lax.ppermute only.
A program may use at most 128 MiB of HBM per device.

```python
import math
import jax
import jax.numpy as jnp
from jax import lax

D_IN = 768
D_LAT = 1280
NLAT = 256
HEADS = 8
HEAD = 160
SEQ_LEN = 2048
STEP = 10
SEQS = 16
TOKENS = 32768


def param_rows(key, shape, centres, spreads):
    noise_val = jnp.clip(jax.random.normal(key, shape, jnp.float32), -4.0, 4.0)
    lead_shape = (shape[0],) + (1,) * (len(shape) - 1)
    centre_col = jnp.asarray(centres, jnp.float32).reshape(lead_shape)
    spread_col = jnp.asarray(spreads, jnp.float32).reshape(lead_shape)
    return centre_col + noise_val * spread_col


def state_rows(key, shape, factors, centres, spreads):
    key_one, key_two, key_three = jax.random.split(key, 3)
    lead_shape = (shape[0],) + (1,) * (len(shape) - 1)
    grad_size = jnp.asarray(factors, jnp.float32).reshape(lead_shape) / (math.sqrt(2.0) * D_LAT)
    moment_one = jnp.clip(jax.random.normal(key_one, shape, jnp.float32), -4.0, 4.0) * grad_size * (0.1 / 0.9)
    spread_two = jnp.exp(jax.random.uniform(key_two, shape, jnp.float32, 0.0, math.log(4.0)))
    root_two = jnp.sqrt(spread_two) * grad_size * math.sqrt(0.001 / 0.999)
    average = param_rows(key_three, shape, centres, spreads)
    return jnp.stack([moment_one, root_two, average])


def square_scales():
    return [2.0 / math.sqrt(D_LAT), math.sqrt(32.0 / D_LAT), 1.0 / math.sqrt(D_LAT), math.sqrt(2.0 / D_LAT)]


def draw_square(key, part):
    return param_rows(jax.random.fold_in(key, 11), (4, D_LAT, D_LAT), [0.0, 0.0, 0.0, 0.0], square_scales())


def draw_square_state(key, part):
    return state_rows(jax.random.fold_in(key, 12), (4, D_LAT, D_LAT), [0.2, 0.3, 1.0, 1.0], [0.0, 0.0, 0.0, 0.0], square_scales())


def draw_kv_state(key, part):
    spread_kv = 1.0 / math.sqrt(D_IN)
    return state_rows(jax.random.fold_in(key, 13), (2, D_IN, D_LAT), [0.15, 0.15], [0.0, 0.0], [spread_kv, spread_kv])


def draw_latents_state(key, part):
    return state_rows(jax.random.fold_in(key, 14), (NLAT, D_LAT), [0.13] * NLAT, [0.0] * NLAT, [1.0] * NLAT)


def draw_in_params(key, part):
    return param_rows(jax.random.fold_in(key, 15), (3, D_IN), [1.0, 0.0, 0.0], [0.2, 0.5, 1.0])


def draw_in_state(key, part):
    return state_rows(jax.random.fold_in(key, 16), (3, D_IN), [0.2, 0.2, 0.08], [1.0, 0.0, 0.0], [0.2, 0.5, 1.0])


def draw_lat_params(key, part):
    return param_rows(jax.random.fold_in(key, 17), (4, D_LAT), [1.0, 0.0, 1.0, 0.0], [0.2, 0.5, 0.2, 0.5])


def draw_lat_state(key, part):
    return state_rows(jax.random.fold_in(key, 18), (4, D_LAT), [0.3, 0.3, 1.0, 1.0], [1.0, 0.0, 1.0, 0.0], [0.2, 0.5, 0.2, 0.5])


def set_ends(entries, own_key, low, largest):
    dims = entries.shape
    spot = [jax.random.randint(jax.random.fold_in(own_key, axis), (), 0, dims[axis]) for axis in range(len(dims))]
    entries = entries.at[tuple(spot)].set(low)
    longest = dims.index(max(dims))
    spot[longest] = (spot[longest] + 1) % dims[longest]
    return entries.at[tuple(spot)].set(largest)


def block_levels(stream_key, shape, shards, low, top_value):
    def one(axis_at, blocks):
        draws = jax.random.uniform(jax.random.fold_in(jax.random.fold_in(stream_key, 6), axis_at), (blocks,), jnp.float32, low / len(shards), top_value / len(shards))
        return jnp.repeat(jnp.exp(draws), shape[axis_at] // blocks).reshape((-1,) + (1,) * (len(shape) - axis_at - 1))

    factor_of = one(*shards[0])
    for cut in shards[1:]:
        factor_of = factor_of * one(*cut)
    return factor_of


def scatter_about(key, dims, deviation, reach, cuts=(), dtype=jnp.bfloat16):
    loudness = block_levels(key, dims, cuts, -0.22, 0.18) if cuts else 1.0
    entries = jax.random.normal(key, dims, jnp.float32) * deviation * loudness
    return jnp.minimum(jnp.maximum(entries, -reach), reach).astype(dtype)


def setup_inputs(seed: int = 0) -> dict:
    arg_keys = jax.random.split(jax.random.key(seed), 14)
    return {
        "inputs": scatter_about(arg_keys[0], (TOKENS, D_IN), 1.0, 6.0, ((0, 32),), jnp.float32),
        "mask_flags": set_ends((jax.random.randint(arg_keys[1], (TOKENS,), 0, 100) < 15).astype(jnp.int32), jax.random.fold_in(arg_keys[1], 1), 0, 1),
        "out_grad": scatter_about(arg_keys[2], (SEQS, NLAT, D_LAT), 1.0, 6.0, ((0, 8), (1, 4)), jnp.float32),
        "square": draw_square(jax.random.fold_in(arg_keys[13], 71), 0),
        "square_state": draw_square_state(jax.random.fold_in(arg_keys[13], 71), 0),
        "kv_weights": scatter_about(arg_keys[5], (2, D_IN, D_LAT), D_IN ** -0.5, 0.21875, ((2, 4),), jnp.float32),
        "kv_state": draw_kv_state(jax.random.fold_in(arg_keys[13], 71), 0),
        "latents": scatter_about(arg_keys[7], (NLAT, D_LAT), 1.0, 6.0, ((0, 4),), jnp.float32),
        "latents_state": draw_latents_state(jax.random.fold_in(arg_keys[13], 71), 0),
        "in_params": draw_in_params(jax.random.fold_in(arg_keys[13], 71), 0),
        "in_state": draw_in_state(jax.random.fold_in(arg_keys[13], 71), 0),
        "lat_params": draw_lat_params(jax.random.fold_in(arg_keys[13], 71), 0),
        "lat_state": draw_lat_state(jax.random.fold_in(arg_keys[13], 71), 0),
    }


clip_limit = 1.0
beta_one = 0.9
beta_two = 0.999
adam_eps = 1e-08
learn_rate = 0.05
decay_rate = 0.01
ema_keep = 0.9
norm_eps = 1e-05

@jax.custom_vjp
def low(v):
    return lax.optimization_barrier(v.astype(jnp.bfloat16)).astype(jnp.float32)

@jax.custom_vjp
def low_back(v):
    return v

def low_keep(v):
    return (low(v), None)

def low_pass(kept, grad):
    return (grad,)

def back_keep(v):
    return (v, None)

def back_low(kept, grad):
    return (low(grad),)
low.defvjp(low_keep, low_pass)
low_back.defvjp(back_keep, back_low)

def layer_norm(values, scale_row, shift_row):
    centre = lax.optimization_barrier(jnp.mean(values, -1, keepdims=True))
    centred = values - centre
    inverse = lax.rsqrt(lax.optimization_barrier(jnp.mean(centred * centred, -1, keepdims=True)) + norm_eps)
    return centred * inverse * scale_row + shift_row

def adamw(weight, states, gradient):
    moment_one = beta_one * states[0] + (1.0 - beta_one) * gradient
    root_two = jnp.sqrt(beta_two * states[1] * states[1] + (1.0 - beta_two) * gradient * gradient)
    corrected_one = moment_one / (1.0 - beta_one ** STEP)
    denominator = root_two / math.sqrt(1.0 - beta_two ** STEP) + adam_eps
    new_weight = weight - learn_rate * (corrected_one / denominator + decay_rate * weight)
    ema_new = ema_keep * states[2] + (1.0 - ema_keep) * new_weight
    return (jnp.stack([new_weight, ema_new]), jnp.stack([moment_one, root_two]))

def forward(square, kv_weights, latents, in_params, lat_params, inputs, mask_f):
    high = lax.Precision.HIGHEST
    w_sq = low(square)
    w_kv = low(kv_weights)
    masked = inputs * (1.0 - mask_f) + mask_f * in_params[2]
    normed = low(layer_norm(masked, in_params[0], in_params[1]))
    lat_low = low(layer_norm(latents, lat_params[0], lat_params[1]))
    query_raw = jnp.dot(lat_low, w_sq[0], precision=high)
    score_scale = 1.0 / math.sqrt(HEAD)

    def block_fn(row_block):
        key_rows = low(low_back(jnp.dot(row_block, w_kv[0], precision=high))).reshape(2, SEQ_LEN, HEADS, HEAD)
        value_rows = low(low_back(jnp.dot(row_block, w_kv[1], precision=high))).reshape(2, SEQ_LEN, HEADS, HEAD)
        query_rows = low(low_back(jnp.broadcast_to(query_raw, (2, NLAT, D_LAT)))).reshape(2, NLAT, HEADS, HEAD)
        raw_scores = low_back(jnp.einsum('blhe,bshe->bhls', query_rows, key_rows, precision=high) * score_scale)
        attn_probs = jax.nn.softmax(raw_scores, axis=-1)
        attended = jnp.einsum('bhls,bshe->blhe', low(attn_probs), value_rows, precision=high)
        attended = low(low_back(attended)).reshape(2, NLAT, D_LAT)
        branch = low_back(jnp.einsum('blc,dc->bld', attended, w_sq[1], precision=high))
        residual = latents[None] + branch
        mid_normed = low(layer_norm(residual, lat_params[2], lat_params[3]))
        up_proj = low_back(jnp.einsum('bld,dc->blc', mid_normed, w_sq[2], precision=high))
        hidden = low(jax.nn.gelu(up_proj, approximate=False))
        return residual + low_back(jnp.einsum('blc,dc->bld', hidden, w_sq[3], precision=high))
    blocks = normed.reshape(SEQS // 2, 2 * SEQ_LEN, D_IN)

    def scan_step(carry_in, row_block):
        return (carry_in, jax.checkpoint(block_fn)(row_block))
    _, block_outs = lax.scan(scan_step, jnp.zeros((), jnp.float32), blocks)
    return block_outs.reshape(SEQS, NLAT, D_LAT)

def reference(inputs, mask_flags, out_grad, square, square_state, kv_weights, kv_state, latents, latents_state, in_params, in_state, lat_params, lat_state):
    mask_f = mask_flags.astype(jnp.float32)[:, None]

    def forward_fn(sq_arg, kv_arg, lat_arg, in_arg, lp_arg, x_arg):
        return forward(sq_arg, kv_arg, lat_arg, in_arg, lp_arg, x_arg, mask_f)
    latents_out, pull_back = jax.vjp(forward_fn, square, kv_weights, latents, in_params, lat_params, inputs)
    g_sq, g_kv, g_lat, g_in, g_lp, inputs_grad = pull_back(out_grad)
    total = jnp.sum(g_sq * g_sq) + jnp.sum(g_kv * g_kv) + jnp.sum(g_lat * g_lat) + jnp.sum(g_in * g_in) + jnp.sum(g_lp * g_lp)
    grad_norm = jnp.sqrt(total)
    factor = jnp.minimum(1.0, clip_limit / (grad_norm + 1e-06))
    square_new, square_moments = adamw(square, square_state, g_sq * factor)
    kv_new, kv_moments = adamw(kv_weights, kv_state, g_kv * factor)
    latents_new, latents_moments = adamw(latents, latents_state, g_lat * factor)
    in_new, in_moments = adamw(in_params, in_state, g_in * factor)
    lat_new, lat_moments = adamw(lat_params, lat_state, g_lp * factor)
    return (latents_out, inputs_grad, grad_norm, square_new, square_moments, kv_new, kv_moments, latents_new, latents_moments, in_new, in_moments, lat_new, lat_moments, g_in * factor, g_lp * factor)
```

```python
from functools import partial
import math

import jax
import jax.numpy as jnp
from jax import lax
from jax.sharding import PartitionSpec as P

HEADS = 8
HEAD = 160
SEQ_LEN = 2048
STEP = 10


clip_limit = 1.0
beta_one = 0.9
beta_two = 0.999
adam_eps = 1e-08
learn_rate = 0.05
decay_rate = 0.01
ema_keep = 0.9
norm_eps = 1e-05

f32 = jnp.float32
bf16 = jnp.bfloat16


def norm_rows(values, scale_row, shift_row):
    centre = jnp.mean(values, -1, keepdims=True)
    centred = values - centre
    inverse = lax.rsqrt(jnp.mean(centred * centred, -1, keepdims=True) + norm_eps)
    unit_rows = centred * inverse
    return (unit_rows * scale_row + shift_row, unit_rows, inverse)


def norm_back(upstream, unit_rows, inverse, scale_row):
    scaled = upstream * scale_row
    inner_mean = jnp.mean(scaled, -1, keepdims=True)
    along_mean = jnp.mean(scaled * unit_rows, -1, keepdims=True)
    return inverse * (scaled - inner_mean - unit_rows * along_mean)


def adamw(weight, states, gradient):
    moment_one = beta_one * states[0] + (1.0 - beta_one) * gradient
    root_two = jnp.sqrt(beta_two * states[1] * states[1] + (1.0 - beta_two) * gradient * gradient)
    corrected_one = moment_one / (1.0 - beta_one**STEP)
    denominator = root_two / math.sqrt(1.0 - beta_two**STEP) + adam_eps
    new_weight = weight - learn_rate * (corrected_one / denominator + decay_rate * weight)
    ema_new = ema_keep * states[2] + (1.0 - ema_keep) * new_weight
    return (jnp.stack([new_weight, ema_new]), jnp.stack([moment_one, root_two]))


def flip(value, bits):
    out = 0
    for i in range(bits):
        out = out + ((value >> i) & 1) * (1 << (bits - 1 - i))
    return out


class Links:
    def __init__(self):
        self.S = lax.axis_size("seq")
        self.H = lax.axis_size("hid")
        self.hb = self.H.bit_length() - 1
        self.sb = self.S.bit_length() - 1
        self.s = lax.axis_index("seq")
        self.j = lax.axis_index("hid")
        self.core = self.s & 1

    def swap(self, x, dest):
        pairs = []
        for s in range(self.S):
            for j in range(self.H):
                ds, dj = dest(s, j)
                pairs.append((s * self.H + j, ds * self.H + dj))
        return lax.ppermute(x, ("seq", "hid"), pairs)

    def swap_core(self, x):
        return self.swap(x, lambda s, j: (s ^ 1, j))

    def swap_hid(self, x, mask):
        return self.swap(x, lambda s, j: (s, j ^ mask))

    def swap_seq(self, x, mask):
        return self.swap(x, lambda s, j: (s ^ mask, j))

    def swap_step(self, x, i):
        even, odd = 1 << i, 1 << (self.hb - 1 - i)
        return self.swap(x, lambda s, j: (s, j ^ (odd if s & 1 else even)))

    def slot(self, block, core):
        near = block ^ self.j
        return jnp.where(core == 0, near, flip(near, self.hb))

    def gather(self, half):
        buf = half[None]
        for i in range(self.hb):
            buf = jnp.concatenate([buf, self.swap_step(buf, i)], 0)
        return buf, self.swap_core(buf)

    def whole(self, half):
        mine, other = self.gather(half)
        mine = jnp.stack([lax.dynamic_index_in_dim(mine, self.slot(k, self.core), 0, False) for k in range(self.H)])
        other = jnp.stack([lax.dynamic_index_in_dim(other, self.slot(k, 1 - self.core), 0, False) for k in range(self.H)])
        even = self.core == 0
        return jnp.stack([jnp.where(even, mine, other), jnp.where(even, other, mine)], 1)

    def add(self, mine, other):
        if mine.dtype == f32:
            return mine + other
        return to_low(mine.astype(f32) + other.astype(f32))

    def pick(self, x, index, axis=0):
        return lax.dynamic_index_in_dim(x, index, axis, False)

    def scatter_cores(self, blocks):
        def ordered(core):
            return jnp.stack([self.pick(self.pick(blocks, self.unslot(r, core)), core) for r in range(self.H)])
        return self.add(ordered(self.core), self.swap_core(ordered(1 - self.core)))

    def unslot(self, r, core):
        return self.j ^ jnp.where(core == 0, r, flip(r, self.hb))

    def scatter_hid(self, buf):
        for i in reversed(range(self.hb)):
            n = 1 << i
            buf = self.add(buf[:n], self.swap_step(buf[n:], i))
        return buf[0]

    def scatter_seq(self, blocks):
        n = self.sb - 1
        chip = self.s >> 1
        buf = jnp.stack([self.pick(blocks, chip ^ flip(r, n)) for r in range(1 << n)])
        for i in reversed(range(n)):
            m = 1 << i
            buf = self.add(buf[:m], self.swap_seq(buf[m:], 2 << (n - 1 - i)))
        return buf[0]

    def sum_seq_chips(self, x):
        for i in range(1, self.sb):
            x = self.add(x, self.swap_seq(x, 1 << i))
        return x

    def sum_hid(self, x):
        for i in range(self.hb):
            x = self.add(x, self.swap_hid(x, 1 << i))
        return x

    def sum_all(self, x):
        x = self.add(x, self.swap_core(x))
        return self.sum_seq_chips(self.sum_hid(x))

    def both(self, half):
        other = self.swap_core(half)
        even = self.core == 0
        return jnp.stack([jnp.where(even, half, other), jnp.where(even, other, half)])


def cut(x):
    return lax.reduce_precision(x, 8, 7)


def to_low(x):
    return cut(x).astype(bf16)


def split3(x):
    a = cut(x)
    b = cut(x - a)
    c = cut(x - a - b)
    return jnp.stack([a, b, c]).astype(bf16)


def join3(x):
    x = x.astype(f32)
    return x[0] + x[1] + x[2]


def dot(a, b, dims):
    return lax.dot_general(a, b, (dims, ((), ())), preferred_element_type=f32)


def on_device(
    inputs,
    mask_flags,
    out_grad,
    square,
    square_state,
    kv_weights,
    kv_state,
    latents,
    latents_state,
    in_params,
    in_state,
    lat_params,
    lat_state,
):
    L = Links()
    S, H = L.S, L.H
    rows = inputs.shape[0]
    parts = SEQ_LEN // rows
    seqs = H // parts
    lat_rows = latents.shape[0]
    nlat = lat_rows * H
    d_lat = latents.shape[1]
    d_in = inputs.shape[1]
    wide = square.shape[2]
    half_wide = wide // 2
    score_scale = 1.0 / math.sqrt(HEAD)
    my_seq = L.j // parts

    lat_normed, lat_unit, lat_inverse = norm_rows(latents, lat_params[0], lat_params[1])
    lat_low = lat_normed.astype(bf16)
    lat_half = L.pick(lat_low.reshape(2, lat_rows // 2, d_lat), L.core)
    lat_all = L.whole(lat_half).reshape(nlat, d_lat)
    w_t = square.astype(bf16).transpose(0, 2, 1)
    query_here = dot(w_t[0], lat_all, ((1,), (1,))).astype(bf16)
    query_half = L.pick(query_here.reshape(2, half_wide, nlat), L.core)
    query_t = L.whole(query_half).reshape(d_lat, nlat)

    mask_f = mask_flags.astype(f32)[:, None]
    masked = inputs * (1.0 - mask_f) + mask_f * in_params[2]
    normed, in_unit, in_inverse = norm_rows(masked, in_params[0], in_params[1])
    in_low = normed.astype(bf16)
    kv_half = L.pick(kv_weights, L.core).astype(bf16).T
    kv_t = L.whole(kv_half)
    key_w = kv_t[:, 0].reshape(d_lat, d_in)
    value_w = kv_t[:, 1].reshape(d_lat, d_in)
    key_t = dot(key_w, in_low, ((1,), (1,))).astype(bf16)
    value_t = dot(value_w, in_low, ((1,), (1,))).astype(bf16)

    w_half = L.pick(w_t[1:].reshape(3, 2, half_wide, d_lat), L.core, 1)
    w_out = L.whole(w_half[0]).reshape(d_lat, d_lat)
    w_up = L.whole(w_half[1]).reshape(d_lat, d_lat)
    w_down = L.whole(w_half[2]).reshape(d_lat, d_lat)

    q_h = query_t.reshape(HEADS, HEAD, nlat)
    k_h = key_t.reshape(HEADS, HEAD, rows)
    v_h = value_t.reshape(HEADS, HEAD, rows)
    scores = jnp.einsum("heq,het->hqt", q_h, k_h, preferred_element_type=f32) * score_scale
    peak = jnp.max(scores, -1, keepdims=True)
    weight = jnp.exp(scores - peak)
    total = jnp.sum(weight, -1, keepdims=True)
    mix = jnp.einsum("hqt,het->qhe", weight.astype(bf16), v_h, preferred_element_type=f32)
    mix = mix / total[..., 0].T[..., None]
    log_part = (peak + jnp.log(total))[..., 0].T
    packed = jnp.concatenate(
        [
            mix.astype(bf16).reshape(nlat, d_lat),
            split3(log_part).transpose(1, 0, 2).reshape(nlat, 3 * HEADS),
            jnp.zeros((nlat, 128 - 3 * HEADS), bf16),
        ],
        1,
    ).reshape(H, lat_rows, d_lat + 128)
    got = [L.pick(packed, L.j)] + [L.swap_hid(L.pick(packed, L.j ^ m), m) for m in range(1, H)]
    got = jnp.stack(got)
    got = jnp.stack([L.pick(got, k ^ L.j) for k in range(H)]).reshape(seqs, parts, lat_rows, d_lat + 128)
    logs = join3(got[..., d_lat : d_lat + 3 * HEADS].reshape(seqs, parts, lat_rows, 3, HEADS).transpose(3, 0, 1, 2, 4))
    log_total = jax.nn.logsumexp(logs, axis=1)
    share = jnp.exp(logs - log_total[:, None])
    att = jnp.sum(
        got[..., :d_lat].astype(f32).reshape(seqs, parts, lat_rows, HEADS, HEAD) * share[..., None], 1
    )
    attended = att.astype(bf16).reshape(seqs * lat_rows, d_lat)

    grad_rows = out_grad.reshape(seqs * lat_rows, d_lat)
    branch = dot(attended, w_out, ((1,), (0,)))
    residual = (latents[None] + branch.reshape(seqs, lat_rows, d_lat)).reshape(seqs * lat_rows, d_lat)
    mid_normed, mid_unit, mid_inverse = norm_rows(residual, lat_params[2], lat_params[3])
    mid_low = mid_normed.astype(bf16)
    up_proj = dot(mid_low, w_up, ((1,), (1,)))
    gelu_exact = partial(jax.nn.gelu, approximate=False)
    hidden_f, gelu_pull = jax.vjp(gelu_exact, up_proj)
    hidden = hidden_f.astype(bf16)
    latents_out = (residual + dot(hidden, w_down, ((1,), (0,)))).reshape(seqs, lat_rows, d_lat)
    grad_y = grad_rows.astype(bf16)
    grad_hidden = dot(grad_y, w_down, ((1,), (1,)))
    up_grad = gelu_pull(grad_hidden)[0].astype(bf16)
    grad_mid = dot(up_grad, w_up, ((1,), (0,)))
    grad_residual = grad_rows + norm_back(grad_mid, mid_unit, mid_inverse, lat_params[2])
    branch_grad = grad_residual.astype(bf16)
    grad_att = dot(branch_grad, w_out, ((1,), (1,))).astype(bf16)
    inner = jnp.sum(
        grad_att.astype(f32).reshape(seqs, lat_rows, HEADS, HEAD) * att, -1
    )
    packed_back = jnp.concatenate(
        [
            grad_att.reshape(seqs, lat_rows, d_lat),
            split3(log_total).transpose(1, 2, 0, 3).reshape(seqs, lat_rows, 3 * HEADS),
            split3(inner).transpose(1, 2, 0, 3).reshape(seqs, lat_rows, 3 * HEADS),
            jnp.zeros((seqs, lat_rows, 128 - 6 * HEADS), bf16),
        ],
        2,
    )
    back = [L.pick(packed_back, my_seq)] + [
        L.swap_hid(L.pick(packed_back, (L.j ^ m) // parts), m) for m in range(1, H)
    ]
    back = jnp.stack(back)
    back = jnp.stack([L.pick(back, k ^ L.j) for k in range(H)]).reshape(nlat, d_lat + 128)
    gatt = back[:, :d_lat].reshape(nlat, HEADS, HEAD)
    logs_all = join3(back[:, d_lat : d_lat + 3 * HEADS].reshape(nlat, 3, HEADS).transpose(1, 2, 0))[..., None]
    inner_all = join3(back[:, d_lat + 3 * HEADS : d_lat + 6 * HEADS].reshape(nlat, 3, HEADS).transpose(1, 2, 0))[..., None]

    def outer(a, b):
        return dot(a, b, ((0,), (0,))).astype(bf16).reshape(H, 2, half_wide, d_lat)
    sq_blocks = jnp.stack([outer(attended, branch_grad), outer(up_grad, mid_low), outer(hidden, grad_y)], 2)
    sq_half = L.scatter_hid(L.scatter_cores(sq_blocks))
    d_part = d_lat // S
    sq_half = sq_half.reshape(3 * half_wide, d_lat).T.reshape(S // 2, 2, d_part, 3 * half_wide)
    sq_half = L.scatter_seq(sq_half)
    sq_mine = L.pick(sq_half, L.core)
    sq_other = L.swap_core(L.pick(sq_half, 1 - L.core))
    even = L.core == 0
    sq_tail = jnp.concatenate(
        [
            jnp.where(even, sq_mine, sq_other).reshape(d_part, 3, half_wide),
            jnp.where(even, sq_other, sq_mine).reshape(d_part, 3, half_wide),
        ],
        2,
    ).transpose(1, 0, 2).astype(f32)

    scores_b = jnp.einsum("heq,het->hqt", q_h, k_h, preferred_element_type=f32) * score_scale
    probs = jnp.exp(scores_b - logs_all)
    grad_v = jnp.einsum("hqt,qhe->het", probs.astype(bf16), gatt, preferred_element_type=f32).astype(bf16)
    grad_probs = jnp.einsum("qhe,het->hqt", gatt, v_h, preferred_element_type=f32)
    grad_scores = (probs * (grad_probs - inner_all)).astype(bf16)
    grad_q = (jnp.einsum("hqt,het->heq", grad_scores, k_h, preferred_element_type=f32) * score_scale).astype(bf16)
    grad_k = (jnp.einsum("heq,hqt->het", q_h, grad_scores, preferred_element_type=f32) * score_scale).astype(bf16)
    grad_v = grad_v.reshape(d_lat, rows)
    grad_k = grad_k.reshape(d_lat, rows)

    kv_blocks = jnp.stack(
        [
            dot(grad_k, in_low, ((1,), (0,))).astype(bf16).reshape(H, wide, d_in),
            dot(grad_v, in_low, ((1,), (0,))).astype(bf16).reshape(H, wide, d_in),
        ],
        1,
    )
    kv_half_grad = L.scatter_hid(L.scatter_cores(kv_blocks))
    in_part = d_in // S
    kv_half_grad = L.scatter_seq(kv_half_grad.T.reshape(S // 2, 2, in_part, wide))
    kv_mine = L.pick(kv_half_grad, L.core)
    kv_other = L.swap_core(L.pick(kv_half_grad, 1 - L.core))
    kv_part = jnp.stack([jnp.where(even, kv_mine, kv_other), jnp.where(even, kv_other, kv_mine)]).astype(f32)

    grad_normed = dot(grad_k, key_w, ((0,), (0,))) + dot(grad_v, value_w, ((0,), (0,)))
    grad_masked = norm_back(grad_normed, in_unit, in_inverse, in_params[0])
    inputs_grad = grad_masked * (1.0 - mask_f)
    in_small = jnp.stack(
        [
            jnp.sum(grad_normed * in_unit, 0),
            jnp.sum(grad_normed, 0),
            jnp.sum(grad_masked * mask_f, 0),
        ]
    )
    in_small = L.sum_all(in_small)

    gq_half = L.scatter_hid(L.scatter_cores(grad_q.reshape(H, 2, half_wide, nlat)))
    gq_here = L.both(L.sum_seq_chips(gq_half)).reshape(wide, nlat)
    lat_cols = lax.dynamic_slice_in_dim(lat_all, L.s * d_part, d_part, 1)
    wq_part = dot(lat_cols, gq_here, ((0,), (1,)))
    lat_term = dot(gq_here, w_t[0], ((0,), (0,))).astype(bf16).reshape(H, 2, lat_rows // 2, d_lat)
    lat_term = jnp.stack([L.pick(L.pick(lat_term, L.unslot(r, L.core)), L.core) for r in range(H)])
    grad_lat_low = L.both(L.scatter_hid(lat_term)).reshape(lat_rows, d_lat).astype(f32)
    lat_small_q = L.sum_hid(jnp.stack([jnp.sum(grad_lat_low * lat_unit, 0), jnp.sum(grad_lat_low, 0)]))
    lat_small_m = L.sum_all(jnp.stack([jnp.sum(grad_mid * mid_unit, 0), jnp.sum(grad_mid, 0)]))
    lat_small = jnp.concatenate([lat_small_q, lat_small_m], 0)
    res_sum = to_low(jnp.sum(grad_residual.reshape(seqs, lat_rows, d_lat), 0))
    res_sum = L.sum_seq_chips(L.add(res_sum, L.swap_core(res_sum))).astype(f32)
    grad_lat = res_sum + norm_back(grad_lat_low, lat_unit, lat_inverse, lat_params[0])
    lat_part = lax.dynamic_slice_in_dim(grad_lat, L.s * d_part, d_part, 1)

    sq_part = jnp.concatenate([wq_part[None], sq_tail], 0)
    big_sum = jnp.sum(sq_part * sq_part) + jnp.sum(kv_part * kv_part) + jnp.sum(lat_part * lat_part)
    big_sum = L.sum_all(jnp.broadcast_to(big_sum, (8, 128)))[0, 0]
    grad_norm = jnp.sqrt(big_sum + jnp.sum(in_small * in_small) + jnp.sum(lat_small * lat_small))
    factor = jnp.minimum(1.0, clip_limit / (grad_norm + 1e-06))
    in_part_rows = d_in // S
    sq_old = lax.dynamic_slice_in_dim(square, L.s * d_part, d_part, 1)
    kv_old = lax.dynamic_slice_in_dim(kv_weights, L.s * in_part_rows, in_part_rows, 1)
    lat_old = lax.dynamic_slice_in_dim(latents, L.s * d_part, d_part, 1)
    square_new, square_moments = adamw(sq_old, square_state, sq_part * factor)
    kv_new, kv_moments = adamw(kv_old, kv_state, kv_part * factor)
    latents_new, latents_moments = adamw(lat_old, latents_state, lat_part * factor)
    in_clipped = in_small * factor
    lat_clipped = lat_small * factor
    in_new, in_moments = adamw(in_params, in_state, in_clipped)
    lat_new, lat_moments = adamw(lat_params, lat_state, lat_clipped)
    return (
        latents_out,
        inputs_grad,
        grad_norm,
        square_new,
        square_moments,
        kv_new,
        kv_moments,
        latents_new,
        latents_moments,
        in_new,
        in_moments,
        lat_new,
        lat_moments,
        in_clipped,
        lat_clipped,
    )


def solution(mesh):
    return jax.shard_map(
        on_device,
        mesh=mesh,
        in_specs=(
            P(("seq", "hid"), None),
            P(("seq", "hid")),
            P("seq", "hid", None),
            P(None, None, "hid"),
            P(None, None, "seq", "hid"),
            P(None, None, "hid"),
            P(None, None, "seq", "hid"),
            P("hid", None),
            P(None, "hid", "seq"),
            P(),
            P(),
            P(),
            P(),
        ),
        out_specs=(
            P("seq", "hid", None),
            P(("seq", "hid"), None),
            P(),
            P(None, None, "seq", "hid"),
            P(None, None, "seq", "hid"),
            P(None, None, "seq", "hid"),
            P(None, None, "seq", "hid"),
            P(None, "hid", "seq"),
            P(None, "hid", "seq"),
            P(),
            P(),
            P(),
            P(),
            P(),
            P(),
        ),
        check_vma=False,
    )
```

```python
from functools import partial as fix
import math

import jax
import jax.numpy as jnp
from jax import lax
from jax.experimental import pallas as pl
from jax.experimental.pallas import tpu as pltpu
from jax.sharding import PartitionSpec as P

HEADS = 8
HEAD = 160
SEQ_LEN = 2048
STEP = 10
SIDE = 128


clip_limit = 1.0
beta_one = 0.9
beta_two = 0.999
adam_eps = 1e-08
learn_rate = 0.05
decay_rate = 0.01
ema_keep = 0.9
norm_eps = 1e-05
score_scale = 1.0 / math.sqrt(HEAD)
score_two = score_scale * math.log2(math.e)

f32 = jnp.float32
bf16 = jnp.bfloat16


def unit_norm(values):
    centre = jnp.mean(values, -1, keepdims=True)
    centred = values - centre
    inverse = lax.rsqrt(jnp.mean(centred * centred, -1, keepdims=True) + norm_eps)
    return centred * inverse, inverse


def norm_back(upstream, unit_rows, inverse, scale_row):
    scaled = upstream * scale_row
    inner_mean = jnp.mean(scaled, -1, keepdims=True)
    along_mean = jnp.mean(scaled * unit_rows, -1, keepdims=True)
    return inverse * (scaled - inner_mean - unit_rows * along_mean)


def adam_step(weight, first, root, average, gradient):
    moment_one = beta_one * first + (1.0 - beta_one) * gradient
    root_two = jnp.sqrt(beta_two * root * root + (1.0 - beta_two) * gradient * gradient)
    corrected_one = moment_one / (1.0 - beta_one**STEP)
    denominator = root_two / math.sqrt(1.0 - beta_two**STEP) + adam_eps
    new_weight = weight - learn_rate * (corrected_one / denominator + decay_rate * weight)
    ema_new = ema_keep * average + (1.0 - ema_keep) * new_weight
    return new_weight, ema_new, moment_one, root_two


def dot(a, b, over_a, over_b):
    return lax.dot_general(a, b, (((over_a,), (over_b,)), ((), ())), preferred_element_type=f32)


def flip(value, bits):
    out = 0
    for i in range(bits):
        out = out + ((value >> i) & 1) * (1 << (bits - 1 - i))
    return out


class Links:
    def __init__(self):
        self.S = lax.axis_size("seq")
        self.H = lax.axis_size("hid")
        self.hb = self.H.bit_length() - 1
        self.sb = self.S.bit_length() - 1
        self.s = lax.axis_index("seq")
        self.j = lax.axis_index("hid")
        self.core = self.s & 1

    def swap(self, x, dest):
        pairs = []
        for s in range(self.S):
            for j in range(self.H):
                ds, dj = dest(s, j)
                pairs.append((s * self.H + j, ds * self.H + dj))
        return lax.ppermute(x, ("seq", "hid"), pairs)

    def swap_core(self, x):
        return self.swap(x, lambda s, j: (s ^ 1, j))

    def swap_hid(self, x, mask):
        return self.swap(x, lambda s, j: (s, j ^ mask))

    def swap_seq(self, x, mask):
        return self.swap(x, lambda s, j: (s ^ mask, j))

    def swap_step(self, x, i):
        even, odd = 1 << i, 1 << (self.hb - 1 - i)
        return self.swap(x, lambda s, j: (s, j ^ (odd if s & 1 else even)))

    def spread(self, first):
        blocks = [None]
        for i, x in enumerate(first):
            blocks += [x] + [self.swap_step(y, i) for y in blocks[1:]]
        return blocks[1:]

    def near(self, x):
        return [self.swap_hid(x, m) for m in range(1, self.H)]

    def sum_all(self, x):
        x = x + self.swap_core(x)
        for i in range(self.hb):
            x = x + self.swap_hid(x, 1 << i)
        for i in range(1, self.sb):
            x = x + self.swap_seq(x, 1 << i)
        return x


class Place:
    def __init__(self, where, H):
        self.H = H
        self.hb = H.bit_length() - 1
        self.s = where[0]
        self.j = where[1]
        self.core = self.s & 1

    def block(self, r, core):
        return self.j ^ jnp.where(core == 0, r, flip(r, self.hb))

    def halves(self):
        mine = [(self.block(r, self.core), self.core) for r in range(self.H)]
        return mine + [(self.block(r, 1 - self.core), 1 - self.core) for r in range(self.H)]


def after(x, *others):
    return lax.optimization_barrier((x, others))[0]


def rows_at(index, size):
    return pl.ds(pl.multiple_of(index * size, size), size)


VMEM = pl.BlockSpec(memory_space=pltpu.VMEM)
SMEM = pl.BlockSpec(memory_space=pltpu.SMEM)
ANY = pl.BlockSpec(memory_space=pl.ANY)


spent = {
    "kv_weight": 2.6,
    "token_norm": 5.0,
    "other_weights": 4.7,
    "kv": 10.0,
    "attention": 8.0,
    "latent": 11.0,
    "square_send": 5.0,
    "square_keep": 5.0,
    "square_top": 6.0,
    "square_step": 4.0,
    "square_turn": 4.0,
    "attention_back": 12.0,
    "kv_send": 6.5,
    "kv_keep": 6.5,
    "token_grad": 4.0,
    "update": 7.0,
}


class Order:
    def __init__(self, where):
        self.where = where
        self.last = []

    def __call__(
        self, kernel, args, outs, scratch=(), name=None, grid=(), in_specs=None, out_specs=None, after=(), onto=None
    ):
        n = len(args)
        waits = self.last + list(after)
        if onto is not None:
            waits = [onto] + waits

        def body(where, *refs):
            kernel(where, *refs[:n], *refs[n + len(waits) :])

        results = pl.pallas_call(
            body,
            out_shape=outs,
            grid=grid,
            in_specs=[SMEM] + (in_specs or [VMEM] * n) + [ANY] * len(waits),
            out_specs=out_specs or [VMEM] * len(outs),
            scratch_shapes=list(scratch),
            compiler_params=pltpu.CompilerParams(vmem_limit_bytes=56 * 1024 * 1024),
            cost_estimate=pl.CostEstimate(
                flops=int(spent.get(name, 2.0) * 3e9), bytes_accessed=0, transcendentals=0
            ),
            name=name,
            input_output_aliases={} if onto is None else {1 + n: 0},
        )(self.where, *args, *waits)
        self.last = [results[0]]
        return results

    def add(self, terms, block, count, name):
        shape = terms[0].shape[1:]
        parts = shape[0] if len(shape) == 3 else 1
        terms = [x.reshape((x.shape[0], parts) + shape[-2:]) for x in terms]

        def kernel(where, *refs):
            out = refs[-1]
            acc = refs[0][...].astype(f32)
            for x in refs[1:-1]:
                acc = acc + x[...].astype(f32)
            out[...] = acc.astype(bf16)

        size = (1, 1) + shape[-2:]
        (out,) = self(
            kernel,
            terms,
            [like((count, parts) + shape[-2:], bf16)],
            name=name,
            grid=(count, parts),
            in_specs=[pl.BlockSpec(size, lambda i, m: (block * count + i, m, 0, 0))] * len(terms),
            out_specs=[pl.BlockSpec(size, lambda i, m: (i, m, 0, 0))],
        )
        return out.reshape((count,) + shape)


def like(shape, dtype):
    return jax.ShapeDtypeStruct(tuple(shape), dtype)


class Halving:
    def __init__(self, go, top, low, bits, swap, name):
        self.go, self.top, self.terms, self.bits, self.swap, self.name = go, top, low, bits, swap, name

    def start(self):
        i = self.bits - 1
        sending = self.top[0] if len(self.top) == 1 else self.go.add(self.top, 0, 1 << i, self.name + "_top")
        self.terms = self.terms + [self.swap(sending, i)]
        self.at = i

    def step(self):
        n = 1 << (self.at - 1)
        sending = self.go.add(self.terms, 1, n, self.name + "_step")
        self.at -= 1
        self.terms = self.terms + [self.swap(sending, self.at)]


def lat_kernel(where, latents, lat_params, out):
    unit, _ = unit_norm(latents[...])
    out[...] = (unit * lat_params[0:1, :] + lat_params[1:2, :]).astype(bf16)


def kv_weight_kernel(H, where, kv, mine, other):
    at = Place(where, H)
    mine[...] = kv[at.core].astype(bf16)
    other[...] = kv[1 - at.core].astype(bf16)


def first_weight_kernel(where, weight, out):
    out[...] = weight[0].astype(bf16)


def other_weight_kernel(H, where, weight, mine, other):
    at = Place(where, H)
    n = mine.shape[1]
    mine[0] = weight[0, rows_at(at.core, n), :].astype(bf16)
    other[0] = weight[0, rows_at(1 - at.core, n), :].astype(bf16)


def query_kernel(H, where, *refs):
    near, (w0, lat_all, mine, other, turned) = refs[:H], refs[H:]
    at = Place(where, H)
    n = near[0].shape[0]
    for m, x in enumerate(near):
        lat_all[rows_at(at.j ^ m, n), :] = x[...]
    turned[...] = dot(w0[...], lat_all[...], 1, 1).astype(bf16)
    half_wide = mine.shape[0]
    mine[...] = turned[rows_at(at.core, half_wide), :]
    other[...] = turned[rows_at(1 - at.core, half_wide), :]


def token_kernel(where, inputs, mask, in_params, out, turned):
    masked = jnp.where(mask[...] > 0, in_params[2:3, :], inputs[...])
    unit, _ = unit_norm(masked)
    low = (unit * in_params[0:1, :] + in_params[1:2, :]).astype(bf16)
    out[...] = low
    turned[...] = low.T


def kv_kernel(H, where, in_turned, *refs):
    halves, (kv, weights, sems) = refs[: 2 * H], refs[2 * H :]
    at = Place(where, H)
    wide = halves[0].shape[0]
    d_lat = wide * H
    copies = []
    for i, (block, which) in enumerate(at.halves()):
        copies.append(pltpu.make_async_copy(halves[i], weights.at[which, rows_at(block, wide), :], sems.at[i]))
        copies[-1].start()
    for copy in copies:
        copy.wait()
    for which in range(2):
        kv[which] = dot(weights[which], in_turned[...], 1, 0).astype(bf16)


def three_way(x, lane):
    a = x.astype(bf16).astype(f32)
    b = (x - a).astype(bf16).astype(f32)
    part = (lane // HEADS) % 3
    return jnp.where(part == 0, a, jnp.where(part == 1, b, x - a - b)).astype(bf16)


def three_sum(x):
    return x + pltpu.roll(x, SIDE - HEADS, 1) + pltpu.roll(x, SIDE - 2 * HEADS, 1)


def attention_kernel(H, where, *refs):
    halves, kv, query = refs[: 2 * H], refs[2 * H], refs[2 * H + 1]
    packs, mix, packed = refs[2 * H + 2 : -2], refs[-2], refs[-1]
    at = Place(where, H)
    n = halves[0].shape[0]
    for i, x in enumerate(halves):
        half = at.core if i < H else 1 - at.core
        query[rows_at((at.j ^ (i % H)) * 2 + half, n), :] = x[...]
    d_lat, nlat = query.shape
    lane = lax.broadcasted_iota(jnp.int32, (nlat, SIDE), 1)
    logs = jnp.zeros((nlat, SIDE), f32)
    for h in range(HEADS):
        span = slice(h * HEAD, (h + 1) * HEAD)
        scores = dot(query[span, :], kv[0, span, :], 0, 0)
        peak = jnp.max(scores, -1, keepdims=True)
        weight = jnp.exp2((scores - peak) * score_two)
        total = jnp.sum(weight, -1, keepdims=True)
        probs = (weight * (1.0 / total)).astype(bf16)
        mix[span, :] = dot(kv[1, span, :], probs, 1, 1)
        log_part = peak * score_two + jnp.log2(total)
        logs = jnp.where((lane % HEADS == h) & (lane < 3 * HEADS), log_part, logs)
    packed[:, :d_lat] = mix[...].T.astype(bf16)
    packed[:, d_lat:] = three_way(logs, lane)
    lat_rows = nlat // H
    for m, out in enumerate(packs):
        out[...] = packed[rows_at(at.j ^ m, lat_rows), :]


def head_lanes(shape):
    return lax.broadcasted_iota(jnp.int32, shape, 1) // HEAD


def latent_kernel(H, parts, where, *refs):
    seqs = H // parts
    got, refs = refs[:H], refs[H:]
    latents, out_grad, lat_params, refs = refs[0], refs[1], refs[2], refs[3:]
    pieces, refs = refs[: 2 * H], refs[2 * H :]
    (latents_out, attended, branch_grad, up_grad, mid_low, hidden, grad_y, small, res_sum), refs = refs[:9], refs[9:]
    backs, (weights, sems, gathered, att, packed) = refs[:H], refs[H:]
    at = Place(where, H)
    lat_rows, d_lat = latents.shape
    half_wide = pieces[0].shape[1]
    copies = []
    for m in range(3):
        group = []
        for i, (block, half) in enumerate(at.halves()):
            group.append(
                pltpu.make_async_copy(
                    pieces[i].at[m],
                    weights.at[m, rows_at(block * 2 + half, half_wide), :],
                    sems.at[m, i],
                )
            )
            group[-1].start()
        copies.append(group)

    def arrived(m):
        for copy in copies[m]:
            copy.wait()

    for m in range(H):
        gathered[at.j ^ m] = got[m][...]
    heads = head_lanes((lat_rows, d_lat))
    log_totals = []
    for b in range(seqs):
        logs = [three_sum(gathered[b * parts + p, :, d_lat:].astype(f32)) for p in range(parts)]
        peak = logs[0]
        for x in logs[1:]:
            peak = jnp.maximum(peak, x)
        log_total = peak + jnp.log2(sum(jnp.exp2(x - peak) for x in logs))
        log_totals.append(log_total)
        mixed = jnp.zeros((lat_rows, d_lat), f32)
        for p in range(parts):
            share = jnp.exp2(logs[p] - log_total)
            spread = jnp.zeros((lat_rows, d_lat), f32)
            for h in range(HEADS):
                spread = jnp.where(heads == h, share[:, h : h + 1], spread)
            mixed = mixed + spread * gathered[b * parts + p, :, :d_lat].astype(f32)
        att[b * lat_rows : (b + 1) * lat_rows, :] = mixed
    attended[...] = att[...].astype(bf16)
    grad_y[...] = jnp.concatenate([out_grad[b] for b in range(seqs)], 0).astype(bf16)

    arrived(0)
    branch = dot(attended[...], weights[0], 1, 0)
    residual = jnp.concatenate([latents[...]] * seqs, 0) + branch
    unit, inverse = unit_norm(residual)
    mid_low[...] = (unit * lat_params[2:3, :] + lat_params[3:4, :]).astype(bf16)
    arrived(1)
    up_proj = dot(mid_low[...], weights[1], 1, 1)
    below = 0.5 + 0.5 * lax.erf(up_proj * math.sqrt(0.5))
    hidden[...] = (up_proj * below).astype(bf16)
    slope = below + up_proj * jnp.exp(-0.5 * up_proj * up_proj) * (1.0 / math.sqrt(2.0 * math.pi))
    arrived(2)
    latents_out[...] = residual + dot(hidden[...], weights[2], 1, 0)
    up_grad[...] = (dot(grad_y[...], weights[2], 1, 1) * slope).astype(bf16)
    grad_mid = dot(up_grad[...], weights[1], 1, 0)
    small[0:1, :] = jnp.sum(grad_mid * unit, 0, keepdims=True)
    small[1:2, :] = jnp.sum(grad_mid, 0, keepdims=True)
    grad_residual = jnp.concatenate([out_grad[b] for b in range(seqs)], 0) + norm_back(
        grad_mid, unit, inverse, lat_params[2:3, :]
    )
    branch_grad[...] = grad_residual.astype(bf16)
    folded = grad_residual[0:lat_rows]
    for b in range(1, seqs):
        folded = folded + grad_residual[b * lat_rows : (b + 1) * lat_rows]
    res_sum[...] = folded.astype(bf16)
    grad_att = dot(branch_grad[...], weights[0], 1, 1).astype(bf16)
    along = grad_att.astype(f32) * att[...]
    heads = head_lanes((seqs * lat_rows, d_lat))
    lane = lax.broadcasted_iota(jnp.int32, (lat_rows, SIDE), 1)
    inner = []
    for h in range(HEADS):
        lo, hi = h * HEAD // 128 * 128, -(-(h + 1) * HEAD // 128) * 128
        inner.append(jnp.sum(jnp.where(heads[:, lo:hi] == h, along[:, lo:hi], 0.0), -1, keepdims=True))
    for b in range(seqs):
        t = log_totals[b]
        side = jnp.where(lane < HEADS, t, jnp.where(lane < 2 * HEADS, pltpu.roll(t, HEADS, 1), pltpu.roll(t, 2 * HEADS, 1)))
        for h in range(HEADS):
            own = (lane % HEADS == h) & (lane >= 3 * HEADS)
            side = jnp.where(own, inner[h][b * lat_rows : (b + 1) * lat_rows], side)
        side = jnp.where(lane < 6 * HEADS, side, 0.0)
        packed[b, :, :d_lat] = grad_att[b * lat_rows : (b + 1) * lat_rows]
        packed[b, :, d_lat:] = three_way(side, lane)
    for m, out in enumerate(backs):
        out[...] = packed[(at.j ^ m) // parts]


def square_grad_kernel(H, keep, where, *refs):
    lefts, rights = refs[:3], refs[3:6]
    top, low, turned = refs[6:]
    at = Place(where, H)
    core = at.core if keep else 1 - at.core
    for m in range(3):
        turned[m] = lefts[m][...].T
    half_wide = top.shape[2]
    for r in range(H):
        out = low if r < H // 2 else top
        at_row = rows_at(at.block(r, core) * 2 + core, half_wide)
        for m in range(3):
            out[r % (H // 2), m] = dot(turned[m, at_row, :], rights[m][...], 1, 0).astype(bf16)


def attention_back_kernel(H, where, query, kv, *refs):
    backs, refs = refs[:H], refs[H:]
    grad_kv, send_top, send_low, keep_top, keep_low, packed, turned, grad_q = refs
    at = Place(where, H)
    d_lat, nlat = query.shape
    lat_rows = nlat // H
    for m in range(H):
        packed[rows_at(at.j ^ m, lat_rows), :] = backs[m][...]
    turned[...] = packed[:, :d_lat].T
    side = three_sum(packed[:, d_lat:].astype(f32))
    for h in range(HEADS):
        span = slice(h * HEAD, (h + 1) * HEAD)
        scores = dot(query[span, :], kv[0, span, :], 0, 0)
        probs = jnp.exp2(scores * score_two - side[:, h : h + 1])
        grad_kv[1, span, :] = dot(turned[span, :], probs.astype(bf16), 1, 0).astype(bf16)
        grad_probs = dot(turned[span, :], kv[1, span, :], 0, 0)
        grad_scores = (probs * (grad_probs - side[:, 3 * HEADS + h : 3 * HEADS + h + 1])).astype(bf16)
        grad_q[span, :] = (dot(kv[0, span, :], grad_scores, 1, 1) * score_scale).astype(bf16)
        grad_kv[0, span, :] = (dot(query[span, :], grad_scores, 1, 0) * score_scale).astype(bf16)
    slots_out(at, 1 - at.core, grad_q, send_top, send_low)
    slots_out(at, at.core, grad_q, keep_top, keep_low)


def slots_out(at, core, whole, top, low):
    n = top.shape[1]
    per = whole.shape[0] // (at.H * n)
    for r in range(at.H):
        out = low if r < at.H // 2 else top
        block = at.block(r, core)
        out[r % (at.H // 2)] = whole[rows_at(block * 2 + core if per == 2 else block, n), :]


def kv_grad_kernel(H, keep, where, grad_kv, in_low, top, low, whole):
    at = Place(where, H)
    core = at.core if keep else 1 - at.core
    whole[...] = dot(grad_kv[core], in_low[...], 1, 0).astype(bf16)
    slots_out(at, core, whole, top, low)


def token_grad_kernel(where, inputs, mask, in_params, grad_kv, weights, inputs_grad, small, normed):
    normed[...] = dot(grad_kv[0], weights[0], 0, 0) + dot(grad_kv[1], weights[1], 0, 0)
    rows, d_in = inputs.shape
    step = min(rows, 128)
    small[...] = jnp.zeros_like(small)
    for i in range(rows // step):
        span = slice(i * step, (i + 1) * step)
        masked_row = mask[span, :] > 0
        unit, inverse = unit_norm(jnp.where(masked_row, in_params[2:3, :], inputs[span, :]))
        upstream = normed[span, :]
        grad = norm_back(upstream, unit, inverse, in_params[0:1, :])
        inputs_grad[span, :] = jnp.where(masked_row, 0.0, grad)
        for r, term in enumerate((upstream * unit, upstream, jnp.where(masked_row, grad, 0.0))):
            small[0, r : r + 1, :] += jnp.sum(term, 0, keepdims=True)


def turn(where, total, turned, top, low):
    turned[...] = total[...].T.astype(bf16)
    chip = where[0] >> 1
    half, rows, lanes = top.shape
    for r in range(2 * half):
        out = low if r < half else top
        out[r % half] = turned[rows_at(chip ^ flip(r, half.bit_length()), rows), 0:lanes]


def square_turn_kernel(where, *refs):
    terms, (lat_mine, lat_other, top, low, total, turned) = refs[:-6], refs[-6:]
    half = terms[0].shape[2]
    for m in range(3):
        acc = terms[0][0, m].astype(f32)
        for x in terms[1:]:
            acc = acc + x[0, m].astype(f32)
        total[m * half : (m + 1) * half, :] = acc
    n = lat_mine.shape[0]
    total[3 * half : 3 * half + n, :] = lat_mine[...].astype(f32) + lat_other[...].astype(f32)
    if 3 * half + n < total.shape[0]:
        total[3 * half + n :, :] = jnp.zeros((total.shape[0] - 3 * half - n, total.shape[1]), f32)
    turn(where, total, turned, top, low)


def kv_turn_kernel(where, *refs):
    terms, (top, low, total, turned) = refs[:-4], refs[-4:]
    acc = terms[0][0].astype(f32)
    for x in terms[1:]:
        acc = acc + x[0].astype(f32)
    total[...] = acc
    turn(where, total, turned, top, low)


def first_blocks(terms):
    return [pl.BlockSpec((1,) + x.shape[1:], lambda i, z=(0,) * x.ndim: z) for x in terms]


def whole_blocks(arrays):
    return [pl.BlockSpec(x.shape, lambda i, z=(0,) * len(x.shape): z) for x in arrays]


def halve_end_kernel(where, *refs):
    terms, (mine, other, total) = refs[:-3], refs[-3:]
    core = where[0] & 1
    acc = terms[0][0].astype(f32)
    for x in terms[1:]:
        acc = acc + x[0].astype(f32)
    total[...] = acc
    n = mine.shape[0]
    mine[...] = total[rows_at(core, n), :]
    other[...] = total[rows_at(1 - core, n), :].astype(bf16)


def latent_end_kernel(where, mine, other, latents, lat_params, extra, small, turned):
    core = where[0] & 1
    first, second = mine[...].astype(f32), other[...].astype(f32)
    low = jnp.concatenate([jnp.where(core == 0, first, second), jnp.where(core == 0, second, first)], 0)
    unit, inverse = unit_norm(latents[...])
    once = jnp.where(where[0] == 0, 1.0, 0.0)
    small[0:1, :] = jnp.sum(low * unit, 0, keepdims=True) * once
    small[1:2, :] = jnp.sum(low, 0, keepdims=True) * once
    turned[...] = norm_back(low, unit, inverse, lat_params[0:1, :]).T
    extra[...] = turned[rows_at(where[0], extra.shape[0]), :]


def core_rows_kernel(where, pair, mine, other):
    core = where[0] & 1
    n = mine.shape[0]
    mine[...] = pair[rows_at(core, n), :]
    other[...] = pair[rows_at(1 - core, n), :]


def update_kernel(count, where, sums, *refs):
    ins, outs = refs[: 3 * (count - 2) + 4], refs[3 * (count - 2) + 4 :]
    small = sums[0:7, :]
    squares = jnp.sum(jnp.sum(small * small, 1, keepdims=True), 0, keepdims=True) + sums[7:8, 0:1]
    norm = jnp.sqrt(squares)
    outs[0][...] = norm
    factor = jnp.minimum(1.0, clip_limit / (norm + 1e-06))
    for i in range(count - 2):
        weight, state, gradient = ins[3 * i : 3 * i + 3]
        new, moments = outs[1 + 2 * i : 3 + 2 * i]
        scale = factor if gradient.ndim == 2 else factor[None]
        new[0], new[1], moments[0], moments[1] = adam_step(
            weight[...], state[0], state[1], state[2], gradient[...] * scale
        )
    lat_params, lat_state, in_params, in_state = ins[-4:]
    lat_new, lat_moments, in_new, in_moments, lat_clipped, in_clipped = outs[1 + 2 * (count - 2) :]
    lat_clipped[...] = sums[0:4, :] * factor
    lat_new[0], lat_new[1], lat_moments[0], lat_moments[1] = adam_step(
        lat_params[...], lat_state[0], lat_state[1], lat_state[2], lat_clipped[...]
    )
    in_clipped[...] = sums[4:7, 0 : in_params.shape[1]] * factor
    results = adam_step(in_params[...], in_state[0], in_state[1], in_state[2], in_clipped[...])
    for i in range(3):
        row = slice(i, i + 1)
        in_new[i, 0:1], in_new[i, 1:2], in_moments[i, 0:1], in_moments[i, 1:2] = (x[row] for x in results)


def query_back_kernel(H, where, lat_all, w0, mine, other, wq, top, low, grad_q, whole, term):
    at = Place(where, H)
    half_wide = mine.shape[0]
    grad_q[rows_at(at.core, half_wide), :] = mine[...]
    grad_q[rows_at(1 - at.core, half_wide), :] = other[...]
    term[...] = dot(grad_q[...], w0[...], 0, 0).astype(bf16)
    slots_out(at, at.core, term, top, low)
    whole[...] = dot(lat_all[...], grad_q[...], 0, 1)
    wq[...] = whole[rows_at(at.s, wq.shape[0]), :]


def finish_kernel(
    where, wq, sq_mine, sq_other, kv_mine, kv_other, lat_extra, lat_small, mid_small, in_sums_a, in_sums_b, in_sums_c, in_sums_d,
    square_grad, kv_grad, lat_grad, sums,
):
    core = where[0] & 1
    half = wq.shape[1] // 2
    mine, other = sq_mine[...], sq_other[...].astype(f32)
    low, high = jnp.where(core == 0, mine, other), jnp.where(core == 0, other, mine)
    square_grad[0] = wq[...]
    for m in range(3):
        square_grad[1 + m, :, 0:half] = low[:, m * half : (m + 1) * half]
        square_grad[1 + m, :, half:] = high[:, m * half : (m + 1) * half]
    kv_grad[core] = kv_mine[...]
    kv_grad[1 - core] = kv_other[...].astype(f32)
    n = lat_extra.shape[1] // 2
    ends = slice(3 * half, 3 * half + n)
    lat_grad[...] = (lat_extra[...] + jnp.concatenate([low[:, ends], high[:, ends]], 1)).T

    def squares(x):
        return jnp.sum(jnp.sum(x * x, 0, keepdims=True), 1, keepdims=True)

    own = slice(0, 3 * half)
    out = squares(wq[...]) + squares(mine[:, own]) + squares(other[:, own]) + squares(lat_grad[...])
    out = out + squares(kv_mine[...]) + squares(kv_other[...].astype(f32))
    sums[...] = jnp.zeros_like(sums)
    sums[0:2, :] = lat_small[...]
    sums[2:4, :] = mid_small[...]
    d_in = in_sums_a.shape[2]
    sums[4:7, 0:d_in] = (in_sums_a[0] + in_sums_b[0]) + (in_sums_c[0] + in_sums_d[0])
    sums[7:8, :] = jnp.broadcast_to(out, (1, sums.shape[1]))


def on_device(
    inputs,
    mask_flags,
    out_grad,
    square,
    square_state,
    kv_weights,
    kv_state,
    latents,
    latents_state,
    in_params,
    in_state,
    lat_params,
    lat_state,
):
    L = Links()
    S, H = L.S, L.H
    go = Order(jnp.stack([L.s, L.j]).astype(jnp.int32))
    rows, d_in = inputs.shape
    parts = SEQ_LEN // rows
    seqs = H // parts
    lat_rows, d_lat = latents.shape
    nlat = lat_rows * H
    wide = square.shape[2]
    half_wide = wide // 2
    d_part, in_part = d_lat // S, d_in // S
    chips = S // 2
    mine_rows = seqs * lat_rows

    def low(*shape):
        return like(shape, bf16)

    def full(*shape):
        return like(shape, f32)

    square_t, kv_t = jnp.swapaxes(square, 1, 2), jnp.swapaxes(kv_weights, 1, 2)
    (lat_low,) = go(lat_kernel, [latents, lat_params], [low(lat_rows, d_lat)], name="lat_norm")
    kv_pair = go(fix(kv_weight_kernel, H), [kv_t], [low(wide, d_in)] * 2, name="kv_weight")
    kv_first = [L.swap_step(kv_pair[0], i) for i in range(L.hb)]
    lat_near = L.near(lat_low)
    mask = mask_flags.reshape(rows, 1)
    step = min(rows, 256)
    in_low, in_turned = go(
        token_kernel,
        [inputs, mask, in_params],
        [low(rows, d_in), low(d_in, rows)],
        name="token_norm",
        grid=(rows // step,),
        in_specs=[
            pl.BlockSpec((step, d_in), lambda i: (i, 0)),
            pl.BlockSpec((step, 1), lambda i: (i, 0)),
            pl.BlockSpec(in_params.shape, lambda i: (0, 0)),
        ],
        out_specs=[pl.BlockSpec((step, d_in), lambda i: (i, 0)), pl.BlockSpec((d_in, step), lambda i: (0, i))],
    )
    (w0,) = go(
        first_weight_kernel,
        [square_t],
        [low(wide, d_lat)],
        name="first_weight",
        grid=(1,),
        in_specs=[pl.BlockSpec((1, wide, d_lat), lambda i: (0, 0, 0))],
        out_specs=[pl.BlockSpec((wide, d_lat), lambda i: (0, 0))],
    )
    kv_first = [after(x, w0) for x in kv_first]
    kv_mine = [kv_pair[0]] + L.spread(kv_first)
    kv_halves = kv_mine + [kv_pair[1]] + [L.swap_core(x) for x in kv_mine[1:]]
    lat_near = [lat_low] + [after(x, *kv_first) for x in lat_near]
    lat_all, query_mine, query_other = go(
        fix(query_kernel, H),
        [*lat_near, w0],
        [low(nlat, d_lat)] + [low(half_wide, nlat)] * 2,
        [pltpu.VMEM((wide, nlat), bf16)],
        name="query",
    )
    query_near = L.near(query_mine)
    sq_mine, sq_other = go(
        fix(other_weight_kernel, H),
        [square_t],
        [low(3, half_wide, d_lat)] * 2,
        name="other_weights",
        grid=(3,),
        in_specs=[pl.BlockSpec((1, wide, d_lat), lambda i: (1 + i, 0, 0))],
        out_specs=[pl.BlockSpec((1, half_wide, d_lat), lambda i: (i, 0, 0))] * 2,
    )
    sq_sent = after(sq_mine, kv_mine[-1])
    sq_near = [L.swap_step(sq_sent, i) for i in range(L.hb)]

    kv, kv_all = go(
        fix(kv_kernel, H),
        [in_turned, *kv_halves],
        [low(2, d_lat, rows), low(2, d_lat, d_in)],
        [pltpu.SemaphoreType.DMA((2 * H,))],
        name="kv",
        in_specs=[VMEM] + [ANY] * (2 * H),
        after=[sq_sent],
    )
    query_near = [after(x, kv) for x in query_near]
    query_halves = [query_mine] + query_near + [query_other] + [L.swap_core(x) for x in query_near]
    query, *packs = go(
        fix(attention_kernel, H),
        [*query_halves, kv],
        [low(d_lat, nlat)] + [low(lat_rows, d_lat + SIDE)] * H,
        [pltpu.VMEM((d_lat, nlat), f32), pltpu.VMEM((nlat, d_lat + SIDE), bf16)],
        name="attention",
    )
    got = [packs[0]] + [L.swap_hid(packs[m], m) for m in range(1, H)]
    sq_near = [after(x, *got) for x in sq_near]
    sq_all = [sq_mine] + L.spread(sq_near)
    sq_halves = sq_all + [sq_other] + [L.swap_core(x) for x in sq_all[1:]]

    latents_out, attended, branch_grad, up_grad, mid_low, hidden, grad_y, mid_small, res_sum, *backs = go(
        fix(latent_kernel, H, parts),
        [*got, latents, out_grad, lat_params, *sq_halves],
        [full(mine_rows, d_lat)]
        + [low(mine_rows, d_lat)] * 6
        + [full(2, d_lat), low(lat_rows, d_lat)]
        + [low(lat_rows, d_lat + SIDE)] * H,
        [
            pltpu.VMEM((3, d_lat, d_lat), bf16),
            pltpu.SemaphoreType.DMA((3, 2 * H)),
            pltpu.VMEM((H, lat_rows, d_lat + SIDE), bf16),
            pltpu.VMEM((mine_rows, d_lat), f32),
            pltpu.VMEM((seqs, lat_rows, d_lat + SIDE), bf16),
        ],
        name="latent",
        in_specs=[VMEM] * (H + 3) + [ANY] * (2 * H),
    )
    back = [backs[0]] + [L.swap_hid(backs[m], m) for m in range(1, H)]

    sq_args = [attended, up_grad, hidden, branch_grad, mid_low, grad_y]
    sq_scratch = [pltpu.VMEM((3, d_lat, mine_rows), bf16)]
    sq_like = [low(H // 2, 3, half_wide, d_lat)] * 2
    sq_send = go(fix(square_grad_kernel, H, False), sq_args, sq_like, sq_scratch, name="square_send")
    sq_got = [L.swap_core(x) for x in sq_send]
    sq_keep = go(fix(square_grad_kernel, H, True), sq_args, sq_like, sq_scratch, name="square_keep")
    sq = Halving(go, [sq_keep[0], sq_got[0]], [sq_keep[1], sq_got[1]], L.hb, L.swap_step, "square")
    sq.start()

    grad_kv, *gq = go(
        fix(attention_back_kernel, H),
        [query, kv, *back],
        [low(2, d_lat, rows)] + [low(H // 2, half_wide, nlat)] * 4,
        [
            pltpu.VMEM((nlat, d_lat + SIDE), bf16),
            pltpu.VMEM((d_lat, nlat), bf16),
            pltpu.VMEM((d_lat, nlat), bf16),
        ],
        name="attention_back",
    )
    gq_got = [L.swap_core(x) for x in gq[:2]]
    kv_scratch = [pltpu.VMEM((d_lat, d_in), bf16)]
    kv_like = [low(H // 2, wide, d_in)] * 2
    kv_send = go(fix(kv_grad_kernel, H, False), [grad_kv, in_low], kv_like, kv_scratch, name="kv_send")
    kv_got = [L.swap_core(x) for x in kv_send]
    gq_sums = Halving(go, [gq[2], gq_got[0]], [gq[3], gq_got[1]], L.hb, L.swap_step, "query")
    gq_sums.start()
    kv_keep = go(fix(kv_grad_kernel, H, True), [grad_kv, in_low], kv_like, kv_scratch, name="kv_keep")
    kv_sums = Halving(go, [kv_keep[0], kv_got[0]], [kv_keep[1], kv_got[1]], L.hb, L.swap_step, "kv")
    kv_sums.start()

    quarter = rows // 4
    in_sums = []
    inputs_grad = None

    def token_grad():
        nonlocal inputs_grad
        i = len(in_sums)
        outs = [full(rows, d_in), full(1, 3, d_in)]
        inputs_grad, sums = go(
            token_grad_kernel,
            [inputs, mask, in_params, grad_kv, kv_all],
            outs,
            [pltpu.VMEM((quarter, d_in), f32)],
            name="token_grad",
            grid=(1,),
            in_specs=[
                pl.BlockSpec((quarter, d_in), lambda g: (i, 0)),
                pl.BlockSpec((quarter, 1), lambda g: (i, 0)),
                pl.BlockSpec(in_params.shape, lambda g: (0, 0)),
                pl.BlockSpec((2, d_lat, quarter), lambda g: (0, 0, i)),
                pl.BlockSpec(kv_all.shape, lambda g: (0, 0, 0)),
            ],
            out_specs=[pl.BlockSpec((quarter, d_in), lambda g: (i, 0)), pl.BlockSpec((1, 3, d_in), lambda g: (0, 0, 0))],
            onto=inputs_grad,
        )
        in_sums.append(sums)

    lanes = 3 * half_wide + lat_rows // 2
    padded = -(-lanes // 128) * 128

    def turn_to_chips(kernel, terms, extra, n, lanes, padded, name):
        d = terms[0].shape[-1]
        out = [low(chips // 2, n, lanes)] * 2
        return go(
            kernel,
            [*terms, *extra],
            out,
            [pltpu.VMEM((padded, d), f32), pltpu.VMEM((d, padded), bf16)],
            name=name,
            grid=(1,),
            in_specs=first_blocks(terms) + whole_blocks(extra),
            out_specs=whole_blocks(out),
        )

    n = L.sb - 1

    def chip_step(x, i):
        return L.swap_seq(x, 2 << (n - 1 - i))

    def end(terms, n, lanes, name):
        return go(
            halve_end_kernel,
            terms,
            [full(n, lanes), low(n, lanes)],
            [pltpu.VMEM((2 * n, lanes), f32)],
            name=name,
            grid=(1,),
            in_specs=first_blocks(terms),
            out_specs=[pl.BlockSpec((n, lanes), lambda i: (0, 0))] * 2,
        )

    sq.step()
    gq_sums.step()
    token_grad()
    kv_sums.step()
    for _ in range(L.hb - 2):
        gq_sums.step()
        kv_sums.step()
        sq.step()
    gq_mine = go.add(gq_sums.terms, 0, 1, "query_sum")
    gq_near = L.swap_seq(gq_mine, 2)
    res_mine, res_send = go(core_rows_kernel, [res_sum], [low(lat_rows // 2, d_lat)] * 2, name="latent_rows")
    res_other = L.swap_core(res_send)
    token_grad()
    kv_top, kv_low = turn_to_chips(kv_turn_kernel, kv_sums.terms, [], 2 * in_part, wide, wide, "kv_turn")
    kv_chips = Halving(go, [kv_top], [kv_low], n, chip_step, "kv_chip")
    kv_chips.start()
    gq_mine = go.add([gq_mine, gq_near], 0, 1, "query_chip")
    gq_near = L.swap_seq(gq_mine, 4)
    token_grad()
    sq_top, sq_low = turn_to_chips(
        square_turn_kernel, sq.terms, [res_mine, res_other], 2 * d_part, lanes, padded, "square_turn"
    )
    sq_chips = Halving(go, [sq_top], [sq_low], n, chip_step, "square_chip")
    sq_chips.start()
    for i in range(2, L.sb):
        gq_mine = go.add([gq_mine, gq_near], 0, 1, "query_chip")
        if i + 1 < L.sb:
            gq_near = L.swap_seq(gq_mine, 2 << i)
    gq_mine = gq_mine[0]
    gq_other = L.swap_core(gq_mine)
    kv_chips.step()
    wq_part, lat_top, lat_low_half = go(
        fix(query_back_kernel, H),
        [lat_all, w0, gq_mine, gq_other],
        [full(d_part, wide)] + [low(H // 2, lat_rows // 2, d_lat)] * 2,
        [pltpu.VMEM((wide, nlat), bf16), pltpu.VMEM((d_lat, wide), f32), pltpu.VMEM((nlat, d_lat), bf16)],
        name="query_back",
    )
    lat_sums = Halving(go, [lat_top], [lat_low_half], L.hb, L.swap_step, "latent")
    lat_sums.start()
    token_grad()
    sq_chips.step()
    for _ in range(L.hb - 1):
        lat_sums.step()
    for _ in range(n - 2):
        kv_chips.step()
        sq_chips.step()
    kv_mine, kv_send = end(kv_chips.terms, in_part, wide, "kv_end")
    kv_other = L.swap_core(kv_send)
    low_mine = go.add(lat_sums.terms, 0, 1, "latent_sum")[0]
    low_other = L.swap_core(low_mine)
    lat_extra, lat_small = go(
        latent_end_kernel,
        [low_mine, low_other, latents, lat_params],
        [full(d_part, lat_rows), full(2, d_lat)],
        [pltpu.VMEM((d_lat, lat_rows), f32)],
        name="latent_end",
    )
    sq_mine, sq_send = end(sq_chips.terms, d_part, lanes, "square_end")
    sq_other = L.swap_core(sq_send)

    square_grad, kv_grad, lat_grad, sums = go(
        finish_kernel,
        [wq_part, sq_mine, sq_other, kv_mine, kv_other, lat_extra, lat_small, mid_small, *in_sums],
        [full(4, d_part, wide), full(2, in_part, wide), full(lat_rows, d_part), full(8, d_lat)],
        name="finish",
    )
    sums = L.sum_all(sums)
    sq_old = lax.dynamic_slice_in_dim(square, L.s * d_part, d_part, 1)
    kv_old = lax.dynamic_slice_in_dim(kv_weights, L.s * in_part, in_part, 1)
    lat_old = lax.dynamic_slice_in_dim(latents, L.s * d_part, d_part, 1)
    pair = [full(3, 2, d_in)] * 2
    outs = [full(1, 1)]
    for x in (sq_old, kv_old, lat_old, lat_params):
        outs += [full(2, *x.shape)] * 2
    results = go(
        fix(update_kernel, 5),
        [sums, sq_old, square_state, square_grad, kv_old, kv_state, kv_grad, lat_old, latents_state, lat_grad]
        + [lat_params, lat_state, in_params, in_state],
        outs + pair + [full(*lat_params.shape), full(*in_params.shape)],
        name="update",
    )
    (grad_norm, square_new, square_moments, kv_new, kv_moments, latents_new, latents_moments) = results[:7]
    (lat_new, lat_moments, in_new, in_moments, lat_clipped, in_clipped) = results[7:]
    grad_norm = grad_norm[0, 0]
    in_new, in_moments = jnp.swapaxes(in_new, 0, 1), jnp.swapaxes(in_moments, 0, 1)
    return (
        latents_out.reshape(seqs, lat_rows, d_lat),
        inputs_grad,
        grad_norm,
        square_new,
        square_moments,
        kv_new,
        kv_moments,
        latents_new,
        latents_moments,
        in_new,
        in_moments,
        lat_new,
        lat_moments,
        in_clipped,
        lat_clipped,
    )


def solution(mesh):
    return jax.shard_map(
        on_device,
        mesh=mesh,
        in_specs=(
            P(("seq", "hid"), None),
            P(("seq", "hid")),
            P("seq", "hid", None),
            P(None, None, "hid"),
            P(None, None, "seq", "hid"),
            P(None, None, "hid"),
            P(None, None, "seq", "hid"),
            P("hid", None),
            P(None, "hid", "seq"),
            P(),
            P(),
            P(),
            P(),
        ),
        out_specs=(
            P("seq", "hid", None),
            P(("seq", "hid"), None),
            P(),
            P(None, None, "seq", "hid"),
            P(None, None, "seq", "hid"),
            P(None, None, "seq", "hid"),
            P(None, None, "seq", "hid"),
            P(None, "hid", "seq"),
            P(None, "hid", "seq"),
            P(),
            P(),
            P(),
            P(),
            P(),
            P(),
        ),
        check_vma=False,
    )
```

```python
from functools import partial as fix
import math

import jax
import jax.numpy as jnp
from jax import lax
from jax.experimental import pallas as pl
from jax.experimental.pallas import tpu as pltpu
from jax.sharding import PartitionSpec as P

HEADS = 8
HEAD = 160
SEQ_LEN = 2048
STEP = 10
SIDE = 128


clip_limit = 1.0
beta_one = 0.9
beta_two = 0.999
adam_eps = 1e-08
learn_rate = 0.05
decay_rate = 0.01
ema_keep = 0.9
norm_eps = 1e-05
score_scale = 1.0 / math.sqrt(HEAD)
score_two = score_scale * math.log2(math.e)

f32 = jnp.float32
bf16 = jnp.bfloat16


def unit_norm(values):
    centre = jnp.mean(values, -1, keepdims=True)
    centred = values - centre
    inverse = lax.rsqrt(jnp.mean(centred * centred, -1, keepdims=True) + norm_eps)
    return centred * inverse, inverse


def norm_back(upstream, unit_rows, inverse, scale_row):
    scaled = upstream * scale_row
    inner_mean = jnp.mean(scaled, -1, keepdims=True)
    along_mean = jnp.mean(scaled * unit_rows, -1, keepdims=True)
    return inverse * (scaled - inner_mean - unit_rows * along_mean)


def adam_step(weight, first, root, average, gradient):
    moment_one = beta_one * first + (1.0 - beta_one) * gradient
    root_two = jnp.sqrt(beta_two * root * root + (1.0 - beta_two) * gradient * gradient)
    corrected_one = moment_one * (learn_rate / (1.0 - beta_one**STEP))
    denominator = root_two * (1.0 / math.sqrt(1.0 - beta_two**STEP)) + adam_eps
    new_weight = weight * (1.0 - learn_rate * decay_rate) - corrected_one / denominator
    ema_new = ema_keep * average + (1.0 - ema_keep) * new_weight
    return new_weight, ema_new, moment_one, root_two


def dot(a, b, over_a, over_b):
    return lax.dot_general(a, b, (((over_a,), (over_b,)), ((), ())), preferred_element_type=f32)


def flip(value, bits):
    out = 0
    for i in range(bits):
        out = out + ((value >> i) & 1) * (1 << (bits - 1 - i))
    return out


class Links:
    def __init__(self):
        self.S = lax.axis_size("seq")
        self.H = lax.axis_size("hid")
        self.hb = self.H.bit_length() - 1
        self.sb = self.S.bit_length() - 1
        self.s = lax.axis_index("seq")
        self.j = lax.axis_index("hid")
        self.core = self.s & 1

    def swap(self, x, dest):
        pairs = []
        for s in range(self.S):
            for j in range(self.H):
                ds, dj = dest(s, j)
                pairs.append((s * self.H + j, ds * self.H + dj))
        return lax.ppermute(x, ("seq", "hid"), pairs)

    def swap_core(self, x):
        return self.swap(x, lambda s, j: (s ^ 1, j))

    def swap_hid(self, x, mask):
        return self.swap(x, lambda s, j: (s, j ^ mask))

    def swap_seq(self, x, mask):
        return self.swap(x, lambda s, j: (s ^ mask, j))

    def swap_step(self, x, i):
        even, odd = 1 << i, 1 << (self.hb - 1 - i)
        return self.swap(x, lambda s, j: (s, j ^ (odd if s & 1 else even)))

    def spread(self, first):
        blocks = [None]
        for i, x in enumerate(first):
            blocks += [x] + [self.swap_step(y, i) for y in blocks[1:]]
        return blocks[1:]

    def near(self, x):
        return [self.swap_hid(x, m) for m in range(1, self.H)]

    def near_chips(self, x):
        return [self.swap_seq(x, 2 * m) for m in range(1, self.S // 2)]

    def sum_all(self, x, last):
        x = x + self.swap_core(x)
        x = tree_sum([x] + self.near(x))
        return tree_sum([x] + after(self.near_chips(x), last))


def tree_sum(terms):
    while len(terms) > 1:
        terms = [a + b for a, b in zip(terms[::2], terms[1::2])]
    return terms[0]


class Place:
    def __init__(self, where, H):
        self.H = H
        self.hb = H.bit_length() - 1
        self.s = where[0]
        self.j = where[1]
        self.core = self.s & 1

    def block(self, r, core):
        return self.j ^ jnp.where(core == 0, r, flip(r, self.hb))

    def halves(self):
        mine = [(self.block(r, self.core), self.core) for r in range(self.H)]
        return mine + [(self.block(r, 1 - self.core), 1 - self.core) for r in range(self.H)]


def after(x, *others):
    return lax.optimization_barrier((x, others))[0]


def rows_at(index, size):
    return pl.ds(pl.multiple_of(index * size, size), size)


VMEM = pl.BlockSpec(memory_space=pltpu.VMEM)
SMEM = pl.BlockSpec(memory_space=pltpu.SMEM)
ANY = pl.BlockSpec(memory_space=pl.ANY)


spent = {
    "kv_weight": 5.0,
    "first_weight": 0.1,
    "query": 4.0,
    "token_norm": 10.0,
    "other_weights": 0.1,
    "kv": 0.1,
    "attention": 0.1,
    "kv_turned": 0.1,
    "latent": 11.0,
    "square_grad": 5.0,
    "attention_back": 12.0,
    "token_grad_0": 0.1,
    "query_core": 0.1,
    "square_step": 4.0,
    "query_hid": 0.1,
    "kv_grad": 1.0,
    "query_chips": 10.0,
    "square_turn": 0.1,
    "query_back": 0.1,
    "kv_step": 0.1,
    "square_chip_step": 0.1,
    "kv_turn": 0.1,
    "latent_end": 3.0,
    "token_grad_1": 0.1,
    "kv_chip_step": 0.1,
    "square_end": 3.0,
    "update": 7.0,
}


class Order:
    def __init__(self, where):
        self.where = where
        self.last = []

    def __call__(
        self, kernel, args, outs, scratch=(), name=None, grid=(), in_specs=None, out_specs=None, after=(), onto=None
    ):
        n = len(args)
        waits = self.last + list(after)
        if onto is not None:
            waits = [onto] + waits

        def body(where, *refs):
            kernel(where, *refs[:n], *refs[n + len(waits) :])

        results = pl.pallas_call(
            body,
            out_shape=outs,
            grid=grid,
            in_specs=[SMEM] + (in_specs or [VMEM] * n) + [ANY] * len(waits),
            out_specs=out_specs or [VMEM] * len(outs),
            scratch_shapes=list(scratch),
            compiler_params=pltpu.CompilerParams(vmem_limit_bytes=56 * 1024 * 1024),
            cost_estimate=pl.CostEstimate(
                flops=int(spent.get(name, 2.0) * 1e9), bytes_accessed=0, transcendentals=0
            ),
            name=name,
            input_output_aliases={} if onto is None else {1 + n: 0},
        )(self.where, *args, *waits)
        self.last = [results[-1]]
        return results

    def tree(self, terms, name):
        def kernel(where, *refs):
            refs[-1][...] = tree_sum([x[...].astype(f32) for x in refs[:-1]]).astype(bf16)

        return self(kernel, terms, [like(terms[0].shape, bf16)], name=name)[0]

    def add(self, terms, block, count, name):
        shape = terms[0].shape[1:]
        parts = shape[0] if len(shape) == 3 else 1
        terms = [x.reshape((x.shape[0], parts) + shape[-2:]) for x in terms]

        def kernel(where, *refs):
            out = refs[-1]
            acc = refs[0][...].astype(f32)
            for x in refs[1:-1]:
                acc = acc + x[...].astype(f32)
            out[...] = acc.astype(bf16)

        size = (1, 1) + shape[-2:]
        (out,) = self(
            kernel,
            terms,
            [like((count, parts) + shape[-2:], bf16)],
            name=name,
            grid=(count, parts),
            in_specs=[pl.BlockSpec(size, lambda i, m: (block * count + i, m, 0, 0))] * len(terms),
            out_specs=[pl.BlockSpec(size, lambda i, m: (i, m, 0, 0))],
        )
        return out.reshape((count,) + shape)


def like(shape, dtype):
    return jax.ShapeDtypeStruct(tuple(shape), dtype)


class Halving:
    def __init__(self, go, top, low, bits, swap, name):
        self.go, self.top, self.terms, self.bits, self.swap, self.name = go, top, low, bits, swap, name

    def start(self):
        i = self.bits - 1
        sending = self.top[0] if len(self.top) == 1 else self.go.add(self.top, 0, 1 << i, self.name + "_top")
        self.terms = self.terms + [self.swap(sending, i)]
        self.at = i

    def step(self):
        n = 1 << (self.at - 1)
        sending = self.go.add(self.terms, 1, n, self.name + "_step")
        self.at -= 1
        self.terms = self.terms + [self.swap(sending, self.at)]


def lat_kernel(where, latents, lat_params, out):
    unit, _ = unit_norm(latents[...])
    out[...] = (unit * lat_params[0:1, :] + lat_params[1:2, :]).astype(bf16)


def kv_weight_kernel(H, where, kv, mine, other):
    at = Place(where, H)
    mine[...] = kv[at.core].astype(bf16)
    other[...] = kv[1 - at.core].astype(bf16)


def first_weight_kernel(where, weight, out):
    out[...] = weight[0].astype(bf16)


def other_weight_kernel(H, where, weight, mine, other):
    at = Place(where, H)
    n = mine.shape[1]
    mine[0] = weight[0, rows_at(at.core, n), :].astype(bf16)
    other[0] = weight[0, rows_at(1 - at.core, n), :].astype(bf16)


def query_kernel(H, where, *refs):
    near, (w0, lat_all, query) = refs[:H], refs[H:]
    at = Place(where, H)
    n = near[0].shape[0]
    for m, x in enumerate(near):
        lat_all[rows_at(at.j ^ m, n), :] = x[...]
    query[...] = dot(w0[...], lat_all[...], 1, 1).astype(bf16)


def token_kernel(where, inputs, mask, in_params, out, turned):
    masked = jnp.where(mask[...] > 0, in_params[2:3, :], inputs[...])
    unit, _ = unit_norm(masked)
    low = (unit * in_params[0:1, :] + in_params[1:2, :]).astype(bf16)
    out[...] = low
    turned[...] = low.T


def started(copies):
    for copy in copies:
        copy.start()
    return copies


def waited(copies):
    for copy in copies:
        copy.wait()


def kv_kernel(H, where, in_turned, *refs):
    halves, (kv, kv_all, weights, product, sems, out_sems) = refs[: 2 * H], refs[2 * H :]
    at = Place(where, H)
    wide = halves[0].shape[0]
    d_lat = wide * H
    copies = started(
        [
            pltpu.make_async_copy(halves[i], weights.at[which, rows_at(block, wide), :], sems.at[i])
            for i, (block, which) in enumerate(at.halves())
        ]
    )
    waited(copies)
    outs = started([pltpu.make_async_copy(weights, kv_all, out_sems.at[4])])
    for which in range(2):
        for part in range(2):
            span = slice(part * d_lat // 2, (part + 1) * d_lat // 2)
            product[which, span, :] = dot(weights[which, span, :], in_turned[...], 1, 0).astype(bf16)
            copy = pltpu.make_async_copy(
                product.at[which, span, :], kv.at[which, span, :], out_sems.at[2 * which + part]
            )
            outs += started([copy])
    waited(outs)


def kv_turned_kernel(where, kv_all, out):
    out[0] = kv_all[0].T


def three_way(x, lane):
    a = x.astype(bf16).astype(f32)
    b = (x - a).astype(bf16).astype(f32)
    part = (lane // HEADS) % 3
    return jnp.where(part == 0, a, jnp.where(part == 1, b, x - a - b)).astype(bf16)


def three_sum(x):
    return x + pltpu.roll(x, SIDE - HEADS, 1) + pltpu.roll(x, SIDE - 2 * HEADS, 1)


def attention_kernel(H, where, *refs):
    near, kv, query = refs[:H], refs[H], refs[H + 1]
    packs, (mix, packed) = refs[H + 2 : -2], refs[-2:]
    at = Place(where, H)
    n = near[0].shape[0]
    for m, x in enumerate(near):
        query[rows_at(at.j ^ m, n), :] = x[...]
    d_lat, nlat = query.shape
    lane = lax.broadcasted_iota(jnp.int32, (nlat, SIDE), 1)
    logs = jnp.zeros((nlat, SIDE), f32)
    for h in range(HEADS):
        span = slice(h * HEAD, (h + 1) * HEAD)
        scores = dot(query[span, :], kv[0, span, :], 0, 0)
        peak = jnp.max(scores, -1, keepdims=True)
        weight = jnp.exp2((scores - peak) * score_two)
        total = jnp.sum(weight, -1, keepdims=True)
        probs = (weight * (1.0 / total)).astype(bf16)
        mix[span, :] = dot(kv[1, span, :], probs, 1, 1)
        log_part = peak * score_two + jnp.log2(total)
        logs = jnp.where((lane % HEADS == h) & (lane < 3 * HEADS), log_part, logs)
    packed[:, :d_lat] = mix[...].T.astype(bf16)
    packed[:, d_lat:] = three_way(logs, lane)
    lat_rows = nlat // H
    for m, out in enumerate(packs):
        out[...] = packed[rows_at(at.j ^ m, lat_rows), :]


def head_lanes(shape):
    return lax.broadcasted_iota(jnp.int32, shape, 1) // HEAD


def latent_kernel(H, parts, where, *refs):
    seqs = H // parts
    got, refs = refs[:H], refs[H:]
    latents, out_grad, lat_params, refs = refs[0], refs[1], refs[2], refs[3:]
    pieces, refs = refs[: 2 * H], refs[2 * H :]
    (latents_out, acts, small, res_mine, res_send), refs = refs[:5], refs[5:]
    attended, up_grad, hidden, branch_grad, mid_low, grad_y = (acts.at[i] for i in range(6))
    backs, (weights, sems, gathered, att, packed, res) = refs[:H], refs[H:]
    at = Place(where, H)
    lat_rows, d_lat = latents.shape
    half_wide = pieces[0].shape[1]
    copies = []
    for m in range(3):
        group = []
        for i, (block, half) in enumerate(at.halves()):
            group.append(
                pltpu.make_async_copy(
                    pieces[i].at[m],
                    weights.at[m, rows_at(block * 2 + half, half_wide), :],
                    sems.at[m, i],
                )
            )
            group[-1].start()
        copies.append(group)

    def arrived(m):
        for copy in copies[m]:
            copy.wait()

    for m in range(H):
        gathered[at.j ^ m] = got[m][...]
    heads = head_lanes((lat_rows, d_lat))
    log_totals = []
    for b in range(seqs):
        logs = [three_sum(gathered[b * parts + p, :, d_lat:].astype(f32)) for p in range(parts)]
        peak = logs[0]
        for x in logs[1:]:
            peak = jnp.maximum(peak, x)
        log_total = peak + jnp.log2(sum(jnp.exp2(x - peak) for x in logs))
        log_totals.append(log_total)
        mixed = jnp.zeros((lat_rows, d_lat), f32)
        for p in range(parts):
            share = jnp.exp2(logs[p] - log_total)
            spread = jnp.zeros((lat_rows, d_lat), f32)
            for h in range(HEADS):
                spread = jnp.where(heads == h, share[:, h : h + 1], spread)
            mixed = mixed + spread * gathered[b * parts + p, :, :d_lat].astype(f32)
        att[b * lat_rows : (b + 1) * lat_rows, :] = mixed
    attended[...] = att[...].astype(bf16)
    grad_y[...] = jnp.concatenate([out_grad[b] for b in range(seqs)], 0).astype(bf16)

    arrived(0)
    branch = dot(attended[...], weights[0], 1, 0)
    residual = jnp.concatenate([latents[...]] * seqs, 0) + branch
    unit, inverse = unit_norm(residual)
    mid_low[...] = (unit * lat_params[2:3, :] + lat_params[3:4, :]).astype(bf16)
    arrived(1)
    up_proj = dot(mid_low[...], weights[1], 1, 1)
    below = 0.5 + 0.5 * lax.erf(up_proj * math.sqrt(0.5))
    hidden[...] = (up_proj * below).astype(bf16)
    slope = below + up_proj * jnp.exp(-0.5 * up_proj * up_proj) * (1.0 / math.sqrt(2.0 * math.pi))
    arrived(2)
    latents_out[...] = residual + dot(hidden[...], weights[2], 1, 0)
    up_grad[...] = (dot(grad_y[...], weights[2], 1, 1) * slope).astype(bf16)
    grad_mid = dot(up_grad[...], weights[1], 1, 0)
    small[0:1, :] = jnp.sum(grad_mid * unit, 0, keepdims=True)
    small[1:2, :] = jnp.sum(grad_mid, 0, keepdims=True)
    grad_residual = jnp.concatenate([out_grad[b] for b in range(seqs)], 0) + norm_back(
        grad_mid, unit, inverse, lat_params[2:3, :]
    )
    branch_grad[...] = grad_residual.astype(bf16)
    folded = grad_residual[0:lat_rows]
    for b in range(1, seqs):
        folded = folded + grad_residual[b * lat_rows : (b + 1) * lat_rows]
    res[...] = folded.astype(bf16)
    res_mine[...] = res[rows_at(at.core, lat_rows // 2), :]
    res_send[...] = res[rows_at(1 - at.core, lat_rows // 2), :]
    grad_att = dot(branch_grad[...], weights[0], 1, 1).astype(bf16)
    along = grad_att.astype(f32) * att[...]
    heads = head_lanes((seqs * lat_rows, d_lat))
    lane = lax.broadcasted_iota(jnp.int32, (lat_rows, SIDE), 1)
    inner = []
    for h in range(HEADS):
        lo, hi = h * HEAD // 128 * 128, -(-(h + 1) * HEAD // 128) * 128
        inner.append(jnp.sum(jnp.where(heads[:, lo:hi] == h, along[:, lo:hi], 0.0), -1, keepdims=True))
    for b in range(seqs):
        t = log_totals[b]
        side = jnp.where(lane < HEADS, t, jnp.where(lane < 2 * HEADS, pltpu.roll(t, HEADS, 1), pltpu.roll(t, 2 * HEADS, 1)))
        for h in range(HEADS):
            own = (lane % HEADS == h) & (lane >= 3 * HEADS)
            side = jnp.where(own, inner[h][b * lat_rows : (b + 1) * lat_rows], side)
        side = jnp.where(lane < 6 * HEADS, side, 0.0)
        packed[b, :, :d_lat] = grad_att[b * lat_rows : (b + 1) * lat_rows]
        packed[b, :, d_lat:] = three_way(side, lane)
    for m, out in enumerate(backs):
        out[...] = packed[(at.j ^ m) // parts]


def square_grad_kernel(H, where, acts, others, top, low, turned, rights):
    at = Place(where, H)
    rows = acts.shape[1]
    for m in range(3):
        turned[m, :, 0:rows] = acts[m].T
        turned[m, :, rows:] = others[m].T
        rights[m, 0:rows, :] = acts[3 + m]
        rights[m, rows:, :] = others[3 + m]
    half_wide = top.shape[2]
    for r in range(H):
        out = low if r < H // 2 else top
        at_row = rows_at(at.block(r, at.core) * 2 + at.core, half_wide)
        for m in range(3):
            out[r % (H // 2), m] = dot(turned[m, at_row, :], rights[m], 1, 0).astype(bf16)


def attention_back_kernel(H, where, query, *refs):
    backs, refs = refs[:H], refs[H:]
    kv, mine, send, q_keep, q_send, packed, turned, grad_q, grad_kv = refs
    at = Place(where, H)
    d_lat, nlat = query.shape
    lat_rows = nlat // H
    for m in range(H):
        packed[rows_at(at.j ^ m, lat_rows), :] = backs[m][...]
    turned[...] = packed[:, :d_lat].T
    side = three_sum(packed[:, d_lat:].astype(f32))
    for h in range(HEADS):
        span = slice(h * HEAD, (h + 1) * HEAD)
        scores = dot(query[span, :], kv[0, span, :], 0, 0)
        probs = jnp.exp2(scores * score_two - side[:, h : h + 1])
        grad_kv[1, span, :] = dot(turned[span, :], probs.astype(bf16), 1, 0).astype(bf16)
        grad_probs = dot(turned[span, :], kv[1, span, :], 0, 0)
        grad_scores = (probs * (grad_probs - side[:, 3 * HEADS + h : 3 * HEADS + h + 1])).astype(bf16)
        grad_q[span, :] = (dot(kv[0, span, :], grad_scores, 1, 1) * score_scale).astype(bf16)
        grad_kv[0, span, :] = (dot(query[span, :], grad_scores, 1, 0) * score_scale).astype(bf16)
    n = q_keep.shape[1]
    for m in range(H):
        block = (at.j ^ m) * 2
        q_keep[m] = grad_q[rows_at(block + at.core, n), :]
        q_send[m] = grad_q[rows_at(block + 1 - at.core, n), :]
    mine[...] = grad_kv[at.core]
    send[...] = grad_kv[1 - at.core]


def query_core_kernel(where, keep, got, *outs):
    for m, out in enumerate(outs):
        out[...] = (keep[m].astype(f32) + got[m].astype(f32)).astype(bf16)


def slots_out(at, core, whole, top, low):
    n = top.shape[1]
    per = whole.shape[0] // (at.H * n)
    for r in range(at.H):
        out = low if r < at.H // 2 else top
        block = at.block(r, core)
        out[r % (at.H // 2)] = whole[rows_at(block * 2 + core if per == 2 else block, n), :]


def kv_grad_kernel(H, where, mine, got, in_low, in_other, top, low, whole):
    at = Place(where, H)
    whole[...] = (dot(mine[...], in_low[...], 1, 0) + dot(got[...], in_other[...], 1, 0)).astype(bf16)
    slots_out(at, at.core, whole, top, low)


def token_grad_kernel(where, inputs, mask, in_params, mine, send, weights, inputs_grad, small):
    core = where[0] & 1
    upstream = (dot(weights[core], mine[...], 1, 0) + dot(weights[1 - core], send[...], 1, 0)).T
    masked_row = mask[...] > 0
    unit, inverse = unit_norm(jnp.where(masked_row, in_params[2:3, :], inputs[...]))
    grad = norm_back(upstream, unit, inverse, in_params[0:1, :])
    inputs_grad[...] = jnp.where(masked_row, 0.0, grad)

    @pl.when(pl.program_id(0) == 0)
    def _():
        small[...] = jnp.zeros_like(small)

    for r, term in enumerate((upstream * unit, upstream, jnp.where(masked_row, grad, 0.0))):
        small[0, r : r + 1, :] += jnp.sum(term, 0, keepdims=True)


def turn(where, total, turned, top, low):
    turned[...] = total[...].T.astype(bf16)
    chip = where[0] >> 1
    half, rows, lanes = top.shape
    for r in range(2 * half):
        out = low if r < half else top
        out[r % half] = turned[rows_at(chip ^ flip(r, half.bit_length()), rows), 0:lanes]


def square_turn_kernel(where, *refs):
    terms, (lat_mine, lat_other, top, low, total, turned) = refs[:-6], refs[-6:]
    half = terms[0].shape[2]
    for m in range(3):
        acc = terms[0][0, m].astype(f32)
        for x in terms[1:]:
            acc = acc + x[0, m].astype(f32)
        total[m * half : (m + 1) * half, :] = acc
    n = lat_mine.shape[0]
    total[3 * half : 3 * half + n, :] = lat_mine[...].astype(f32) + lat_other[...].astype(f32)
    if 3 * half + n < total.shape[0]:
        total[3 * half + n :, :] = jnp.zeros((total.shape[0] - 3 * half - n, total.shape[1]), f32)
    turn(where, total, turned, top, low)


def kv_turn_kernel(where, *refs):
    terms, (top, low, total, turned) = refs[:-4], refs[-4:]
    acc = terms[0][0].astype(f32)
    for x in terms[1:]:
        acc = acc + x[0].astype(f32)
    total[...] = acc
    turn(where, total, turned, top, low)


def first_blocks(terms):
    return [pl.BlockSpec((1,) + x.shape[1:], lambda i, z=(0,) * x.ndim: z) for x in terms]


def whole_blocks(arrays):
    return [pl.BlockSpec(x.shape, lambda i, z=(0,) * len(x.shape): z) for x in arrays]


def squares(x):
    return jnp.sum(jnp.sum(x * x, 0, keepdims=True), 1, keepdims=True)


def square_end_kernel(where, *refs):
    terms, (extra, wq_squares, mine, other, total_squares, total) = refs[:-6], refs[-6:]
    core = where[0] & 1
    acc = terms[0][0].astype(f32)
    for x in terms[1:]:
        acc = acc + x[0].astype(f32)
    total[...] = acc
    lanes = extra.shape[1]
    total[:, acc.shape[1] - lanes :] += extra[...]
    total_squares[...] = squares(total[...]) + wq_squares[...]
    n = mine.shape[0]
    mine[...] = total[rows_at(core, n), :]
    other[...] = total[rows_at(1 - core, n), :].astype(bf16)


def kv_end_kernel(where, *refs):
    terms, refs = refs[:-9], refs[-9:]
    sq_squares, lat_small, mid_small, in_a, in_b, mine, other, sums, total = refs
    core = where[0] & 1
    acc = terms[0][0].astype(f32)
    for x in terms[1:]:
        acc = acc + x[0].astype(f32)
    total[...] = acc
    n = mine.shape[0]
    mine[...] = total[rows_at(core, n), :]
    other[...] = total[rows_at(1 - core, n), :].astype(bf16)
    sums[...] = jnp.zeros_like(sums)
    sums[0:2, :] = lat_small[...]
    sums[2:4, :] = mid_small[...]
    sums[4:7, 0 : in_a.shape[2]] = in_a[0] + in_b[0]
    sums[7:8, :] = jnp.broadcast_to(squares(acc) + sq_squares[...], (1, sums.shape[1]))


def latent_end_kernel(H, where, *refs):
    terms, (latents, lat_params, extra, small, turned) = refs[:H], refs[H:]
    low = tree_sum([x[...].astype(f32) for x in terms])
    unit, inverse = unit_norm(latents[...])
    once = jnp.where(where[0] == 0, 1.0, 0.0)
    small[0:1, :] = jnp.sum(low * unit, 0, keepdims=True) * once
    small[1:2, :] = jnp.sum(low, 0, keepdims=True) * once
    turned[...] = norm_back(low, unit, inverse, lat_params[0:1, :]).T
    both = turned[rows_at(where[0] >> 1, extra.shape[0]), :]
    n = extra.shape[1]
    extra[...] = jnp.where((where[0] & 1) == 0, both[:, 0:n], both[:, n:])


def update_kernel(where, sums, *refs):
    square, kv, refs = refs[:3], refs[3:6], refs[6:]
    rest, (norm_out, sq_new, sq_moments, kv_new, kv_moments), outs = refs[:7], refs[7:12], refs[12:]
    small = sums[0:7, :]
    norm = jnp.sqrt(jnp.sum(jnp.sum(small * small, 1, keepdims=True), 0, keepdims=True) + sums[7:8, 0:1])
    factor = jnp.minimum(1.0, clip_limit / (norm + 1e-06))
    for (weight, state, gradient), new, moments in ((square, sq_new, sq_moments), (kv, kv_new, kv_moments)):
        new[0, 0], new[1, 0], moments[0, 0], moments[1, 0] = adam_step(
            weight[0], state[0, 0], state[1, 0], state[2, 0], gradient[0] * factor
        )

    @pl.when(pl.program_id(0) == 0)
    def _():
        latents, latents_state, lat_grad, lat_params, lat_state, in_params, in_state = rest
        (latents_new, latents_moments, lat_new, lat_moments, in_new, in_moments, lat_clipped, in_clipped) = outs
        norm_out[...] = norm
        latents_new[0], latents_new[1], latents_moments[0], latents_moments[1] = adam_step(
            latents[...], latents_state[0], latents_state[1], latents_state[2], lat_grad[...] * factor
        )
        lat_clipped[...] = sums[0:4, :] * factor
        lat_new[0], lat_new[1], lat_moments[0], lat_moments[1] = adam_step(
            lat_params[...], lat_state[0], lat_state[1], lat_state[2], lat_clipped[...]
        )
        in_clipped[...] = sums[4:7, 0 : in_params.shape[1]] * factor
        results = adam_step(in_params[...], in_state[0], in_state[1], in_state[2], in_clipped[...])
        for i in range(3):
            row = slice(i, i + 1)
            in_new[i, 0:1], in_new[i, 1:2], in_moments[i, 0:1], in_moments[i, 1:2] = (x[row] for x in results)


def query_back_kernel(H, where, lat_all, w0, mine, other, wq, wq_squares, *refs):
    outs, (grad_q, whole, term) = refs[:H], refs[H:]
    at = Place(where, H)
    half_wide = mine.shape[0]
    grad_q[rows_at(at.core, half_wide), :] = mine[...]
    grad_q[rows_at(1 - at.core, half_wide), :] = other[...]
    term[...] = dot(grad_q[...], w0[...], 0, 0).astype(bf16)
    for m, out in enumerate(outs):
        out[...] = term[rows_at(at.j ^ m, out.shape[0]), :]
    whole[...] = dot(lat_all[...], grad_q[...], 0, 1)
    wq[...] = whole[rows_at(at.s, wq.shape[0]), :]
    wq_squares[...] = squares(wq[...])


def finish_kernel(where, wq, sq_mine, sq_other, kv_mine, kv_other, square_grad, kv_grad, lat_grad):
    core = where[0] & 1
    half = wq.shape[1] // 2
    mine, other = sq_mine[...], sq_other[...].astype(f32)
    low, high = jnp.where(core == 0, mine, other), jnp.where(core == 0, other, mine)
    square_grad[0] = wq[...]
    for m in range(3):
        square_grad[1 + m, :, 0:half] = low[:, m * half : (m + 1) * half]
        square_grad[1 + m, :, half:] = high[:, m * half : (m + 1) * half]
    kv_grad[core] = kv_mine[...]
    kv_grad[1 - core] = kv_other[...].astype(f32)
    n = lat_grad.shape[0] // 2
    ends = slice(3 * half, 3 * half + n)
    lat_grad[...] = jnp.concatenate([low[:, ends], high[:, ends]], 1).T


def on_device(
    inputs,
    mask_flags,
    out_grad,
    square,
    square_state,
    kv_weights,
    kv_state,
    latents,
    latents_state,
    in_params,
    in_state,
    lat_params,
    lat_state,
):
    L = Links()
    S, H = L.S, L.H
    go = Order(jnp.stack([L.s, L.j]).astype(jnp.int32))
    rows, d_in = inputs.shape
    parts = SEQ_LEN // rows
    seqs = H // parts
    lat_rows, d_lat = latents.shape
    nlat = lat_rows * H
    wide = square.shape[2]
    half_wide = wide // 2
    d_part, in_part = d_lat // S, d_in // S
    chips = S // 2
    mine_rows = seqs * lat_rows

    def low(*shape):
        return like(shape, bf16)

    def full(*shape):
        return like(shape, f32)

    square_t, kv_t = jnp.swapaxes(square, 1, 2), jnp.swapaxes(kv_weights, 1, 2)
    (lat_low,) = go(lat_kernel, [latents, lat_params], [low(lat_rows, d_lat)], name="lat_norm")
    kv_pair = go(fix(kv_weight_kernel, H), [kv_t], [low(wide, d_in)] * 2, name="kv_weight")
    kv_first = [L.swap_step(kv_pair[0], i) for i in range(L.hb)]
    lat_near = L.near(lat_low)
    (w0,) = go(
        first_weight_kernel,
        [square_t],
        [low(wide, d_lat)],
        name="first_weight",
        grid=(1,),
        in_specs=[pl.BlockSpec((1, wide, d_lat), lambda i: (0, 0, 0))],
        out_specs=[pl.BlockSpec((wide, d_lat), lambda i: (0, 0))],
    )
    lat_near = [lat_low] + lat_near
    lat_all, query_mine = go(
        fix(query_kernel, H), [*lat_near, w0], [low(nlat, d_lat), low(wide, nlat)], name="query"
    )
    query_near = [query_mine] + L.near(query_mine)
    mask = mask_flags.reshape(rows, 1)
    step = min(rows, 256)
    in_low, in_turned = go(
        token_kernel,
        [inputs, mask, in_params],
        [low(rows, d_in), low(d_in, rows)],
        name="token_norm",
        grid=(rows // step,),
        in_specs=[
            pl.BlockSpec((step, d_in), lambda i: (i, 0)),
            pl.BlockSpec((step, 1), lambda i: (i, 0)),
            pl.BlockSpec(in_params.shape, lambda i: (0, 0)),
        ],
        out_specs=[pl.BlockSpec((step, d_in), lambda i: (i, 0)), pl.BlockSpec((d_in, step), lambda i: (0, i))],
    )
    kv_first = after(kv_first, query_mine)
    kv_mine = [kv_pair[0]] + L.spread(kv_first)
    kv_halves = kv_mine + [kv_pair[1]] + [L.swap_core(x) for x in kv_mine[1:]]
    sq_mine, sq_other = go(
        fix(other_weight_kernel, H),
        [square_t],
        [low(3, half_wide, d_lat)] * 2,
        name="other_weights",
        grid=(3,),
        in_specs=[pl.BlockSpec((1, wide, d_lat), lambda i: (1 + i, 0, 0))],
        out_specs=[pl.BlockSpec((1, half_wide, d_lat), lambda i: (i, 0, 0))] * 2,
    )
    sq_sent = after(sq_mine, kv_mine[-1], *query_near)
    sq_near = [L.swap_step(sq_sent, i) for i in range(L.hb)]

    kv, kv_all = go(
        fix(kv_kernel, H),
        [in_turned, *kv_halves],
        [low(2, d_lat, rows), low(2, d_lat, d_in)],
        [
            pltpu.VMEM((2, d_lat, d_in), bf16),
            pltpu.VMEM((2, d_lat, rows), bf16),
            pltpu.SemaphoreType.DMA((2 * H,)),
            pltpu.SemaphoreType.DMA((5,)),
        ],
        name="kv",
        in_specs=[VMEM] + [ANY] * (2 * H),
        out_specs=[ANY] * 2,
        after=[sq_sent],
    )
    query, *packs = go(
        fix(attention_kernel, H),
        [*query_near, kv],
        [low(d_lat, nlat)] + [low(lat_rows, d_lat + SIDE)] * H,
        [
            pltpu.VMEM((d_lat, nlat), f32),
            pltpu.VMEM((nlat, d_lat + SIDE), bf16),
        ],
        name="attention",
    )
    got = [packs[0]] + [L.swap_hid(packs[m], m) for m in range(1, H)]
    sq_old = lax.dynamic_slice_in_dim(square, L.s * d_part, d_part, 1)
    kv_old = lax.dynamic_slice_in_dim(kv_weights, L.s * in_part, in_part, 1)
    lat_old = lax.dynamic_slice_in_dim(latents, L.s * d_part, d_part, 1)
    (kv_turned,) = go(
        kv_turned_kernel,
        [kv_all],
        [low(2, d_in, d_lat)],
        name="kv_turned",
        grid=(2,),
        in_specs=[pl.BlockSpec((1, d_lat, d_in), lambda i: (i, 0, 0))],
        out_specs=[pl.BlockSpec((1, d_in, d_lat), lambda i: (i, 0, 0))],
        after=[sq_old, kv_old, lat_old],
    )
    in_other = L.swap_core(in_low)
    sq_near = after(sq_near, *got, kv_turned)
    sq_all = [sq_mine] + L.spread(sq_near)
    sq_halves = sq_all + [sq_other] + [L.swap_core(x) for x in sq_all[1:]]

    latents_out, acts, mid_small, res_mine, res_send, *backs = go(
        fix(latent_kernel, H, parts),
        [*got, latents, out_grad, lat_params, *sq_halves],
        [full(mine_rows, d_lat), low(6, mine_rows, d_lat), full(2, d_lat)]
        + [low(lat_rows // 2, d_lat)] * 2
        + [low(lat_rows, d_lat + SIDE)] * H,
        [
            pltpu.VMEM((3, d_lat, d_lat), bf16),
            pltpu.SemaphoreType.DMA((3, 2 * H)),
            pltpu.VMEM((H, lat_rows, d_lat + SIDE), bf16),
            pltpu.VMEM((mine_rows, d_lat), f32),
            pltpu.VMEM((seqs, lat_rows, d_lat + SIDE), bf16),
            pltpu.VMEM((lat_rows, d_lat), bf16),
        ],
        name="latent",
        in_specs=[VMEM] * (H + 3) + [ANY] * (2 * H),
        after=[in_other],
    )
    back = [backs[0]] + [L.swap_hid(backs[m], m) for m in range(1, H)]

    sq_top, sq_low = go(
        fix(square_grad_kernel, H),
        [acts, L.swap_core(acts)],
        [low(H // 2, 3, half_wide, d_lat)] * 2,
        [pltpu.VMEM((3, d_lat, 2 * mine_rows), bf16), pltpu.VMEM((3, 2 * mine_rows, d_lat), bf16)],
        name="square_grad",
    )
    sq = Halving(go, [sq_top], [sq_low], L.hb, L.swap_step, "square")
    sq.start()
    res_other = L.swap_core(res_send)

    gkv_mine, gkv_send, gq_keep, gq_send = go(
        fix(attention_back_kernel, H),
        [query, *back, kv],
        [low(d_lat, rows)] * 2 + [low(H, half_wide, nlat)] * 2,
        [
            pltpu.VMEM((nlat, d_lat + SIDE), bf16),
            pltpu.VMEM((d_lat, nlat), bf16),
            pltpu.VMEM((d_lat, nlat), bf16),
            pltpu.VMEM((2, d_lat, rows), bf16),
        ],
        name="attention_back",
        after=[res_other],
    )
    gkv_got = L.swap_core(gkv_send)
    gq_got = L.swap_core(gq_send)

    in_sums = []
    inputs_grad = None
    block = min(rows // 2, 256)

    def token_grad():
        nonlocal inputs_grad
        first = len(in_sums) * (rows // 2 // block)
        inputs_grad, sums = go(
            token_grad_kernel,
            [inputs, mask, in_params, gkv_mine, gkv_send, kv_turned],
            [full(rows, d_in), full(1, 3, d_in)],
            name="token_grad_%d" % len(in_sums),
            grid=(rows // 2 // block,),
            in_specs=[
                pl.BlockSpec((block, d_in), lambda g: (first + g, 0)),
                pl.BlockSpec((block, 1), lambda g: (first + g, 0)),
                pl.BlockSpec(in_params.shape, lambda g: (0, 0)),
                pl.BlockSpec((d_lat, block), lambda g: (0, first + g)),
                pl.BlockSpec((d_lat, block), lambda g: (0, first + g)),
                pl.BlockSpec(kv_turned.shape, lambda g: (0, 0, 0)),
            ],
            out_specs=[
                pl.BlockSpec((block, d_in), lambda g: (first + g, 0)),
                pl.BlockSpec((1, 3, d_in), lambda g: (0, 0, 0)),
            ],
            onto=inputs_grad,
        )
        in_sums.append(sums)

    token_grad()
    gq_all = go(query_core_kernel, [gq_keep, gq_got], [low(half_wide, nlat)] * H, name="query_core")
    gq_near = [L.swap_hid(gq_all[m], m) for m in range(1, H)]
    sq.terms = after(sq.terms, *gq_near)
    sq.step()
    gq_mine = go.tree([gq_all[0]] + gq_near, "query_hid")
    gq_chips = L.near_chips(gq_mine)
    kv_top, kv_low = go(
        fix(kv_grad_kernel, H),
        [gkv_mine, gkv_got, in_low, in_other],
        [low(H // 2, wide, d_in)] * 2,
        [pltpu.VMEM((d_lat, d_in), bf16)],
        name="kv_grad",
    )
    kv_sums = Halving(go, [kv_top], [kv_low], L.hb, L.swap_step, "kv")
    kv_sums.start()

    lanes = 3 * half_wide + lat_rows // 2
    padded = -(-lanes // 128) * 128

    def turn_to_chips(kernel, terms, extra, n, lanes, padded, name):
        d = terms[0].shape[-1]
        out = [low(chips // 2, n, lanes)] * 2
        return go(
            kernel,
            [*terms, *extra],
            out,
            [pltpu.VMEM((padded, d), f32), pltpu.VMEM((d, padded), bf16)],
            name=name,
            grid=(1,),
            in_specs=first_blocks(terms) + whole_blocks(extra),
            out_specs=whole_blocks(out),
        )

    n = L.sb - 1

    def chip_step(x, i):
        return L.swap_seq(x, 2 << (n - 1 - i))

    def end(kernel, terms, extra, n, lanes, more, name, after=()):
        outs = [full(n, lanes), low(n, lanes)] + more
        return go(
            kernel,
            [*terms, *extra],
            outs,
            [pltpu.VMEM((2 * n, lanes), f32)],
            name=name,
            grid=(1,),
            in_specs=first_blocks(terms) + whole_blocks(extra),
            out_specs=whole_blocks(outs),
            after=after,
        )

    for _ in range(L.hb - 2):
        sq.step()
        kv_sums.step()
    gq_mine = go.tree([gq_mine] + gq_chips, "query_chips")
    gq_other = L.swap_core(gq_mine)
    sq_top, sq_low = turn_to_chips(
        square_turn_kernel, sq.terms, [res_mine, res_other], 2 * d_part, lanes, padded, "square_turn"
    )
    sq_chips = Halving(go, [sq_top], [sq_low], n, chip_step, "square_chip")
    sq_chips.start()
    wq_part, wq_squares, *lat_blocks = go(
        fix(query_back_kernel, H),
        [lat_all, w0, gq_mine, gq_other],
        [full(d_part, wide), full(1, 1)] + [low(lat_rows, d_lat)] * H,
        [pltpu.VMEM((wide, nlat), bf16), pltpu.VMEM((d_lat, wide), f32), pltpu.VMEM((nlat, d_lat), bf16)],
        name="query_back",
    )
    lat_near = [L.swap_hid(lat_blocks[m], m) for m in range(1, H)]
    kv_sums.step()
    sq_chips.step()
    kv_top, kv_low = turn_to_chips(kv_turn_kernel, kv_sums.terms, [], 2 * in_part, wide, wide, "kv_turn")
    kv_chips = Halving(go, [kv_top], [kv_low], n, chip_step, "kv_chip")
    kv_chips.start()
    lat_extra, lat_small = go(
        fix(latent_end_kernel, H),
        [lat_blocks[0], *lat_near, latents, lat_params],
        [full(2 * d_part, lat_rows // 2), full(2, d_lat)],
        [pltpu.VMEM((d_lat, lat_rows), f32)],
        name="latent_end",
    )
    token_grad()
    kv_chips.step()
    for _ in range(n - 2):
        sq_chips.step()
        kv_chips.step()
    sq_mine, sq_send, sq_squares = end(
        square_end_kernel,
        sq_chips.terms,
        [lat_extra, wq_squares],
        d_part,
        lanes,
        [full(1, 1)],
        "square_end",
    )
    sq_other = L.swap_core(sq_send)
    kv_mine, kv_send, sums = end(
        kv_end_kernel,
        kv_chips.terms,
        [sq_squares, lat_small, mid_small, *in_sums],
        in_part,
        wide,
        [full(8, d_lat)],
        "kv_end",
    )
    kv_other = L.swap_core(kv_send)

    square_grad, kv_grad, lat_grad = go(
        finish_kernel,
        [wq_part, sq_mine, sq_other, kv_mine, kv_other],
        [full(4, d_part, wide), full(2, in_part, wide), full(lat_rows, d_part)],
        name="finish",
    )
    sums = L.sum_all(sums, square_grad)
    pair = [full(3, 2, d_in)] * 2
    rest = [lat_old, latents_state, lat_grad, lat_params, lat_state, in_params, in_state]
    outs = [full(2, *lat_old.shape)] * 2 + [full(2, *lat_params.shape)] * 2 + pair
    outs += [full(*lat_params.shape), full(*in_params.shape)]
    half = in_part // 2
    sq_out = pl.BlockSpec((2, 1, d_part, wide), lambda g: (0, g, 0, 0))
    kv_out = pl.BlockSpec((2, 1, half, wide), lambda g: (0, g // 2, g % 2, 0))
    results = go(
        update_kernel,
        [sums, sq_old, square_state, square_grad, kv_old, kv_state, kv_grad, *rest],
        [full(1, 1)] + [full(2, *sq_old.shape)] * 2 + [full(2, *kv_old.shape)] * 2 + outs,
        name="update",
        grid=(4,),
        in_specs=whole_blocks([sums])
        + [
            pl.BlockSpec((1, d_part, wide), lambda g: (g, 0, 0)),
            pl.BlockSpec((3, 1, d_part, wide), lambda g: (0, g, 0, 0)),
            pl.BlockSpec((1, d_part, wide), lambda g: (g, 0, 0)),
            pl.BlockSpec((1, half, wide), lambda g: (g // 2, g % 2, 0)),
            pl.BlockSpec((3, 1, half, wide), lambda g: (0, g // 2, g % 2, 0)),
            pl.BlockSpec((1, half, wide), lambda g: (g // 2, g % 2, 0)),
        ]
        + whole_blocks(rest),
        out_specs=whole_blocks([full(1, 1)]) + [sq_out] * 2 + [kv_out] * 2 + whole_blocks(outs),
    )
    (grad_norm, square_new, square_moments, kv_new, kv_moments, latents_new, latents_moments) = results[:7]
    (lat_new, lat_moments, in_new, in_moments, lat_clipped, in_clipped) = results[7:]
    grad_norm = grad_norm[0, 0]
    in_new, in_moments = jnp.swapaxes(in_new, 0, 1), jnp.swapaxes(in_moments, 0, 1)
    return (
        latents_out.reshape(seqs, lat_rows, d_lat),
        inputs_grad,
        grad_norm,
        square_new,
        square_moments,
        kv_new,
        kv_moments,
        latents_new,
        latents_moments,
        in_new,
        in_moments,
        lat_new,
        lat_moments,
        in_clipped,
        lat_clipped,
    )


def solution(mesh):
    return jax.shard_map(
        on_device,
        mesh=mesh,
        in_specs=(
            P(("seq", "hid"), None),
            P(("seq", "hid")),
            P("seq", "hid", None),
            P(None, None, "hid"),
            P(None, None, "seq", "hid"),
            P(None, None, "hid"),
            P(None, None, "seq", "hid"),
            P("hid", None),
            P(None, "hid", "seq"),
            P(),
            P(),
            P(),
            P(),
        ),
        out_specs=(
            P("seq", "hid", None),
            P(("seq", "hid"), None),
            P(),
            P(None, None, "seq", "hid"),
            P(None, None, "seq", "hid"),
            P(None, None, "seq", "hid"),
            P(None, None, "seq", "hid"),
            P(None, "hid", "seq"),
            P(None, "hid", "seq"),
            P(),
            P(),
            P(),
            P(),
            P(),
            P(),
        ),
        check_vma=False,
    )
```

```python
from functools import partial as fix
import math

import jax
import jax.numpy as jnp
from jax import lax
from jax.experimental import pallas as pl
from jax.experimental.pallas import tpu as pltpu
from jax.sharding import PartitionSpec as P

HEADS = 8
HEAD = 160
SEQ_LEN = 2048
STEP = 10
SIDE = 128


clip_limit = 1.0
beta_one = 0.9
beta_two = 0.999
adam_eps = 1e-08
learn_rate = 0.05
decay_rate = 0.01
ema_keep = 0.9
norm_eps = 1e-05
score_scale = 1.0 / math.sqrt(HEAD)
score_two = score_scale * math.log2(math.e)

f32 = jnp.float32
bf16 = jnp.bfloat16


def unit_norm(values):
    centre = jnp.mean(values, -1, keepdims=True)
    centred = values - centre
    inverse = lax.rsqrt(jnp.mean(centred * centred, -1, keepdims=True) + norm_eps)
    return centred * inverse, inverse


def norm_back(upstream, unit_rows, inverse, scale_row):
    scaled = upstream * scale_row
    inner_mean = jnp.mean(scaled, -1, keepdims=True)
    along_mean = jnp.mean(scaled * unit_rows, -1, keepdims=True)
    return inverse * (scaled - inner_mean - unit_rows * along_mean)


def adam_step(weight, first, root, average, gradient):
    moment_one = beta_one * first + (1.0 - beta_one) * gradient
    root_two = jnp.sqrt(beta_two * root * root + (1.0 - beta_two) * gradient * gradient)
    corrected_one = moment_one * (learn_rate / (1.0 - beta_one**STEP))
    denominator = root_two * (1.0 / math.sqrt(1.0 - beta_two**STEP)) + adam_eps
    new_weight = weight * (1.0 - learn_rate * decay_rate) - corrected_one / denominator
    ema_new = ema_keep * average + (1.0 - ema_keep) * new_weight
    return new_weight, ema_new, moment_one, root_two


def dot(a, b, over_a, over_b):
    return lax.dot_general(a, b, (((over_a,), (over_b,)), ((), ())), preferred_element_type=f32)


def flip(value, bits):
    out = 0
    for i in range(bits):
        out = out + ((value >> i) & 1) * (1 << (bits - 1 - i))
    return out


class Links:
    def __init__(self):
        self.S = lax.axis_size("seq")
        self.H = lax.axis_size("hid")
        self.hb = self.H.bit_length() - 1
        self.sb = self.S.bit_length() - 1
        self.s = lax.axis_index("seq")
        self.j = lax.axis_index("hid")
        self.core = self.s & 1
        self.paired = self.H == 4 and self.S >= 4

    def side(self, s):
        return (s & 1) ^ ((s >> 1) & 1) if self.paired else s & 1

    def swap(self, x, dest):
        pairs = []
        for s in range(self.S):
            for j in range(self.H):
                ds, dj = dest(s, j)
                pairs.append((s * self.H + j, ds * self.H + dj))
        return lax.ppermute(x, ("seq", "hid"), pairs)

    def swap_core(self, x):
        return self.swap(x, lambda s, j: (s ^ 1, j))

    def swap_hid(self, x, mask):
        return self.swap(x, lambda s, j: (s, j ^ mask))

    def swap_seq(self, x, mask):
        return self.swap(x, lambda s, j: (s ^ mask, j))

    def swap_step(self, x, i):
        even, odd = 1 << i, 1 << (self.hb - 1 - i)
        return self.swap(x, lambda s, j: (s, j ^ (odd if self.side(s) else even)))

    def first(self, x):
        return [self.swap_step(x, i) for i in range(1 if self.paired else self.hb)]

    def spread(self, first):
        if self.paired:
            return [first[0], self.swap_seq(first[0], 2), self.swap_step(first[0], 1)]
        blocks = [None]
        for i, x in enumerate(first):
            blocks += [x] + [self.swap_step(y, i) for y in blocks[1:]]
        return blocks[1:]

    def near(self, x):
        return [self.swap_hid(x, m) for m in range(1, self.H)]

    def near_chips(self, x):
        return [self.swap_seq(x, 2 * m) for m in range(1, self.S // 2)]

    def sum_all(self, x, last):
        x = x + self.swap_core(x)
        x = tree_sum([x] + self.near(x))
        return tree_sum([x] + after(self.near_chips(x), last))


def tree_sum(terms):
    while len(terms) > 1:
        terms = [a + b for a, b in zip(terms[::2], terms[1::2])]
    return terms[0]


class Place:
    def __init__(self, where, H):
        self.H = H
        self.hb = H.bit_length() - 1
        self.s = where[0]
        self.j = where[1]
        self.core = self.s & 1
        self.parity = where[2]

    def block(self, r, core):
        return self.j ^ jnp.where((core ^ self.parity) == 0, r, flip(r, self.hb))

    def halves(self):
        mine = [(self.block(r, self.core), self.core) for r in range(self.H)]
        return mine + [(self.block(r, 1 - self.core), 1 - self.core) for r in range(self.H)]


def after(x, *others):
    return lax.optimization_barrier((x, others))[0]


def rows_at(index, size):
    return pl.ds(pl.multiple_of(index * size, size), size)


VMEM = pl.BlockSpec(memory_space=pltpu.VMEM)
SMEM = pl.BlockSpec(memory_space=pltpu.SMEM)
ANY = pl.BlockSpec(memory_space=pl.ANY)


spent = {
    "kv_weight": 5.0,
    "first_weight": 0.1,
    "query": 4.0,
    "token_norm": 10.0,
    "other_weights": 0.1,
    "kv": 0.1,
    "attention": 0.1,
    "kv_turned": 0.1,
    "latent": 11.0,
    "square_grad": 5.0,
    "attention_back": 12.0,
    "token_grad_0": 22.0,
    "query_core": 0.1,
    "square_step": 4.0,
    "query_hid": 0.1,
    "kv_grad": 1.0,
    "query_chips": 10.0,
    "square_turn": 0.1,
    "query_back": 0.1,
    "kv_step": 0.1,
    "square_chip_step": 0.1,
    "kv_turn": 0.1,
    "latent_end": 3.0,
    "token_grad_1": 0.1,
    "kv_chip_step": 0.1,
    "square_end": 3.0,
    "update": 7.0,
}


class Order:
    def __init__(self, where):
        self.where = where
        self.last = []

    def __call__(
        self, kernel, args, outs, scratch=(), name=None, grid=(), in_specs=None, out_specs=None, after=(), onto=None
    ):
        n = len(args)
        waits = self.last + list(after)
        if onto is not None:
            waits = [onto] + waits

        def body(where, *refs):
            kernel(where, *refs[:n], *refs[n + len(waits) :])

        results = pl.pallas_call(
            body,
            out_shape=outs,
            grid=grid,
            in_specs=[SMEM] + (in_specs or [VMEM] * n) + [ANY] * len(waits),
            out_specs=out_specs or [VMEM] * len(outs),
            scratch_shapes=list(scratch),
            compiler_params=pltpu.CompilerParams(vmem_limit_bytes=56 * 1024 * 1024),
            cost_estimate=pl.CostEstimate(
                flops=int(spent.get(name, 2.0) * 1e9), bytes_accessed=0, transcendentals=0
            ),
            name=name,
            input_output_aliases={} if onto is None else {1 + n: 0},
        )(self.where, *args, *waits)
        self.last = [results[-1]]
        return results

    def tree(self, terms, name):
        def kernel(where, *refs):
            refs[-1][...] = tree_sum([x[...].astype(f32) for x in refs[:-1]]).astype(bf16)

        return self(kernel, terms, [like(terms[0].shape, bf16)], name=name)[0]

    def add(self, terms, block, count, name):
        shape = terms[0].shape[1:]
        parts = shape[0] if len(shape) == 3 else 1
        terms = [x.reshape((x.shape[0], parts) + shape[-2:]) for x in terms]

        def kernel(where, *refs):
            out = refs[-1]
            acc = refs[0][...].astype(f32)
            for x in refs[1:-1]:
                acc = acc + x[...].astype(f32)
            out[...] = acc.astype(bf16)

        size = (1, 1) + shape[-2:]
        (out,) = self(
            kernel,
            terms,
            [like((count, parts) + shape[-2:], bf16)],
            name=name,
            grid=(count, parts),
            in_specs=[pl.BlockSpec(size, lambda i, m: (block * count + i, m, 0, 0))] * len(terms),
            out_specs=[pl.BlockSpec(size, lambda i, m: (i, m, 0, 0))],
        )
        return out.reshape((count,) + shape)


def like(shape, dtype):
    return jax.ShapeDtypeStruct(tuple(shape), dtype)


class Halving:
    def __init__(self, go, top, low, bits, swap, name):
        self.go, self.top, self.terms, self.bits, self.swap, self.name = go, top, low, bits, swap, name

    def start(self):
        i = self.bits - 1
        sending = self.top[0] if len(self.top) == 1 else self.go.add(self.top, 0, 1 << i, self.name + "_top")
        self.terms = self.terms + [self.swap(sending, i)]
        self.at = i

    def step(self):
        n = 1 << (self.at - 1)
        sending = self.go.add(self.terms, 1, n, self.name + "_step")
        self.at -= 1
        self.terms = self.terms + [self.swap(sending, self.at)]


def lat_kernel(where, latents, lat_params, out):
    unit, _ = unit_norm(latents[...])
    out[...] = (unit * lat_params[0:1, :] + lat_params[1:2, :]).astype(bf16)


def kv_weight_kernel(H, where, kv, mine, other):
    at = Place(where, H)
    mine[...] = kv[at.core].astype(bf16)
    other[...] = kv[1 - at.core].astype(bf16)


def first_weight_kernel(where, weight, out):
    out[...] = weight[0].astype(bf16)


def other_weight_kernel(H, where, weight, mine, other):
    at = Place(where, H)
    n = mine.shape[1]
    mine[0] = weight[0, rows_at(at.core, n), :].astype(bf16)
    other[0] = weight[0, rows_at(1 - at.core, n), :].astype(bf16)


def query_kernel(H, where, *refs):
    near, (w0, lat_all, query) = refs[:H], refs[H:]
    at = Place(where, H)
    n = near[0].shape[0]
    for m, x in enumerate(near):
        lat_all[rows_at(at.j ^ m, n), :] = x[...]
    query[...] = dot(w0[...], lat_all[...], 1, 1).astype(bf16)


def token_kernel(where, inputs, mask, in_params, out, turned):
    masked = jnp.where(mask[...] > 0, in_params[2:3, :], inputs[...])
    unit, _ = unit_norm(masked)
    low = (unit * in_params[0:1, :] + in_params[1:2, :]).astype(bf16)
    out[...] = low
    turned[...] = low.T


def started(copies):
    for copy in copies:
        copy.start()
    return copies


def waited(copies):
    for copy in copies:
        copy.wait()


def kv_kernel(H, where, in_turned, *refs):
    halves, (kv, kv_all, weights, product, sems, out_sems) = refs[: 2 * H], refs[2 * H :]
    at = Place(where, H)
    wide = halves[0].shape[0]
    d_lat = wide * H
    copies = started(
        [
            pltpu.make_async_copy(halves[i], weights.at[which, rows_at(block, wide), :], sems.at[i])
            for i, (block, which) in enumerate(at.halves())
        ]
    )
    waited(copies)
    outs = started([pltpu.make_async_copy(weights, kv_all, out_sems.at[4])])
    for which in range(2):
        for part in range(2):
            span = slice(part * d_lat // 2, (part + 1) * d_lat // 2)
            product[which, span, :] = dot(weights[which, span, :], in_turned[...], 1, 0).astype(bf16)
            copy = pltpu.make_async_copy(
                product.at[which, span, :], kv.at[which, span, :], out_sems.at[2 * which + part]
            )
            outs += started([copy])
    waited(outs)


def kv_turned_kernel(where, kv_all, out):
    out[0] = kv_all[0].T


def three_way(x, lane):
    a = x.astype(bf16).astype(f32)
    b = (x - a).astype(bf16).astype(f32)
    part = (lane // HEADS) % 3
    return jnp.where(part == 0, a, jnp.where(part == 1, b, x - a - b)).astype(bf16)


def three_sum(x):
    return x + pltpu.roll(x, SIDE - HEADS, 1) + pltpu.roll(x, SIDE - 2 * HEADS, 1)


def attention_kernel(H, where, *refs):
    near, kv, query = refs[:H], refs[H], refs[H + 1]
    packs, (mix, packed) = refs[H + 2 : -2], refs[-2:]
    at = Place(where, H)
    n = near[0].shape[0]
    for m, x in enumerate(near):
        query[rows_at(at.j ^ m, n), :] = x[...]
    d_lat, nlat = query.shape
    lane = lax.broadcasted_iota(jnp.int32, (nlat, SIDE), 1)
    logs = jnp.zeros((nlat, SIDE), f32)
    for h in range(HEADS):
        span = slice(h * HEAD, (h + 1) * HEAD)
        scores = dot(query[span, :], kv[0, span, :], 0, 0)
        peak = jnp.max(scores, -1, keepdims=True)
        weight = jnp.exp2((scores - peak) * score_two)
        total = jnp.sum(weight, -1, keepdims=True)
        probs = (weight * (1.0 / total)).astype(bf16)
        mix[span, :] = dot(kv[1, span, :], probs, 1, 1)
        log_part = peak * score_two + jnp.log2(total)
        logs = jnp.where((lane % HEADS == h) & (lane < 3 * HEADS), log_part, logs)
    packed[:, :d_lat] = mix[...].T.astype(bf16)
    packed[:, d_lat:] = three_way(logs, lane)
    lat_rows = nlat // H
    for m, out in enumerate(packs):
        out[...] = packed[rows_at(at.j ^ m, lat_rows), :]


def head_lanes(shape):
    return lax.broadcasted_iota(jnp.int32, shape, 1) // HEAD


def latent_kernel(H, parts, where, *refs):
    seqs = H // parts
    got, refs = refs[:H], refs[H:]
    latents, out_grad, lat_params, refs = refs[0], refs[1], refs[2], refs[3:]
    pieces, refs = refs[: 2 * H], refs[2 * H :]
    (latents_out, acts, small, res_mine, res_send), refs = refs[:5], refs[5:]
    attended, up_grad, hidden, branch_grad, mid_low, grad_y = (acts.at[i] for i in range(6))
    backs, (weights, sems, gathered, att, packed, res) = refs[:H], refs[H:]
    at = Place(where, H)
    lat_rows, d_lat = latents.shape
    half_wide = pieces[0].shape[1]
    copies = []
    for m in range(3):
        group = []
        for i, (block, half) in enumerate(at.halves()):
            group.append(
                pltpu.make_async_copy(
                    pieces[i].at[m],
                    weights.at[m, rows_at(block * 2 + half, half_wide), :],
                    sems.at[m, i],
                )
            )
            group[-1].start()
        copies.append(group)

    def arrived(m):
        for copy in copies[m]:
            copy.wait()

    for m in range(H):
        gathered[at.j ^ m] = got[m][...]
    heads = head_lanes((lat_rows, d_lat))
    log_totals = []
    for b in range(seqs):
        logs = [three_sum(gathered[b * parts + p, :, d_lat:].astype(f32)) for p in range(parts)]
        peak = logs[0]
        for x in logs[1:]:
            peak = jnp.maximum(peak, x)
        log_total = peak + jnp.log2(sum(jnp.exp2(x - peak) for x in logs))
        log_totals.append(log_total)
        mixed = jnp.zeros((lat_rows, d_lat), f32)
        for p in range(parts):
            share = jnp.exp2(logs[p] - log_total)
            spread = jnp.zeros((lat_rows, d_lat), f32)
            for h in range(HEADS):
                spread = jnp.where(heads == h, share[:, h : h + 1], spread)
            mixed = mixed + spread * gathered[b * parts + p, :, :d_lat].astype(f32)
        att[b * lat_rows : (b + 1) * lat_rows, :] = mixed
    attended[...] = att[...].astype(bf16)
    grad_y[...] = jnp.concatenate([out_grad[b] for b in range(seqs)], 0).astype(bf16)

    arrived(0)
    branch = dot(attended[...], weights[0], 1, 0)
    residual = jnp.concatenate([latents[...]] * seqs, 0) + branch
    unit, inverse = unit_norm(residual)
    mid_low[...] = (unit * lat_params[2:3, :] + lat_params[3:4, :]).astype(bf16)
    arrived(1)
    up_proj = dot(mid_low[...], weights[1], 1, 1)
    below = 0.5 + 0.5 * lax.erf(up_proj * math.sqrt(0.5))
    hidden[...] = (up_proj * below).astype(bf16)
    slope = below + up_proj * jnp.exp(-0.5 * up_proj * up_proj) * (1.0 / math.sqrt(2.0 * math.pi))
    arrived(2)
    latents_out[...] = residual + dot(hidden[...], weights[2], 1, 0)
    up_grad[...] = (dot(grad_y[...], weights[2], 1, 1) * slope).astype(bf16)
    grad_mid = dot(up_grad[...], weights[1], 1, 0)
    small[0:1, :] = jnp.sum(grad_mid * unit, 0, keepdims=True)
    small[1:2, :] = jnp.sum(grad_mid, 0, keepdims=True)
    grad_residual = jnp.concatenate([out_grad[b] for b in range(seqs)], 0) + norm_back(
        grad_mid, unit, inverse, lat_params[2:3, :]
    )
    branch_grad[...] = grad_residual.astype(bf16)
    folded = grad_residual[0:lat_rows]
    for b in range(1, seqs):
        folded = folded + grad_residual[b * lat_rows : (b + 1) * lat_rows]
    res[...] = folded.astype(bf16)
    res_mine[...] = res[rows_at(at.core, lat_rows // 2), :]
    res_send[...] = res[rows_at(1 - at.core, lat_rows // 2), :]
    grad_att = dot(branch_grad[...], weights[0], 1, 1).astype(bf16)
    along = grad_att.astype(f32) * att[...]
    heads = head_lanes((seqs * lat_rows, d_lat))
    lane = lax.broadcasted_iota(jnp.int32, (lat_rows, SIDE), 1)
    inner = []
    for h in range(HEADS):
        lo, hi = h * HEAD // 128 * 128, -(-(h + 1) * HEAD // 128) * 128
        inner.append(jnp.sum(jnp.where(heads[:, lo:hi] == h, along[:, lo:hi], 0.0), -1, keepdims=True))
    for b in range(seqs):
        t = log_totals[b]
        side = jnp.where(lane < HEADS, t, jnp.where(lane < 2 * HEADS, pltpu.roll(t, HEADS, 1), pltpu.roll(t, 2 * HEADS, 1)))
        for h in range(HEADS):
            own = (lane % HEADS == h) & (lane >= 3 * HEADS)
            side = jnp.where(own, inner[h][b * lat_rows : (b + 1) * lat_rows], side)
        side = jnp.where(lane < 6 * HEADS, side, 0.0)
        packed[b, :, :d_lat] = grad_att[b * lat_rows : (b + 1) * lat_rows]
        packed[b, :, d_lat:] = three_way(side, lane)
    for m, out in enumerate(backs):
        out[...] = packed[(at.j ^ m) // parts]


def square_grad_kernel(H, where, acts, others, top, low, turned, rights):
    at = Place(where, H)
    rows = acts.shape[1]
    for m in range(3):
        turned[m, :, 0:rows] = acts[m].T
        turned[m, :, rows:] = others[m].T
        rights[m, 0:rows, :] = acts[3 + m]
        rights[m, rows:, :] = others[3 + m]
    half_wide = top.shape[2]
    for r in range(H):
        out = low if r < H // 2 else top
        at_row = rows_at(at.block(r, at.core) * 2 + at.core, half_wide)
        for m in range(3):
            out[r % (H // 2), m] = dot(turned[m, at_row, :], rights[m], 1, 0).astype(bf16)


def attention_back_kernel(H, where, query, *refs):
    backs, refs = refs[:H], refs[H:]
    kv, mine, send, q_keep, q_send, packed, turned, grad_q, grad_kv = refs
    at = Place(where, H)
    d_lat, nlat = query.shape
    lat_rows = nlat // H
    for m in range(H):
        packed[rows_at(at.j ^ m, lat_rows), :] = backs[m][...]
    turned[...] = packed[:, :d_lat].T
    side = three_sum(packed[:, d_lat:].astype(f32))
    for h in range(HEADS):
        span = slice(h * HEAD, (h + 1) * HEAD)
        scores = dot(query[span, :], kv[0, span, :], 0, 0)
        probs = jnp.exp2(scores * score_two - side[:, h : h + 1])
        grad_kv[1, span, :] = dot(turned[span, :], probs.astype(bf16), 1, 0).astype(bf16)
        grad_probs = dot(turned[span, :], kv[1, span, :], 0, 0)
        grad_scores = (probs * (grad_probs - side[:, 3 * HEADS + h : 3 * HEADS + h + 1])).astype(bf16)
        grad_q[span, :] = (dot(kv[0, span, :], grad_scores, 1, 1) * score_scale).astype(bf16)
        grad_kv[0, span, :] = (dot(query[span, :], grad_scores, 1, 0) * score_scale).astype(bf16)
    n = q_keep.shape[1]
    for m in range(H):
        block = (at.j ^ m) * 2
        q_keep[m] = grad_q[rows_at(block + at.core, n), :]
        q_send[m] = grad_q[rows_at(block + 1 - at.core, n), :]
    mine[...] = grad_kv[at.core]
    send[...] = grad_kv[1 - at.core]


def query_core_kernel(where, keep, got, *outs):
    for m, out in enumerate(outs):
        out[...] = (keep[m].astype(f32) + got[m].astype(f32)).astype(bf16)


def slots_out(at, core, whole, top, low):
    n = top.shape[1]
    per = whole.shape[0] // (at.H * n)
    for r in range(at.H):
        out = low if r < at.H // 2 else top
        block = at.block(r, core)
        out[r % (at.H // 2)] = whole[rows_at(block * 2 + core if per == 2 else block, n), :]


def kv_grad_kernel(H, where, mine, got, in_low, in_other, top, low, whole):
    at = Place(where, H)
    whole[...] = (dot(mine[...], in_low[...], 1, 0) + dot(got[...], in_other[...], 1, 0)).astype(bf16)
    slots_out(at, at.core, whole, top, low)


def token_grad_kernel(where, inputs, mask, in_params, mine, send, weights, inputs_grad, small):
    core = where[0] & 1
    upstream = (dot(weights[core], mine[...], 1, 0) + dot(weights[1 - core], send[...], 1, 0)).T
    masked_row = mask[...] > 0
    unit, inverse = unit_norm(jnp.where(masked_row, in_params[2:3, :], inputs[...]))
    grad = norm_back(upstream, unit, inverse, in_params[0:1, :])
    inputs_grad[...] = jnp.where(masked_row, 0.0, grad)

    @pl.when(pl.program_id(0) == 0)
    def _():
        small[...] = jnp.zeros_like(small)

    for r, term in enumerate((upstream * unit, upstream, jnp.where(masked_row, grad, 0.0))):
        small[0, r : r + 1, :] += jnp.sum(term, 0, keepdims=True)


def turn(where, total, turned, top, low):
    turned[...] = total[...].T.astype(bf16)
    chip = where[0] >> 1
    half, rows, lanes = top.shape
    for r in range(2 * half):
        out = low if r < half else top
        out[r % half] = turned[rows_at(chip ^ flip(r, half.bit_length()), rows), 0:lanes]


def square_turn_kernel(where, *refs):
    terms, (lat_mine, lat_other, top, low, total, turned) = refs[:-6], refs[-6:]
    half = terms[0].shape[2]
    for m in range(3):
        acc = terms[0][0, m].astype(f32)
        for x in terms[1:]:
            acc = acc + x[0, m].astype(f32)
        total[m * half : (m + 1) * half, :] = acc
    n = lat_mine.shape[0]
    total[3 * half : 3 * half + n, :] = lat_mine[...].astype(f32) + lat_other[...].astype(f32)
    if 3 * half + n < total.shape[0]:
        total[3 * half + n :, :] = jnp.zeros((total.shape[0] - 3 * half - n, total.shape[1]), f32)
    turn(where, total, turned, top, low)


def kv_turn_kernel(where, *refs):
    terms, (top, low, total, turned) = refs[:-4], refs[-4:]
    acc = terms[0][0].astype(f32)
    for x in terms[1:]:
        acc = acc + x[0].astype(f32)
    total[...] = acc
    turn(where, total, turned, top, low)


def first_blocks(terms):
    return [pl.BlockSpec((1,) + x.shape[1:], lambda i, z=(0,) * x.ndim: z) for x in terms]


def whole_blocks(arrays):
    return [pl.BlockSpec(x.shape, lambda i, z=(0,) * len(x.shape): z) for x in arrays]


def squares(x):
    return jnp.sum(jnp.sum(x * x, 0, keepdims=True), 1, keepdims=True)


def square_end_kernel(where, *refs):
    terms, (extra, wq_squares, mine, other, total_squares, total) = refs[:-6], refs[-6:]
    core = where[0] & 1
    acc = terms[0][0].astype(f32)
    for x in terms[1:]:
        acc = acc + x[0].astype(f32)
    total[...] = acc
    lanes = extra.shape[1]
    total[:, acc.shape[1] - lanes :] += extra[...]
    total_squares[...] = squares(total[...]) + wq_squares[...]
    n = mine.shape[0]
    mine[...] = total[rows_at(core, n), :]
    other[...] = total[rows_at(1 - core, n), :].astype(bf16)


def kv_end_kernel(where, *refs):
    terms, refs = refs[:-9], refs[-9:]
    sq_squares, lat_small, mid_small, in_a, in_b, mine, other, sums, total = refs
    core = where[0] & 1
    acc = terms[0][0].astype(f32)
    for x in terms[1:]:
        acc = acc + x[0].astype(f32)
    total[...] = acc
    n = mine.shape[0]
    mine[...] = total[rows_at(core, n), :]
    other[...] = total[rows_at(1 - core, n), :].astype(bf16)
    sums[...] = jnp.zeros_like(sums)
    sums[0:2, :] = lat_small[...]
    sums[2:4, :] = mid_small[...]
    sums[4:7, 0 : in_a.shape[2]] = in_a[0] + in_b[0]
    sums[7:8, :] = jnp.broadcast_to(squares(acc) + sq_squares[...], (1, sums.shape[1]))


def latent_end_kernel(H, where, *refs):
    terms, (latents, lat_params, extra, small, turned) = refs[:H], refs[H:]
    low = tree_sum([x[...].astype(f32) for x in terms])
    unit, inverse = unit_norm(latents[...])
    once = jnp.where(where[0] == 0, 1.0, 0.0)
    small[0:1, :] = jnp.sum(low * unit, 0, keepdims=True) * once
    small[1:2, :] = jnp.sum(low, 0, keepdims=True) * once
    turned[...] = norm_back(low, unit, inverse, lat_params[0:1, :]).T
    both = turned[rows_at(where[0] >> 1, extra.shape[0]), :]
    n = extra.shape[1]
    extra[...] = jnp.where((where[0] & 1) == 0, both[:, 0:n], both[:, n:])


def update_kernel(where, sums, *refs):
    square, kv, refs = refs[:3], refs[3:6], refs[6:]
    rest, (norm_out, sq_new, sq_moments, kv_new, kv_moments), outs = refs[:7], refs[7:12], refs[12:]
    small = sums[0:7, :]
    norm = jnp.sqrt(jnp.sum(jnp.sum(small * small, 1, keepdims=True), 0, keepdims=True) + sums[7:8, 0:1])
    factor = jnp.minimum(1.0, clip_limit / (norm + 1e-06))
    for (weight, state, gradient), new, moments in ((square, sq_new, sq_moments), (kv, kv_new, kv_moments)):
        new[0, 0], new[1, 0], moments[0, 0], moments[1, 0] = adam_step(
            weight[0], state[0, 0], state[1, 0], state[2, 0], gradient[0] * factor
        )

    @pl.when(pl.program_id(0) == 0)
    def _():
        latents, latents_state, lat_grad, lat_params, lat_state, in_params, in_state = rest
        (latents_new, latents_moments, lat_new, lat_moments, in_new, in_moments, lat_clipped, in_clipped) = outs
        norm_out[...] = norm
        latents_new[0], latents_new[1], latents_moments[0], latents_moments[1] = adam_step(
            latents[...], latents_state[0], latents_state[1], latents_state[2], lat_grad[...] * factor
        )
        lat_clipped[...] = sums[0:4, :] * factor
        lat_new[0], lat_new[1], lat_moments[0], lat_moments[1] = adam_step(
            lat_params[...], lat_state[0], lat_state[1], lat_state[2], lat_clipped[...]
        )
        in_clipped[...] = sums[4:7, 0 : in_params.shape[1]] * factor
        results = adam_step(in_params[...], in_state[0], in_state[1], in_state[2], in_clipped[...])
        for i in range(3):
            row = slice(i, i + 1)
            in_new[i, 0:1], in_new[i, 1:2], in_moments[i, 0:1], in_moments[i, 1:2] = (x[row] for x in results)


def query_back_kernel(H, where, lat_all, w0, mine, other, wq, wq_squares, *refs):
    outs, (grad_q, whole, term) = refs[:H], refs[H:]
    at = Place(where, H)
    half_wide = mine.shape[0]
    grad_q[rows_at(at.core, half_wide), :] = mine[...]
    grad_q[rows_at(1 - at.core, half_wide), :] = other[...]
    term[...] = dot(grad_q[...], w0[...], 0, 0).astype(bf16)
    for m, out in enumerate(outs):
        out[...] = term[rows_at(at.j ^ m, out.shape[0]), :]
    whole[...] = dot(lat_all[...], grad_q[...], 0, 1)
    wq[...] = whole[rows_at(at.s, wq.shape[0]), :]
    wq_squares[...] = squares(wq[...])


def finish_kernel(where, wq, sq_mine, sq_other, kv_mine, kv_other, square_grad, kv_grad, lat_grad):
    core = where[0] & 1
    half = wq.shape[1] // 2
    mine, other = sq_mine[...], sq_other[...].astype(f32)
    low, high = jnp.where(core == 0, mine, other), jnp.where(core == 0, other, mine)
    square_grad[0] = wq[...]
    for m in range(3):
        square_grad[1 + m, :, 0:half] = low[:, m * half : (m + 1) * half]
        square_grad[1 + m, :, half:] = high[:, m * half : (m + 1) * half]
    kv_grad[core] = kv_mine[...]
    kv_grad[1 - core] = kv_other[...].astype(f32)
    n = lat_grad.shape[0] // 2
    ends = slice(3 * half, 3 * half + n)
    lat_grad[...] = jnp.concatenate([low[:, ends], high[:, ends]], 1).T


def on_device(
    inputs,
    mask_flags,
    out_grad,
    square,
    square_state,
    kv_weights,
    kv_state,
    latents,
    latents_state,
    in_params,
    in_state,
    lat_params,
    lat_state,
):
    L = Links()
    S, H = L.S, L.H
    parity = (L.s >> 1) & 1 if L.paired else 0 * L.s
    go = Order(jnp.stack([L.s, L.j, parity]).astype(jnp.int32))
    rows, d_in = inputs.shape
    parts = SEQ_LEN // rows
    seqs = H // parts
    lat_rows, d_lat = latents.shape
    nlat = lat_rows * H
    wide = square.shape[2]
    half_wide = wide // 2
    d_part, in_part = d_lat // S, d_in // S
    chips = S // 2
    mine_rows = seqs * lat_rows

    def low(*shape):
        return like(shape, bf16)

    def full(*shape):
        return like(shape, f32)

    square_t, kv_t = jnp.swapaxes(square, 1, 2), jnp.swapaxes(kv_weights, 1, 2)
    (lat_low,) = go(lat_kernel, [latents, lat_params], [low(lat_rows, d_lat)], name="lat_norm")
    kv_pair = go(fix(kv_weight_kernel, H), [kv_t], [low(wide, d_in)] * 2, name="kv_weight")
    kv_first = L.first(kv_pair[0])
    lat_near = L.near(lat_low)
    (w0,) = go(
        first_weight_kernel,
        [square_t],
        [low(wide, d_lat)],
        name="first_weight",
        grid=(1,),
        in_specs=[pl.BlockSpec((1, wide, d_lat), lambda i: (0, 0, 0))],
        out_specs=[pl.BlockSpec((wide, d_lat), lambda i: (0, 0))],
    )
    lat_near = [lat_low] + lat_near
    lat_all, query_mine = go(
        fix(query_kernel, H), [*lat_near, w0], [low(nlat, d_lat), low(wide, nlat)], name="query"
    )
    query_near = [query_mine] + L.near(query_mine)
    mask = mask_flags.reshape(rows, 1)
    step = min(rows, 256)
    in_low, in_turned = go(
        token_kernel,
        [inputs, mask, in_params],
        [low(rows, d_in), low(d_in, rows)],
        name="token_norm",
        grid=(rows // step,),
        in_specs=[
            pl.BlockSpec((step, d_in), lambda i: (i, 0)),
            pl.BlockSpec((step, 1), lambda i: (i, 0)),
            pl.BlockSpec(in_params.shape, lambda i: (0, 0)),
        ],
        out_specs=[pl.BlockSpec((step, d_in), lambda i: (i, 0)), pl.BlockSpec((d_in, step), lambda i: (0, i))],
    )
    kv_first = after(kv_first, query_mine)
    kv_mine = [kv_pair[0]] + L.spread(kv_first)
    kv_halves = kv_mine + [kv_pair[1]] + [L.swap_core(x) for x in kv_mine[1:]]
    sq_mine, sq_other = go(
        fix(other_weight_kernel, H),
        [square_t],
        [low(3, half_wide, d_lat)] * 2,
        name="other_weights",
        grid=(3,),
        in_specs=[pl.BlockSpec((1, wide, d_lat), lambda i: (1 + i, 0, 0))],
        out_specs=[pl.BlockSpec((1, half_wide, d_lat), lambda i: (i, 0, 0))] * 2,
    )
    sq_sent = after(sq_mine, *kv_mine[1:], *query_near)
    sq_first = L.first(sq_sent)

    kv, kv_all = go(
        fix(kv_kernel, H),
        [in_turned, *kv_halves],
        [low(2, d_lat, rows), low(2, d_lat, d_in)],
        [
            pltpu.VMEM((2, d_lat, d_in), bf16),
            pltpu.VMEM((2, d_lat, rows), bf16),
            pltpu.SemaphoreType.DMA((2 * H,)),
            pltpu.SemaphoreType.DMA((5,)),
        ],
        name="kv",
        in_specs=[VMEM] + [ANY] * (2 * H),
        out_specs=[ANY] * 2,
        after=[sq_sent],
    )
    sq_all = [sq_mine] + L.spread(after(sq_first, kv))
    in_other = L.swap_core(in_low)
    query, *packs = go(
        fix(attention_kernel, H),
        [*query_near, kv],
        [low(d_lat, nlat)] + [low(lat_rows, d_lat + SIDE)] * H,
        [
            pltpu.VMEM((d_lat, nlat), f32),
            pltpu.VMEM((nlat, d_lat + SIDE), bf16),
        ],
        name="attention",
        after=[in_other],
    )
    got = [packs[0]] + [L.swap_hid(packs[m], m) for m in range(1, H)]
    sq_old = lax.dynamic_slice_in_dim(square, L.s * d_part, d_part, 1)
    kv_old = lax.dynamic_slice_in_dim(kv_weights, L.s * in_part, in_part, 1)
    lat_old = lax.dynamic_slice_in_dim(latents, L.s * d_part, d_part, 1)
    (kv_turned,) = go(
        kv_turned_kernel,
        [kv_all],
        [low(2, d_in, d_lat)],
        name="kv_turned",
        grid=(2,),
        in_specs=[pl.BlockSpec((1, d_lat, d_in), lambda i: (i, 0, 0))],
        out_specs=[pl.BlockSpec((1, d_in, d_lat), lambda i: (i, 0, 0))],
        after=[sq_old, kv_old, lat_old],
    )
    sq_all = after(sq_all, *got, kv_turned)
    sq_halves = sq_all + [sq_other] + [L.swap_core(x) for x in sq_all[1:]]

    latents_out, acts, mid_small, res_mine, res_send, *backs = go(
        fix(latent_kernel, H, parts),
        [*got, latents, out_grad, lat_params, *sq_halves],
        [full(mine_rows, d_lat), low(6, mine_rows, d_lat), full(2, d_lat)]
        + [low(lat_rows // 2, d_lat)] * 2
        + [low(lat_rows, d_lat + SIDE)] * H,
        [
            pltpu.VMEM((3, d_lat, d_lat), bf16),
            pltpu.SemaphoreType.DMA((3, 2 * H)),
            pltpu.VMEM((H, lat_rows, d_lat + SIDE), bf16),
            pltpu.VMEM((mine_rows, d_lat), f32),
            pltpu.VMEM((seqs, lat_rows, d_lat + SIDE), bf16),
            pltpu.VMEM((lat_rows, d_lat), bf16),
        ],
        name="latent",
        in_specs=[VMEM] * (H + 3) + [ANY] * (2 * H),
    )
    back = [backs[0]] + [L.swap_hid(backs[m], m) for m in range(1, H)]

    sq_top, sq_low = go(
        fix(square_grad_kernel, H),
        [acts, L.swap_core(acts)],
        [low(H // 2, 3, half_wide, d_lat)] * 2,
        [pltpu.VMEM((3, d_lat, 2 * mine_rows), bf16), pltpu.VMEM((3, 2 * mine_rows, d_lat), bf16)],
        name="square_grad",
    )
    sq = Halving(go, [sq_top], [sq_low], L.hb, L.swap_step, "square")
    sq.start()
    res_other = L.swap_core(res_send)

    gkv_mine, gkv_send, gq_keep, gq_send = go(
        fix(attention_back_kernel, H),
        [query, *back, kv],
        [low(d_lat, rows)] * 2 + [low(H, half_wide, nlat)] * 2,
        [
            pltpu.VMEM((nlat, d_lat + SIDE), bf16),
            pltpu.VMEM((d_lat, nlat), bf16),
            pltpu.VMEM((d_lat, nlat), bf16),
            pltpu.VMEM((2, d_lat, rows), bf16),
        ],
        name="attention_back",
        after=[res_other],
    )
    gkv_got = L.swap_core(gkv_send)
    gq_got = L.swap_core(gq_send)

    in_sums = []
    inputs_grad = None
    block = min(rows // 2, 256)

    def token_grad():
        nonlocal inputs_grad
        first = len(in_sums) * (rows // 2 // block)
        inputs_grad, sums = go(
            token_grad_kernel,
            [inputs, mask, in_params, gkv_mine, gkv_send, kv_turned],
            [full(rows, d_in), full(1, 3, d_in)],
            name="token_grad_%d" % len(in_sums),
            grid=(rows // 2 // block,),
            in_specs=[
                pl.BlockSpec((block, d_in), lambda g: (first + g, 0)),
                pl.BlockSpec((block, 1), lambda g: (first + g, 0)),
                pl.BlockSpec(in_params.shape, lambda g: (0, 0)),
                pl.BlockSpec((d_lat, block), lambda g: (0, first + g)),
                pl.BlockSpec((d_lat, block), lambda g: (0, first + g)),
                pl.BlockSpec(kv_turned.shape, lambda g: (0, 0, 0)),
            ],
            out_specs=[
                pl.BlockSpec((block, d_in), lambda g: (first + g, 0)),
                pl.BlockSpec((1, 3, d_in), lambda g: (0, 0, 0)),
            ],
            onto=inputs_grad,
        )
        in_sums.append(sums)

    gq_all = go(query_core_kernel, [gq_keep, gq_got], [low(half_wide, nlat)] * H, name="query_core")
    gq_near = [L.swap_hid(gq_all[m], m) for m in range(1, H)]
    token_grad()
    sq.terms = after(sq.terms, *gq_near)
    sq.step()
    gq_mine = go.tree([gq_all[0]] + gq_near, "query_hid")
    gq_chips = L.near_chips(gq_mine)
    kv_top, kv_low = go(
        fix(kv_grad_kernel, H),
        [gkv_mine, gkv_got, in_low, in_other],
        [low(H // 2, wide, d_in)] * 2,
        [pltpu.VMEM((d_lat, d_in), bf16)],
        name="kv_grad",
    )
    kv_sums = Halving(go, [kv_top], [kv_low], L.hb, L.swap_step, "kv")
    kv_sums.start()

    lanes = 3 * half_wide + lat_rows // 2
    padded = -(-lanes // 128) * 128

    def turn_to_chips(kernel, terms, extra, n, lanes, padded, name):
        d = terms[0].shape[-1]
        out = [low(chips // 2, n, lanes)] * 2
        return go(
            kernel,
            [*terms, *extra],
            out,
            [pltpu.VMEM((padded, d), f32), pltpu.VMEM((d, padded), bf16)],
            name=name,
            grid=(1,),
            in_specs=first_blocks(terms) + whole_blocks(extra),
            out_specs=whole_blocks(out),
        )

    n = L.sb - 1

    def chip_step(x, i):
        return L.swap_seq(x, 2 << (n - 1 - i))

    def end(kernel, terms, extra, n, lanes, more, name, after=()):
        outs = [full(n, lanes), low(n, lanes)] + more
        return go(
            kernel,
            [*terms, *extra],
            outs,
            [pltpu.VMEM((2 * n, lanes), f32)],
            name=name,
            grid=(1,),
            in_specs=first_blocks(terms) + whole_blocks(extra),
            out_specs=whole_blocks(outs),
            after=after,
        )

    for _ in range(L.hb - 2):
        sq.step()
        kv_sums.step()
    gq_mine = go.tree([gq_mine] + gq_chips, "query_chips")
    gq_other = L.swap_core(gq_mine)
    sq_top, sq_low = turn_to_chips(
        square_turn_kernel, sq.terms, [res_mine, res_other], 2 * d_part, lanes, padded, "square_turn"
    )
    sq_chips = Halving(go, [sq_top], [sq_low], n, chip_step, "square_chip")
    sq_chips.start()
    wq_part, wq_squares, *lat_blocks = go(
        fix(query_back_kernel, H),
        [lat_all, w0, gq_mine, gq_other],
        [full(d_part, wide), full(1, 1)] + [low(lat_rows, d_lat)] * H,
        [pltpu.VMEM((wide, nlat), bf16), pltpu.VMEM((d_lat, wide), f32), pltpu.VMEM((nlat, d_lat), bf16)],
        name="query_back",
    )
    lat_near = [L.swap_hid(lat_blocks[m], m) for m in range(1, H)]
    kv_sums.step()
    sq_chips.step()
    kv_top, kv_low = turn_to_chips(kv_turn_kernel, kv_sums.terms, [], 2 * in_part, wide, wide, "kv_turn")
    kv_chips = Halving(go, [kv_top], [kv_low], n, chip_step, "kv_chip")
    kv_chips.start()
    lat_extra, lat_small = go(
        fix(latent_end_kernel, H),
        [lat_blocks[0], *lat_near, latents, lat_params],
        [full(2 * d_part, lat_rows // 2), full(2, d_lat)],
        [pltpu.VMEM((d_lat, lat_rows), f32)],
        name="latent_end",
    )
    token_grad()
    kv_chips.step()
    for _ in range(n - 2):
        sq_chips.step()
        kv_chips.step()
    sq_mine, sq_send, sq_squares = end(
        square_end_kernel,
        sq_chips.terms,
        [lat_extra, wq_squares],
        d_part,
        lanes,
        [full(1, 1)],
        "square_end",
    )
    sq_other = L.swap_core(sq_send)
    kv_mine, kv_send, sums = end(
        kv_end_kernel,
        kv_chips.terms,
        [sq_squares, lat_small, mid_small, *in_sums],
        in_part,
        wide,
        [full(8, d_lat)],
        "kv_end",
    )
    kv_other = L.swap_core(kv_send)

    square_grad, kv_grad, lat_grad = go(
        finish_kernel,
        [wq_part, sq_mine, sq_other, kv_mine, kv_other],
        [full(4, d_part, wide), full(2, in_part, wide), full(lat_rows, d_part)],
        name="finish",
    )
    sums = L.sum_all(sums, square_grad)
    pair = [full(3, 2, d_in)] * 2
    rest = [lat_old, latents_state, lat_grad, lat_params, lat_state, in_params, in_state]
    outs = [full(2, *lat_old.shape)] * 2 + [full(2, *lat_params.shape)] * 2 + pair
    outs += [full(*lat_params.shape), full(*in_params.shape)]
    half = in_part // 2
    sq_out = pl.BlockSpec((2, 1, d_part, wide), lambda g: (0, g, 0, 0))
    kv_out = pl.BlockSpec((2, 1, half, wide), lambda g: (0, g // 2, g % 2, 0))
    results = go(
        update_kernel,
        [sums, sq_old, square_state, square_grad, kv_old, kv_state, kv_grad, *rest],
        [full(1, 1)] + [full(2, *sq_old.shape)] * 2 + [full(2, *kv_old.shape)] * 2 + outs,
        name="update",
        grid=(4,),
        in_specs=whole_blocks([sums])
        + [
            pl.BlockSpec((1, d_part, wide), lambda g: (g, 0, 0)),
            pl.BlockSpec((3, 1, d_part, wide), lambda g: (0, g, 0, 0)),
            pl.BlockSpec((1, d_part, wide), lambda g: (g, 0, 0)),
            pl.BlockSpec((1, half, wide), lambda g: (g // 2, g % 2, 0)),
            pl.BlockSpec((3, 1, half, wide), lambda g: (0, g // 2, g % 2, 0)),
            pl.BlockSpec((1, half, wide), lambda g: (g // 2, g % 2, 0)),
        ]
        + whole_blocks(rest),
        out_specs=whole_blocks([full(1, 1)]) + [sq_out] * 2 + [kv_out] * 2 + whole_blocks(outs),
    )
    (grad_norm, square_new, square_moments, kv_new, kv_moments, latents_new, latents_moments) = results[:7]
    (lat_new, lat_moments, in_new, in_moments, lat_clipped, in_clipped) = results[7:]
    grad_norm = grad_norm[0, 0]
    in_new, in_moments = jnp.swapaxes(in_new, 0, 1), jnp.swapaxes(in_moments, 0, 1)
    return (
        latents_out.reshape(seqs, lat_rows, d_lat),
        inputs_grad,
        grad_norm,
        square_new,
        square_moments,
        kv_new,
        kv_moments,
        latents_new,
        latents_moments,
        in_new,
        in_moments,
        lat_new,
        lat_moments,
        in_clipped,
        lat_clipped,
    )


def solution(mesh):
    return jax.shard_map(
        on_device,
        mesh=mesh,
        in_specs=(
            P(("seq", "hid"), None),
            P(("seq", "hid")),
            P("seq", "hid", None),
            P(None, None, "hid"),
            P(None, None, "seq", "hid"),
            P(None, None, "hid"),
            P(None, None, "seq", "hid"),
            P("hid", None),
            P(None, "hid", "seq"),
            P(),
            P(),
            P(),
            P(),
        ),
        out_specs=(
            P("seq", "hid", None),
            P(("seq", "hid"), None),
            P(),
            P(None, None, "seq", "hid"),
            P(None, None, "seq", "hid"),
            P(None, None, "seq", "hid"),
            P(None, None, "seq", "hid"),
            P(None, "hid", "seq"),
            P(None, "hid", "seq"),
            P(),
            P(),
            P(),
            P(),
            P(),
            P(),
        ),
        check_vma=False,
    )
```

```python
from functools import partial as fix
import math

import jax
import jax.numpy as jnp
from jax import lax
from jax.experimental import pallas as pl
from jax.experimental.pallas import tpu as pltpu
from jax.sharding import PartitionSpec as P

HEADS = 8
HEAD = 160
SEQ_LEN = 2048
STEP = 10
SIDE = 128


clip_limit = 1.0
beta_one = 0.9
beta_two = 0.999
adam_eps = 1e-08
learn_rate = 0.05
decay_rate = 0.01
ema_keep = 0.9
norm_eps = 1e-05
score_scale = 1.0 / math.sqrt(HEAD)
score_two = score_scale * math.log2(math.e)

f32 = jnp.float32
bf16 = jnp.bfloat16


def unit_norm(values):
    centre = jnp.mean(values, -1, keepdims=True)
    centred = values - centre
    inverse = lax.rsqrt(jnp.mean(centred * centred, -1, keepdims=True) + norm_eps)
    return centred * inverse, inverse


def norm_back(upstream, unit_rows, inverse, scale_row):
    scaled = upstream * scale_row
    inner_mean = jnp.mean(scaled, -1, keepdims=True)
    along_mean = jnp.mean(scaled * unit_rows, -1, keepdims=True)
    return inverse * (scaled - inner_mean - unit_rows * along_mean)


def adam_step(weight, first, root, average, gradient):
    moment_one = beta_one * first + (1.0 - beta_one) * gradient
    root_two = jnp.sqrt(beta_two * root * root + (1.0 - beta_two) * gradient * gradient)
    corrected_one = moment_one * (learn_rate / (1.0 - beta_one**STEP))
    denominator = root_two * (1.0 / math.sqrt(1.0 - beta_two**STEP)) + adam_eps
    new_weight = weight * (1.0 - learn_rate * decay_rate) - corrected_one / denominator
    ema_new = ema_keep * average + (1.0 - ema_keep) * new_weight
    return new_weight, ema_new, moment_one, root_two


def dot(a, b, over_a, over_b):
    return lax.dot_general(a, b, (((over_a,), (over_b,)), ((), ())), preferred_element_type=f32)


def flip(value, bits):
    out = 0
    for i in range(bits):
        out = out + ((value >> i) & 1) * (1 << (bits - 1 - i))
    return out


class Links:
    def __init__(self):
        self.S = lax.axis_size("seq")
        self.H = lax.axis_size("hid")
        self.hb = self.H.bit_length() - 1
        self.sb = self.S.bit_length() - 1
        self.s = lax.axis_index("seq")
        self.j = lax.axis_index("hid")
        self.core = self.s & 1
        self.paired = self.H == 4 and self.S >= 4

    def side(self, s):
        return (s & 1) ^ ((s >> 1) & 1) if self.paired else s & 1

    def swap(self, x, dest):
        pairs = []
        for s in range(self.S):
            for j in range(self.H):
                ds, dj = dest(s, j)
                pairs.append((s * self.H + j, ds * self.H + dj))
        return lax.ppermute(x, ("seq", "hid"), pairs)

    def swap_core(self, x):
        return self.swap(x, lambda s, j: (s ^ 1, j))

    def swap_hid(self, x, mask):
        return self.swap(x, lambda s, j: (s, j ^ mask))

    def swap_seq(self, x, mask):
        return self.swap(x, lambda s, j: (s ^ mask, j))

    def swap_step(self, x, i):
        even, odd = 1 << i, 1 << (self.hb - 1 - i)
        return self.swap(x, lambda s, j: (s, j ^ (odd if self.side(s) else even)))

    def first(self, x):
        return [self.swap_step(x, i) for i in range(1 if self.paired else self.hb)]

    def spread(self, first):
        if self.paired:
            return [first[0], self.swap_seq(first[0], 2), self.swap_step(first[0], 1)]
        blocks = [None]
        for i, x in enumerate(first):
            blocks += [x] + [self.swap_step(y, i) for y in blocks[1:]]
        return blocks[1:]

    def near(self, x):
        return [self.swap_hid(x, m) for m in range(1, self.H)]

    def near_chips(self, x):
        return [self.swap_seq(x, 2 * m) for m in range(1, self.S // 2)]

    def sum_all(self, x, last):
        x = x + self.swap_core(x)
        x = tree_sum([x] + self.near(x))
        return tree_sum([x] + after(self.near_chips(x), last))


def tree_sum(terms):
    while len(terms) > 1:
        terms = [a + b for a, b in zip(terms[::2], terms[1::2])]
    return terms[0]


class Place:
    def __init__(self, where, H):
        self.H = H
        self.hb = H.bit_length() - 1
        self.s = where[0]
        self.j = where[1]
        self.core = self.s & 1
        self.parity = where[2]

    def block(self, r, core):
        return self.j ^ jnp.where((core ^ self.parity) == 0, r, flip(r, self.hb))

    def halves(self):
        mine = [(self.block(r, self.core), self.core) for r in range(self.H)]
        return mine + [(self.block(r, 1 - self.core), 1 - self.core) for r in range(self.H)]


def after(x, *others):
    return lax.optimization_barrier((x, others))[0]


def rows_at(index, size):
    return pl.ds(pl.multiple_of(index * size, size), size)


VMEM = pl.BlockSpec(memory_space=pltpu.VMEM)
SMEM = pl.BlockSpec(memory_space=pltpu.SMEM)
ANY = pl.BlockSpec(memory_space=pl.ANY)


spent = {
    "kv_weight": 5.0,
    "first_weight": 0.1,
    "query": 4.0,
    "token_norm": 10.0,
    "other_weights": 0.1,
    "kv": 0.1,
    "attention": 0.1,
    "kv_turned": 0.1,
    "latent": 11.0,
    "square_grad": 5.0,
    "attention_back": 12.0,
    "token_grad_0": 7.5,
    "query_core": 0.1,
    "square_step": 20.0,
    "query_hid": 0.1,
    "kv_grad": 1.0,
    "query_chips": 5.0,
    "square_turn": 0.1,
    "query_back": 0.1,
    "kv_step": 0.1,
    "square_chip_step": 0.1,
    "kv_turn": 0.1,
    "latent_end": 0.1,
    "token_grad_1": 0.1,
    "kv_chip_step": 0.1,
    "square_end": 0.1,
    "update": 7.0,
}


class Order:
    def __init__(self, where):
        self.where = where
        self.last = []

    def __call__(
        self, kernel, args, outs, scratch=(), name=None, grid=(), in_specs=None, out_specs=None, after=(), onto=None
    ):
        n = len(args)
        waits = self.last + list(after)
        if onto is not None:
            waits = [onto] + waits

        def body(where, *refs):
            kernel(where, *refs[:n], *refs[n + len(waits) :])

        if grid:
            room = 20 << 20
        else:
            held = [x for x, spec in zip(args, in_specs or [VMEM] * n) if spec is not ANY]
            held += [x for x, spec in zip(outs, out_specs or [VMEM] * len(outs)) if spec is not ANY]
            held += [x for x in scratch if "semaphore" not in str(x.dtype) and "dma" not in str(x.dtype)]
            room = sum(math.prod(x.shape) * jnp.dtype(x.dtype).itemsize for x in held) * 5 // 4 + (10 << 20)
        results = pl.pallas_call(
            body,
            out_shape=outs,
            grid=grid,
            in_specs=[SMEM] + (in_specs or [VMEM] * n) + [ANY] * len(waits),
            out_specs=out_specs or [VMEM] * len(outs),
            scratch_shapes=list(scratch),
            compiler_params=pltpu.CompilerParams(vmem_limit_bytes=min(room, 58 << 20)),
            cost_estimate=pl.CostEstimate(
                flops=int(spent.get(name, 2.0) * 1e9), bytes_accessed=0, transcendentals=0
            ),
            name=name,
            input_output_aliases={} if onto is None else {1 + n: 0},
        )(self.where, *args, *waits)
        self.last = [results[-1]]
        return results

    def tree(self, terms, name):
        def kernel(where, *refs):
            refs[-1][...] = tree_sum([x[...].astype(f32) for x in refs[:-1]]).astype(bf16)

        return self(kernel, terms, [like(terms[0].shape, bf16)], name=name)[0]

    def add(self, terms, block, count, name):
        shape = terms[0].shape[1:]
        parts = shape[0] if len(shape) == 3 else 1
        terms = [x.reshape((x.shape[0], parts) + shape[-2:]) for x in terms]

        def kernel(where, *refs):
            out = refs[-1]
            acc = refs[0][...].astype(f32)
            for x in refs[1:-1]:
                acc = acc + x[...].astype(f32)
            out[...] = acc.astype(bf16)

        size = (1, 1) + shape[-2:]
        (out,) = self(
            kernel,
            terms,
            [like((count, parts) + shape[-2:], bf16)],
            name=name,
            grid=(count, parts),
            in_specs=[pl.BlockSpec(size, lambda i, m: (block * count + i, m, 0, 0))] * len(terms),
            out_specs=[pl.BlockSpec(size, lambda i, m: (i, m, 0, 0))],
        )
        return out.reshape((count,) + shape)


def like(shape, dtype):
    return jax.ShapeDtypeStruct(tuple(shape), dtype)


class Halving:
    def __init__(self, go, top, low, bits, swap, name):
        self.go, self.top, self.terms, self.bits, self.swap, self.name = go, top, low, bits, swap, name

    def start(self):
        i = self.bits - 1
        sending = self.top[0] if len(self.top) == 1 else self.go.add(self.top, 0, 1 << i, self.name + "_top")
        self.terms = self.terms + [self.swap(sending, i)]
        self.at = i

    def step(self):
        n = 1 << (self.at - 1)
        sending = self.go.add(self.terms, 1, n, self.name + "_step")
        self.at -= 1
        self.terms = self.terms + [self.swap(sending, self.at)]


class Slots:
    def __init__(self, L, go, slots, name):
        self.L, self.go, self.name = L, go, name
        self.slots = [[x] for x in slots]
        self.early = []
        if L.paired:
            came = L.swap_step(slots[3], 1)
            self.slots[1] += [came, L.swap_seq(slots[2], 2)]
            self.early = [came]
            self.steps = [1]
        else:
            for r in range(L.H // 2, L.H):
                self.slots[r - L.H // 2].append(L.swap_step(slots[r], L.hb - 1))
            self.steps = list(reversed(range(1, L.H // 2)))

    def hold(self, *others):
        for r in self.steps[:1]:
            self.slots[r] = after(self.slots[r], *others)

    def step(self):
        r, self.steps = self.steps[0], self.steps[1:]
        i = r.bit_length() - 1
        sending = self.go.add(self.slots[r], 0, 1, self.name + "_step")
        self.slots[r - (1 << i)].append(self.L.swap_step(sending, i))

    @property
    def terms(self):
        while self.steps:
            self.step()
        return self.slots[0]


def lat_kernel(where, latents, lat_params, out):
    unit, _ = unit_norm(latents[...])
    out[...] = (unit * lat_params[0:1, :] + lat_params[1:2, :]).astype(bf16)


def kv_weight_kernel(H, where, kv, mine, other):
    at = Place(where, H)
    mine[...] = kv[at.core].astype(bf16)
    other[...] = kv[1 - at.core].astype(bf16)


def first_weight_kernel(where, weight, out):
    out[...] = weight[0].astype(bf16)


def other_weight_kernel(H, where, weight, mine, other):
    at = Place(where, H)
    n = mine.shape[1]
    mine[0] = weight[0, rows_at(at.core, n), :].astype(bf16)
    other[0] = weight[0, rows_at(1 - at.core, n), :].astype(bf16)


def query_kernel(H, where, *refs):
    near, (w0, lat_all, query) = refs[:H], refs[H:]
    at = Place(where, H)
    n = near[0].shape[0]
    for m, x in enumerate(near):
        lat_all[rows_at(at.j ^ m, n), :] = x[...]
    query[...] = dot(w0[...], lat_all[...], 1, 1).astype(bf16)


def token_kernel(where, inputs, mask, in_params, out, turned):
    masked = jnp.where(mask[...] > 0, in_params[2:3, :], inputs[...])
    unit, _ = unit_norm(masked)
    low = (unit * in_params[0:1, :] + in_params[1:2, :]).astype(bf16)
    out[...] = low
    turned[...] = low.T


def started(copies):
    for copy in copies:
        copy.start()
    return copies


def waited(copies):
    for copy in copies:
        copy.wait()


def kv_kernel(H, where, in_turned, *refs):
    halves, (kv, weights, sems) = refs[: 2 * H], refs[2 * H :]
    at = Place(where, H)
    wide = halves[0].shape[0]
    d_lat = wide * H
    copies = started(
        [
            pltpu.make_async_copy(halves[i], weights.at[which, rows_at(block, wide), :], sems.at[i])
            for i, (block, which) in enumerate(at.halves())
        ]
    )
    waited(copies)
    for which in range(2):
        kv[which] = dot(weights[which], in_turned[...], 1, 0).astype(bf16)


def kv_turned_kernel(where, kv_all, out):
    out[0] = kv_all[0].T


def three_way(x, lane):
    a = x.astype(bf16).astype(f32)
    b = (x - a).astype(bf16).astype(f32)
    part = (lane // HEADS) % 3
    return jnp.where(part == 0, a, jnp.where(part == 1, b, x - a - b)).astype(bf16)


def three_sum(x):
    return x + pltpu.roll(x, SIDE - HEADS, 1) + pltpu.roll(x, SIDE - 2 * HEADS, 1)


def attention_kernel(H, where, *refs):
    near, kv, query = refs[:H], refs[H], refs[H + 1]
    packs, (mix, packed) = refs[H + 2 : -2], refs[-2:]
    at = Place(where, H)
    n = near[0].shape[0]
    for m, x in enumerate(near):
        query[rows_at(at.j ^ m, n), :] = x[...]
    d_lat, nlat = query.shape
    lane = lax.broadcasted_iota(jnp.int32, (nlat, SIDE), 1)
    logs = jnp.zeros((nlat, SIDE), f32)
    for h in range(HEADS):
        span = slice(h * HEAD, (h + 1) * HEAD)
        scores = dot(query[span, :], kv[0, span, :], 0, 0)
        peak = jnp.max(scores, -1, keepdims=True)
        weight = jnp.exp2((scores - peak) * score_two)
        total = jnp.sum(weight, -1, keepdims=True)
        probs = (weight * (1.0 / total)).astype(bf16)
        mix[span, :] = dot(kv[1, span, :], probs, 1, 1)
        log_part = peak * score_two + jnp.log2(total)
        logs = jnp.where((lane % HEADS == h) & (lane < 3 * HEADS), log_part, logs)
    packed[:, :d_lat] = mix[...].T.astype(bf16)
    packed[:, d_lat:] = three_way(logs, lane)
    lat_rows = nlat // H
    for m, out in enumerate(packs):
        out[...] = packed[rows_at(at.j ^ m, lat_rows), :]


def head_lanes(shape):
    return lax.broadcasted_iota(jnp.int32, shape, 1) // HEAD


def latent_kernel(H, parts, where, *refs):
    seqs = H // parts
    got, refs = refs[:H], refs[H:]
    latents, out_grad, lat_params, refs = refs[0], refs[1], refs[2], refs[3:]
    pieces, refs = refs[: 2 * H], refs[2 * H :]
    (latents_out, acts, small, res_mine, res_send), refs = refs[:5], refs[5:]
    attended, up_grad, hidden, branch_grad, mid_low, grad_y = (acts.at[i] for i in range(6))
    backs, (weights, sems, gathered, att, packed, res) = refs[:H], refs[H:]
    at = Place(where, H)
    lat_rows, d_lat = latents.shape
    half_wide = pieces[0].shape[1]
    copies = []
    for m in range(3):
        group = []
        for i, (block, half) in enumerate(at.halves()):
            group.append(
                pltpu.make_async_copy(
                    pieces[i].at[m],
                    weights.at[m, rows_at(block * 2 + half, half_wide), :],
                    sems.at[m, i],
                )
            )
            group[-1].start()
        copies.append(group)

    def arrived(m):
        for copy in copies[m]:
            copy.wait()

    for m in range(H):
        gathered[at.j ^ m] = got[m][...]
    heads = head_lanes((lat_rows, d_lat))
    log_totals = []
    for b in range(seqs):
        logs = [three_sum(gathered[b * parts + p, :, d_lat:].astype(f32)) for p in range(parts)]
        peak = logs[0]
        for x in logs[1:]:
            peak = jnp.maximum(peak, x)
        log_total = peak + jnp.log2(sum(jnp.exp2(x - peak) for x in logs))
        log_totals.append(log_total)
        mixed = jnp.zeros((lat_rows, d_lat), f32)
        for p in range(parts):
            share = jnp.exp2(logs[p] - log_total)
            spread = jnp.zeros((lat_rows, d_lat), f32)
            for h in range(HEADS):
                spread = jnp.where(heads == h, share[:, h : h + 1], spread)
            mixed = mixed + spread * gathered[b * parts + p, :, :d_lat].astype(f32)
        att[b * lat_rows : (b + 1) * lat_rows, :] = mixed
    attended[...] = att[...].astype(bf16)
    grad_y[...] = jnp.concatenate([out_grad[b] for b in range(seqs)], 0).astype(bf16)

    arrived(0)
    branch = dot(attended[...], weights[0], 1, 0)
    residual = jnp.concatenate([latents[...]] * seqs, 0) + branch
    unit, inverse = unit_norm(residual)
    mid_low[...] = (unit * lat_params[2:3, :] + lat_params[3:4, :]).astype(bf16)
    arrived(1)
    up_proj = dot(mid_low[...], weights[1], 1, 1)
    below = 0.5 + 0.5 * lax.erf(up_proj * math.sqrt(0.5))
    hidden[...] = (up_proj * below).astype(bf16)
    slope = below + up_proj * jnp.exp(-0.5 * up_proj * up_proj) * (1.0 / math.sqrt(2.0 * math.pi))
    arrived(2)
    latents_out[...] = residual + dot(hidden[...], weights[2], 1, 0)
    up_grad[...] = (dot(grad_y[...], weights[2], 1, 1) * slope).astype(bf16)
    grad_mid = dot(up_grad[...], weights[1], 1, 0)
    small[0:1, :] = jnp.sum(grad_mid * unit, 0, keepdims=True)
    small[1:2, :] = jnp.sum(grad_mid, 0, keepdims=True)
    grad_residual = jnp.concatenate([out_grad[b] for b in range(seqs)], 0) + norm_back(
        grad_mid, unit, inverse, lat_params[2:3, :]
    )
    branch_grad[...] = grad_residual.astype(bf16)
    folded = grad_residual[0:lat_rows]
    for b in range(1, seqs):
        folded = folded + grad_residual[b * lat_rows : (b + 1) * lat_rows]
    res[...] = folded.astype(bf16)
    res_mine[...] = res[rows_at(at.core, lat_rows // 2), :]
    res_send[...] = res[rows_at(1 - at.core, lat_rows // 2), :]
    grad_att = dot(branch_grad[...], weights[0], 1, 1).astype(bf16)
    along = grad_att.astype(f32) * att[...]
    heads = head_lanes((seqs * lat_rows, d_lat))
    lane = lax.broadcasted_iota(jnp.int32, (lat_rows, SIDE), 1)
    inner = []
    for h in range(HEADS):
        lo, hi = h * HEAD // 128 * 128, -(-(h + 1) * HEAD // 128) * 128
        inner.append(jnp.sum(jnp.where(heads[:, lo:hi] == h, along[:, lo:hi], 0.0), -1, keepdims=True))
    for b in range(seqs):
        t = log_totals[b]
        side = jnp.where(lane < HEADS, t, jnp.where(lane < 2 * HEADS, pltpu.roll(t, HEADS, 1), pltpu.roll(t, 2 * HEADS, 1)))
        for h in range(HEADS):
            own = (lane % HEADS == h) & (lane >= 3 * HEADS)
            side = jnp.where(own, inner[h][b * lat_rows : (b + 1) * lat_rows], side)
        side = jnp.where(lane < 6 * HEADS, side, 0.0)
        packed[b, :, :d_lat] = grad_att[b * lat_rows : (b + 1) * lat_rows]
        packed[b, :, d_lat:] = three_way(side, lane)
    for m, out in enumerate(backs):
        out[...] = packed[(at.j ^ m) // parts]


def square_grad_kernel(H, where, acts, others, *refs):
    outs, (turned, rights) = refs[:H], refs[H:]
    at = Place(where, H)
    rows = acts.shape[1]
    for m in range(3):
        turned[m, :, 0:rows] = acts[m].T
        turned[m, :, rows:] = others[m].T
        rights[m, 0:rows, :] = acts[3 + m]
        rights[m, rows:, :] = others[3 + m]
    half_wide = outs[0].shape[2]
    for r in range(H):
        at_row = rows_at(at.block(r, at.core) * 2 + at.core, half_wide)
        for m in range(3):
            outs[r][0, m] = dot(turned[m, at_row, :], rights[m], 1, 0).astype(bf16)


def attention_back_kernel(H, where, query, *refs):
    backs, refs = refs[:H], refs[H:]
    kv, mine, send, q_keep, q_send, packed, turned, grad_q, grad_kv = refs
    at = Place(where, H)
    d_lat, nlat = query.shape
    lat_rows = nlat // H
    for m in range(H):
        packed[rows_at(at.j ^ m, lat_rows), :] = backs[m][...]
    turned[...] = packed[:, :d_lat].T
    side = three_sum(packed[:, d_lat:].astype(f32))
    for h in range(HEADS):
        span = slice(h * HEAD, (h + 1) * HEAD)
        scores = dot(query[span, :], kv[0, span, :], 0, 0)
        probs = jnp.exp2(scores * score_two - side[:, h : h + 1])
        grad_kv[1, span, :] = dot(turned[span, :], probs.astype(bf16), 1, 0).astype(bf16)
        grad_probs = dot(turned[span, :], kv[1, span, :], 0, 0)
        grad_scores = (probs * (grad_probs - side[:, 3 * HEADS + h : 3 * HEADS + h + 1])).astype(bf16)
        grad_q[span, :] = (dot(kv[0, span, :], grad_scores, 1, 1) * score_scale).astype(bf16)
        grad_kv[0, span, :] = (dot(query[span, :], grad_scores, 1, 0) * score_scale).astype(bf16)
    n = q_keep.shape[1]
    for m in range(H):
        block = (at.j ^ m) * 2
        q_keep[m] = grad_q[rows_at(block + at.core, n), :]
        q_send[m] = grad_q[rows_at(block + 1 - at.core, n), :]
    mine[...] = grad_kv[at.core]
    send[...] = grad_kv[1 - at.core]


def query_core_kernel(where, keep, got, *outs):
    for m, out in enumerate(outs):
        out[...] = (keep[m].astype(f32) + got[m].astype(f32)).astype(bf16)


def slots_out(at, core, whole, top, low):
    n = top.shape[1]
    per = whole.shape[0] // (at.H * n)
    for r in range(at.H):
        out = low if r < at.H // 2 else top
        block = at.block(r, core)
        out[r % (at.H // 2)] = whole[rows_at(block * 2 + core if per == 2 else block, n), :]


def kv_grad_kernel(H, where, mine, got, in_low, in_other, top, low, whole):
    at = Place(where, H)
    whole[...] = (dot(mine[...], in_low[...], 1, 0) + dot(got[...], in_other[...], 1, 0)).astype(bf16)
    slots_out(at, at.core, whole, top, low)


def token_grad_kernel(where, inputs, mask, in_params, mine, send, weights, inputs_grad, small):
    core = where[0] & 1
    upstream = (dot(weights[core], mine[...], 1, 0) + dot(weights[1 - core], send[...], 1, 0)).T
    masked_row = mask[...] > 0
    unit, inverse = unit_norm(jnp.where(masked_row, in_params[2:3, :], inputs[...]))
    grad = norm_back(upstream, unit, inverse, in_params[0:1, :])
    inputs_grad[...] = jnp.where(masked_row, 0.0, grad)

    @pl.when(pl.program_id(0) == 0)
    def _():
        small[...] = jnp.zeros_like(small)

    for r, term in enumerate((upstream * unit, upstream, jnp.where(masked_row, grad, 0.0))):
        small[0, r : r + 1, :] += jnp.sum(term, 0, keepdims=True)


def turn(where, total, turned, top, low):
    turned[...] = total[...].T.astype(bf16)
    chip = where[0] >> 1
    half, rows, lanes = top.shape
    for r in range(2 * half):
        out = low if r < half else top
        out[r % half] = turned[rows_at(chip ^ flip(r, half.bit_length()), rows), 0:lanes]


def square_turn_kernel(where, *refs):
    terms, (lat_mine, lat_other, top, low, total, turned) = refs[:-6], refs[-6:]
    half = terms[0].shape[2]
    for m in range(3):
        acc = terms[0][0, m].astype(f32)
        for x in terms[1:]:
            acc = acc + x[0, m].astype(f32)
        total[m * half : (m + 1) * half, :] = acc
    n = lat_mine.shape[0]
    total[3 * half : 3 * half + n, :] = lat_mine[...].astype(f32) + lat_other[...].astype(f32)
    if 3 * half + n < total.shape[0]:
        total[3 * half + n :, :] = jnp.zeros((total.shape[0] - 3 * half - n, total.shape[1]), f32)
    turn(where, total, turned, top, low)


def kv_turn_kernel(where, *refs):
    terms, (top, low, total, turned) = refs[:-4], refs[-4:]
    acc = terms[0][0].astype(f32)
    for x in terms[1:]:
        acc = acc + x[0].astype(f32)
    total[...] = acc
    turn(where, total, turned, top, low)


def first_blocks(terms):
    return [pl.BlockSpec((1,) + x.shape[1:], lambda i, z=(0,) * x.ndim: z) for x in terms]


def whole_blocks(arrays):
    return [pl.BlockSpec(x.shape, lambda i, z=(0,) * len(x.shape): z) for x in arrays]


def squares(x):
    return jnp.sum(jnp.sum(x * x, 0, keepdims=True), 1, keepdims=True)


def square_end_kernel(where, *refs):
    terms, (extra, wq_squares, mine, other, total_squares, total) = refs[:-6], refs[-6:]
    core = where[0] & 1
    acc = terms[0][0].astype(f32)
    for x in terms[1:]:
        acc = acc + x[0].astype(f32)
    total[...] = acc
    lanes = extra.shape[1]
    total[:, acc.shape[1] - lanes :] += extra[...]
    total_squares[...] = squares(total[...]) + wq_squares[...]
    n = mine.shape[0]
    mine[...] = total[rows_at(core, n), :]
    other[...] = total[rows_at(1 - core, n), :].astype(bf16)


def kv_end_kernel(where, *refs):
    terms, refs = refs[:-9], refs[-9:]
    sq_squares, lat_small, mid_small, in_a, in_b, mine, other, sums, total = refs
    core = where[0] & 1
    acc = terms[0][0].astype(f32)
    for x in terms[1:]:
        acc = acc + x[0].astype(f32)
    total[...] = acc
    n = mine.shape[0]
    mine[...] = total[rows_at(core, n), :]
    other[...] = total[rows_at(1 - core, n), :].astype(bf16)
    sums[...] = jnp.zeros_like(sums)
    sums[0:2, :] = lat_small[...]
    sums[2:4, :] = mid_small[...]
    sums[4:7, 0 : in_a.shape[2]] = in_a[0] + in_b[0]
    sums[7:8, :] = jnp.broadcast_to(squares(acc) + sq_squares[...], (1, sums.shape[1]))


def latent_end_kernel(H, where, *refs):
    terms, (latents, lat_params, extra, small, turned) = refs[:H], refs[H:]
    low = tree_sum([x[...].astype(f32) for x in terms])
    unit, inverse = unit_norm(latents[...])
    once = jnp.where(where[0] == 0, 1.0, 0.0)
    small[0:1, :] = jnp.sum(low * unit, 0, keepdims=True) * once
    small[1:2, :] = jnp.sum(low, 0, keepdims=True) * once
    turned[...] = norm_back(low, unit, inverse, lat_params[0:1, :]).T
    both = turned[rows_at(where[0] >> 1, extra.shape[0]), :]
    n = extra.shape[1]
    extra[...] = jnp.where((where[0] & 1) == 0, both[:, 0:n], both[:, n:])


def update_kernel(where, sums, *refs):
    square, kv, refs = refs[:3], refs[3:6], refs[6:]
    rest, (norm_out, sq_new, sq_moments, kv_new, kv_moments), outs = refs[:7], refs[7:12], refs[12:]
    small = sums[0:7, :]
    norm = jnp.sqrt(jnp.sum(jnp.sum(small * small, 1, keepdims=True), 0, keepdims=True) + sums[7:8, 0:1])
    factor = jnp.minimum(1.0, clip_limit / (norm + 1e-06))
    for (weight, state, gradient), new, moments in ((square, sq_new, sq_moments), (kv, kv_new, kv_moments)):
        new[0, 0], new[1, 0], moments[0, 0], moments[1, 0] = adam_step(
            weight[0], state[0, 0], state[1, 0], state[2, 0], gradient[0] * factor
        )

    @pl.when(pl.program_id(0) == 0)
    def _():
        latents, latents_state, lat_grad, lat_params, lat_state, in_params, in_state = rest
        (latents_new, latents_moments, lat_new, lat_moments, in_new, in_moments, lat_clipped, in_clipped) = outs
        norm_out[...] = norm
        latents_new[0], latents_new[1], latents_moments[0], latents_moments[1] = adam_step(
            latents[...], latents_state[0], latents_state[1], latents_state[2], lat_grad[...] * factor
        )
        lat_clipped[...] = sums[0:4, :] * factor
        lat_new[0], lat_new[1], lat_moments[0], lat_moments[1] = adam_step(
            lat_params[...], lat_state[0], lat_state[1], lat_state[2], lat_clipped[...]
        )
        in_clipped[...] = sums[4:7, 0 : in_params.shape[1]] * factor
        results = adam_step(in_params[...], in_state[0], in_state[1], in_state[2], in_clipped[...])
        for i in range(3):
            row = slice(i, i + 1)
            in_new[i, 0:1], in_new[i, 1:2], in_moments[i, 0:1], in_moments[i, 1:2] = (x[row] for x in results)


def query_back_kernel(H, where, lat_all, w0, mine, other, wq, wq_squares, *refs):
    outs, (grad_q, whole, term) = refs[:H], refs[H:]
    at = Place(where, H)
    half_wide = mine.shape[0]
    grad_q[rows_at(at.core, half_wide), :] = mine[...]
    grad_q[rows_at(1 - at.core, half_wide), :] = other[...]
    term[...] = dot(grad_q[...], w0[...], 0, 0).astype(bf16)
    for m, out in enumerate(outs):
        out[...] = term[rows_at(at.j ^ m, out.shape[0]), :]
    whole[...] = dot(lat_all[...], grad_q[...], 0, 1)
    wq[...] = whole[rows_at(at.s, wq.shape[0]), :]
    wq_squares[...] = squares(wq[...])


def finish_kernel(where, wq, sq_mine, sq_other, kv_mine, kv_other, square_grad, kv_grad, lat_grad):
    core = where[0] & 1
    half = wq.shape[1] // 2
    mine, other = sq_mine[...], sq_other[...].astype(f32)
    low, high = jnp.where(core == 0, mine, other), jnp.where(core == 0, other, mine)
    square_grad[0] = wq[...]
    for m in range(3):
        square_grad[1 + m, :, 0:half] = low[:, m * half : (m + 1) * half]
        square_grad[1 + m, :, half:] = high[:, m * half : (m + 1) * half]
    kv_grad[core] = kv_mine[...]
    kv_grad[1 - core] = kv_other[...].astype(f32)
    n = lat_grad.shape[0] // 2
    ends = slice(3 * half, 3 * half + n)
    lat_grad[...] = jnp.concatenate([low[:, ends], high[:, ends]], 1).T


def on_device(
    inputs,
    mask_flags,
    out_grad,
    square,
    square_state,
    kv_weights,
    kv_state,
    latents,
    latents_state,
    in_params,
    in_state,
    lat_params,
    lat_state,
):
    L = Links()
    S, H = L.S, L.H
    parity = (L.s >> 1) & 1 if L.paired else 0 * L.s
    go = Order(jnp.stack([L.s, L.j, parity]).astype(jnp.int32))
    rows, d_in = inputs.shape
    parts = SEQ_LEN // rows
    seqs = H // parts
    lat_rows, d_lat = latents.shape
    nlat = lat_rows * H
    wide = square.shape[2]
    half_wide = wide // 2
    d_part, in_part = d_lat // S, d_in // S
    chips = S // 2
    mine_rows = seqs * lat_rows

    def low(*shape):
        return like(shape, bf16)

    def full(*shape):
        return like(shape, f32)

    square_t, kv_t = jnp.swapaxes(square, 1, 2), jnp.swapaxes(kv_weights, 1, 2)
    (lat_low,) = go(lat_kernel, [latents, lat_params], [low(lat_rows, d_lat)], name="lat_norm")
    kv_pair = go(fix(kv_weight_kernel, H), [kv_t], [low(wide, d_in)] * 2, name="kv_weight")
    kv_first = L.first(kv_pair[0])
    lat_near = L.near(lat_low)
    (w0,) = go(
        first_weight_kernel,
        [square_t],
        [low(wide, d_lat)],
        name="first_weight",
        grid=(1,),
        in_specs=[pl.BlockSpec((1, wide, d_lat), lambda i: (0, 0, 0))],
        out_specs=[pl.BlockSpec((wide, d_lat), lambda i: (0, 0))],
    )
    lat_near = [lat_low] + lat_near
    lat_all, query_mine = go(
        fix(query_kernel, H), [*lat_near, w0], [low(nlat, d_lat), low(wide, nlat)], name="query"
    )
    query_near = [query_mine] + L.near(query_mine)
    mask = mask_flags.reshape(rows, 1)
    step = min(rows, 256)
    in_low, in_turned = go(
        token_kernel,
        [inputs, mask, in_params],
        [low(rows, d_in), low(d_in, rows)],
        name="token_norm",
        grid=(rows // step,),
        in_specs=[
            pl.BlockSpec((step, d_in), lambda i: (i, 0)),
            pl.BlockSpec((step, 1), lambda i: (i, 0)),
            pl.BlockSpec(in_params.shape, lambda i: (0, 0)),
        ],
        out_specs=[pl.BlockSpec((step, d_in), lambda i: (i, 0)), pl.BlockSpec((d_in, step), lambda i: (0, i))],
    )
    kv_first = after(kv_first, query_mine)
    kv_mine = [kv_pair[0]] + L.spread(kv_first)
    kv_halves = kv_mine + [kv_pair[1]] + [L.swap_core(x) for x in kv_mine[1:]]
    sq_mine, sq_other = go(
        fix(other_weight_kernel, H),
        [square_t],
        [low(3, half_wide, d_lat)] * 2,
        name="other_weights",
        grid=(3,),
        in_specs=[pl.BlockSpec((1, wide, d_lat), lambda i: (1 + i, 0, 0))],
        out_specs=[pl.BlockSpec((1, half_wide, d_lat), lambda i: (i, 0, 0))] * 2,
    )
    sq_sent = after(sq_mine, *kv_mine[1:], *query_near)
    sq_first = L.first(sq_sent)

    kv, kv_all = go(
        fix(kv_kernel, H),
        [in_turned, *kv_halves],
        [low(2, d_lat, rows), low(2, d_lat, d_in)],
        [pltpu.SemaphoreType.DMA((2 * H,))],
        name="kv",
        in_specs=[VMEM] + [ANY] * (2 * H),
        after=[sq_sent],
    )
    sq_first = after(sq_first, kv)
    sq_rest = L.spread(sq_first)
    sq_early = [L.swap_core(sq_rest[0])] if L.paired else []
    query, *packs = go(
        fix(attention_kernel, H),
        [*query_near, kv],
        [low(d_lat, nlat)] + [low(lat_rows, d_lat + SIDE)] * H,
        [
            pltpu.VMEM((d_lat, nlat), f32),
            pltpu.VMEM((nlat, d_lat + SIDE), bf16),
        ],
        name="attention",
        after=sq_early,
    )
    got = [packs[0]] + [L.swap_hid(packs[m], m) for m in range(1, H)]
    here = after(L.s, *packs)
    sq_old = lax.dynamic_slice_in_dim(square, here * d_part, d_part, 1)
    kv_old = lax.dynamic_slice_in_dim(kv_weights, here * in_part, in_part, 1)
    lat_old = lax.dynamic_slice_in_dim(latents, here * d_part, d_part, 1)
    (kv_turned,) = go(
        kv_turned_kernel,
        [kv_all],
        [low(2, d_in, d_lat)],
        name="kv_turned",
        grid=(2,),
        in_specs=[pl.BlockSpec((1, d_lat, d_in), lambda i: (i, 0, 0))],
        out_specs=[pl.BlockSpec((1, d_in, d_lat), lambda i: (i, 0, 0))],
        after=[sq_old, kv_old, lat_old],
    )
    if L.paired:
        one, two, three = sq_rest
        three = after(three, *got, kv_turned)
        three_other = L.swap_core(three)
        two = after(two, three_other)
        sq_halves = [sq_mine, one, two, three, sq_other, *sq_early, L.swap_core(two), three_other]
    else:
        sq_rest = after(sq_rest, *got, kv_turned)
        sq_halves = [sq_mine] + sq_rest + [sq_other] + [L.swap_core(x) for x in sq_rest]

    latents_out, acts, mid_small, res_mine, res_send, *backs = go(
        fix(latent_kernel, H, parts),
        [*got, latents, out_grad, lat_params, *sq_halves],
        [full(mine_rows, d_lat), low(6, mine_rows, d_lat), full(2, d_lat)]
        + [low(lat_rows // 2, d_lat)] * 2
        + [low(lat_rows, d_lat + SIDE)] * H,
        [
            pltpu.VMEM((3, d_lat, d_lat), bf16),
            pltpu.SemaphoreType.DMA((3, 2 * H)),
            pltpu.VMEM((H, lat_rows, d_lat + SIDE), bf16),
            pltpu.VMEM((mine_rows, d_lat), f32),
            pltpu.VMEM((seqs, lat_rows, d_lat + SIDE), bf16),
            pltpu.VMEM((lat_rows, d_lat), bf16),
        ],
        name="latent",
        in_specs=[VMEM] * (H + 3) + [ANY] * (2 * H),
    )
    back = [backs[0]] + [L.swap_hid(backs[m], m) for m in range(1, H)]

    sq_slots = go(
        fix(square_grad_kernel, H),
        [acts, L.swap_core(acts)],
        [low(1, 3, half_wide, d_lat)] * H,
        [pltpu.VMEM((3, d_lat, 2 * mine_rows), bf16), pltpu.VMEM((3, 2 * mine_rows, d_lat), bf16)],
        name="square_grad",
    )
    sq = Slots(L, go, sq_slots, "square")
    res_other = L.swap_core(res_send)
    in_other = L.swap_core(after(in_low, sq_slots[0], res_other))

    gkv_mine, gkv_send, gq_keep, gq_send = go(
        fix(attention_back_kernel, H),
        [query, *back, kv],
        [low(d_lat, rows)] * 2 + [low(H, half_wide, nlat)] * 2,
        [
            pltpu.VMEM((nlat, d_lat + SIDE), bf16),
            pltpu.VMEM((d_lat, nlat), bf16),
            pltpu.VMEM((d_lat, nlat), bf16),
            pltpu.VMEM((2, d_lat, rows), bf16),
        ],
        name="attention_back",
        after=[res_other],
    )
    gkv_got = L.swap_core(gkv_send)
    gq_got = L.swap_core(gq_send)

    in_sums = []
    inputs_grad = None
    block = min(rows // 2, 256)

    def token_grad():
        nonlocal inputs_grad
        first = len(in_sums) * (rows // 2 // block)
        inputs_grad, sums = go(
            token_grad_kernel,
            [inputs, mask, in_params, gkv_mine, gkv_send, kv_turned],
            [full(rows, d_in), full(1, 3, d_in)],
            name="token_grad_%d" % len(in_sums),
            grid=(rows // 2 // block,),
            in_specs=[
                pl.BlockSpec((block, d_in), lambda g: (first + g, 0)),
                pl.BlockSpec((block, 1), lambda g: (first + g, 0)),
                pl.BlockSpec(in_params.shape, lambda g: (0, 0)),
                pl.BlockSpec((d_lat, block), lambda g: (0, first + g)),
                pl.BlockSpec((d_lat, block), lambda g: (0, first + g)),
                pl.BlockSpec(kv_turned.shape, lambda g: (0, 0, 0)),
            ],
            out_specs=[
                pl.BlockSpec((block, d_in), lambda g: (first + g, 0)),
                pl.BlockSpec((1, 3, d_in), lambda g: (0, 0, 0)),
            ],
            onto=inputs_grad,
        )
        in_sums.append(sums)

    gq_all = go(query_core_kernel, [gq_keep, gq_got], [low(half_wide, nlat)] * H, name="query_core", after=[in_other, *sq.early])
    gq_near = [L.swap_hid(gq_all[m], m) for m in range(1, H)]
    token_grad()
    sq.hold(*gq_near)
    sq.step()
    kv_top, kv_low = go(
        fix(kv_grad_kernel, H),
        [gkv_mine, gkv_got, in_low, in_other],
        [low(H // 2, wide, d_in)] * 2,
        [pltpu.VMEM((d_lat, d_in), bf16)],
        name="kv_grad",
    )
    kv_sums = Halving(go, [kv_top], [kv_low], L.hb, L.swap_step, "kv")
    kv_sums.start()
    gq_mine = go.tree([gq_all[0]] + gq_near, "query_hid")
    gq_chips = L.near_chips(gq_mine)

    lanes = 3 * half_wide + lat_rows // 2
    padded = -(-lanes // 128) * 128

    def turn_to_chips(kernel, terms, extra, n, lanes, padded, name):
        d = terms[0].shape[-1]
        out = [low(chips // 2, n, lanes)] * 2
        return go(
            kernel,
            [*terms, *extra],
            out,
            [pltpu.VMEM((padded, d), f32), pltpu.VMEM((d, padded), bf16)],
            name=name,
            grid=(1,),
            in_specs=first_blocks(terms) + whole_blocks(extra),
            out_specs=whole_blocks(out),
        )

    n = L.sb - 1

    def chip_step(x, i):
        return L.swap_seq(x, 2 << (n - 1 - i))

    def end(kernel, terms, extra, n, lanes, more, name, after=()):
        outs = [full(n, lanes), low(n, lanes)] + more
        return go(
            kernel,
            [*terms, *extra],
            outs,
            [pltpu.VMEM((2 * n, lanes), f32)],
            name=name,
            grid=(1,),
            in_specs=first_blocks(terms) + whole_blocks(extra),
            out_specs=whole_blocks(outs),
            after=after,
        )

    for _ in range(L.hb - 2):
        sq.step()
        kv_sums.step()
    sq_top, sq_low = turn_to_chips(
        square_turn_kernel, sq.terms, [res_mine, res_other], 2 * d_part, lanes, padded, "square_turn"
    )
    sq_chips = Halving(go, [sq_top], [sq_low], n, chip_step, "square_chip")
    sq_chips.start()
    kv_sums.step()
    gq_mine = go.tree([gq_mine] + gq_chips, "query_chips")
    gq_other = L.swap_core(gq_mine)
    wq_part, wq_squares, *lat_blocks = go(
        fix(query_back_kernel, H),
        [lat_all, w0, gq_mine, gq_other],
        [full(d_part, wide), full(1, 1)] + [low(lat_rows, d_lat)] * H,
        [pltpu.VMEM((wide, nlat), bf16), pltpu.VMEM((d_lat, wide), f32), pltpu.VMEM((nlat, d_lat), bf16)],
        name="query_back",
    )
    lat_near = [L.swap_hid(lat_blocks[m], m) for m in range(1, H)]
    kv_top, kv_low = turn_to_chips(kv_turn_kernel, kv_sums.terms, [], 2 * in_part, wide, wide, "kv_turn")
    kv_chips = Halving(go, [kv_top], [kv_low], n, chip_step, "kv_chip")
    kv_chips.start()
    sq_chips.step()
    kv_chips.step()
    token_grad()
    lat_extra, lat_small = go(
        fix(latent_end_kernel, H),
        [lat_blocks[0], *lat_near, latents, lat_params],
        [full(2 * d_part, lat_rows // 2), full(2, d_lat)],
        [pltpu.VMEM((d_lat, lat_rows), f32)],
        name="latent_end",
    )
    for _ in range(n - 2):
        sq_chips.step()
        kv_chips.step()
    sq_mine, sq_send, sq_squares = end(
        square_end_kernel,
        sq_chips.terms,
        [lat_extra, wq_squares],
        d_part,
        lanes,
        [full(1, 1)],
        "square_end",
    )
    sq_other = L.swap_core(sq_send)
    kv_mine, kv_send, sums = end(
        kv_end_kernel,
        kv_chips.terms,
        [sq_squares, lat_small, mid_small, *in_sums],
        in_part,
        wide,
        [full(8, d_lat)],
        "kv_end",
    )
    kv_other = L.swap_core(kv_send)

    square_grad, kv_grad, lat_grad = go(
        finish_kernel,
        [wq_part, sq_mine, sq_other, kv_mine, kv_other],
        [full(4, d_part, wide), full(2, in_part, wide), full(lat_rows, d_part)],
        name="finish",
    )
    sums = L.sum_all(sums, square_grad)
    pair = [full(3, 2, d_in)] * 2
    rest = [lat_old, latents_state, lat_grad, lat_params, lat_state, in_params, in_state]
    outs = [full(2, *lat_old.shape)] * 2 + [full(2, *lat_params.shape)] * 2 + pair
    outs += [full(*lat_params.shape), full(*in_params.shape)]
    half = in_part // 2
    sq_out = pl.BlockSpec((2, 1, d_part, wide), lambda g: (0, g, 0, 0))
    kv_out = pl.BlockSpec((2, 1, half, wide), lambda g: (0, g // 2, g % 2, 0))
    results = go(
        update_kernel,
        [sums, sq_old, square_state, square_grad, kv_old, kv_state, kv_grad, *rest],
        [full(1, 1)] + [full(2, *sq_old.shape)] * 2 + [full(2, *kv_old.shape)] * 2 + outs,
        name="update",
        grid=(4,),
        in_specs=whole_blocks([sums])
        + [
            pl.BlockSpec((1, d_part, wide), lambda g: (g, 0, 0)),
            pl.BlockSpec((3, 1, d_part, wide), lambda g: (0, g, 0, 0)),
            pl.BlockSpec((1, d_part, wide), lambda g: (g, 0, 0)),
            pl.BlockSpec((1, half, wide), lambda g: (g // 2, g % 2, 0)),
            pl.BlockSpec((3, 1, half, wide), lambda g: (0, g // 2, g % 2, 0)),
            pl.BlockSpec((1, half, wide), lambda g: (g // 2, g % 2, 0)),
        ]
        + whole_blocks(rest),
        out_specs=whole_blocks([full(1, 1)]) + [sq_out] * 2 + [kv_out] * 2 + whole_blocks(outs),
    )
    (grad_norm, square_new, square_moments, kv_new, kv_moments, latents_new, latents_moments) = results[:7]
    (lat_new, lat_moments, in_new, in_moments, lat_clipped, in_clipped) = results[7:]
    grad_norm = grad_norm[0, 0]
    in_new, in_moments = jnp.swapaxes(in_new, 0, 1), jnp.swapaxes(in_moments, 0, 1)
    return (
        latents_out.reshape(seqs, lat_rows, d_lat),
        inputs_grad,
        grad_norm,
        square_new,
        square_moments,
        kv_new,
        kv_moments,
        latents_new,
        latents_moments,
        in_new,
        in_moments,
        lat_new,
        lat_moments,
        in_clipped,
        lat_clipped,
    )


def solution(mesh):
    return jax.shard_map(
        on_device,
        mesh=mesh,
        in_specs=(
            P(("seq", "hid"), None),
            P(("seq", "hid")),
            P("seq", "hid", None),
            P(None, None, "hid"),
            P(None, None, "seq", "hid"),
            P(None, None, "hid"),
            P(None, None, "seq", "hid"),
            P("hid", None),
            P(None, "hid", "seq"),
            P(),
            P(),
            P(),
            P(),
        ),
        out_specs=(
            P("seq", "hid", None),
            P(("seq", "hid"), None),
            P(),
            P(None, None, "seq", "hid"),
            P(None, None, "seq", "hid"),
            P(None, None, "seq", "hid"),
            P(None, None, "seq", "hid"),
            P(None, "hid", "seq"),
            P(None, "hid", "seq"),
            P(),
            P(),
            P(),
            P(),
            P(),
            P(),
        ),
        check_vma=False,
    )
```

```python
from functools import partial as fix
import math

import jax
import jax.numpy as jnp
from jax import lax
from jax.experimental import pallas as pl
from jax.experimental.pallas import tpu as pltpu
from jax.sharding import PartitionSpec as P

HEADS = 8
HEAD = 160
SEQ_LEN = 2048
STEP = 10
SIDE = 128


clip_limit = 1.0
beta_one = 0.9
beta_two = 0.999
adam_eps = 1e-08
learn_rate = 0.05
decay_rate = 0.01
ema_keep = 0.9
norm_eps = 1e-05
score_scale = 1.0 / math.sqrt(HEAD)
score_two = score_scale * math.log2(math.e)

f32 = jnp.float32
bf16 = jnp.bfloat16


def unit_norm(values):
    centre = jnp.mean(values, -1, keepdims=True)
    centred = values - centre
    inverse = lax.rsqrt(jnp.mean(centred * centred, -1, keepdims=True) + norm_eps)
    return centred * inverse, inverse


def norm_back(upstream, unit_rows, inverse, scale_row):
    scaled = upstream * scale_row
    inner_mean = jnp.mean(scaled, -1, keepdims=True)
    along_mean = jnp.mean(scaled * unit_rows, -1, keepdims=True)
    return inverse * (scaled - inner_mean - unit_rows * along_mean)


def adam_step(weight, first, root, average, gradient):
    moment_one = beta_one * first + (1.0 - beta_one) * gradient
    root_two = jnp.sqrt(beta_two * root * root + (1.0 - beta_two) * gradient * gradient)
    corrected_one = moment_one * (learn_rate / (1.0 - beta_one**STEP))
    denominator = root_two * (1.0 / math.sqrt(1.0 - beta_two**STEP)) + adam_eps
    new_weight = weight * (1.0 - learn_rate * decay_rate) - corrected_one / denominator
    ema_new = ema_keep * average + (1.0 - ema_keep) * new_weight
    return new_weight, ema_new, moment_one, root_two


def dot(a, b, over_a, over_b):
    return lax.dot_general(a, b, (((over_a,), (over_b,)), ((), ())), preferred_element_type=f32)


def flip(value, bits):
    out = 0
    for i in range(bits):
        out = out + ((value >> i) & 1) * (1 << (bits - 1 - i))
    return out


class Links:
    def __init__(self):
        self.S = lax.axis_size("seq")
        self.H = lax.axis_size("hid")
        self.hb = self.H.bit_length() - 1
        self.sb = self.S.bit_length() - 1
        self.s = lax.axis_index("seq")
        self.j = lax.axis_index("hid")
        self.core = self.s & 1
        self.paired = self.H == 4 and self.S >= 4

    def side(self, s):
        return (s & 1) ^ ((s >> 1) & 1) if self.paired else s & 1

    def swap(self, x, dest):
        pairs = []
        for s in range(self.S):
            for j in range(self.H):
                ds, dj = dest(s, j)
                pairs.append((s * self.H + j, ds * self.H + dj))
        return lax.ppermute(x, ("seq", "hid"), pairs)

    def swap_core(self, x):
        return self.swap(x, lambda s, j: (s ^ 1, j))

    def swap_hid(self, x, mask):
        return self.swap(x, lambda s, j: (s, j ^ mask))

    def swap_seq(self, x, mask):
        return self.swap(x, lambda s, j: (s ^ mask, j))

    def swap_step(self, x, i):
        even, odd = 1 << i, 1 << (self.hb - 1 - i)
        return self.swap(x, lambda s, j: (s, j ^ (odd if self.side(s) else even)))

    def first(self, x):
        return [self.swap_step(x, i) for i in range(1 if self.paired else self.hb)]

    def spread(self, first):
        if self.paired:
            return [first[0], self.swap_seq(first[0], 2), self.swap_step(first[0], 1)]
        blocks = [None]
        for i, x in enumerate(first):
            blocks += [x] + [self.swap_step(y, i) for y in blocks[1:]]
        return blocks[1:]

    def near(self, x):
        return [self.swap_hid(x, m) for m in range(1, self.H)]

    def near_chips(self, x):
        return [self.swap_seq(x, 2 * m) for m in range(1, self.S // 2)]

    def sum_all(self, x, last):
        x = x + self.swap_core(x)
        x = tree_sum([x] + self.near(x))
        return tree_sum([x] + after(self.near_chips(x), last))


def tree_sum(terms):
    while len(terms) > 1:
        terms = [a + b for a, b in zip(terms[::2], terms[1::2])]
    return terms[0]


class Place:
    def __init__(self, where, H):
        self.H = H
        self.hb = H.bit_length() - 1
        self.s = where[0]
        self.j = where[1]
        self.core = self.s & 1
        self.parity = where[2]

    def block(self, r, core):
        return self.j ^ jnp.where((core ^ self.parity) == 0, r, flip(r, self.hb))

    def halves(self):
        mine = [(self.block(r, self.core), self.core) for r in range(self.H)]
        return mine + [(self.block(r, 1 - self.core), 1 - self.core) for r in range(self.H)]


def after(x, *others):
    return lax.optimization_barrier((x, others))[0]


def rows_at(index, size):
    return pl.ds(pl.multiple_of(index * size, size), size)


VMEM = pl.BlockSpec(memory_space=pltpu.VMEM)
SMEM = pl.BlockSpec(memory_space=pltpu.SMEM)
ANY = pl.BlockSpec(memory_space=pl.ANY)


spent = {
    "kv_weight": 5.0,
    "first_weight": 0.1,
    "query": 4.0,
    "token_norm": 10.0,
    "other_weights": 0.1,
    "kv": 0.1,
    "attention": 0.1,
    "kv_turned": 0.1,
    "latent": 11.0,
    "square_grad": 5.0,
    "attention_back": 12.0,
    "query_core": 0.1,
    "token_grad_0": 0.1,
    "square_step": 17.0,
    "query_hid": 0.1,
    "kv_grad": 1.0,
    "query_chips": 0.1,
    "square_turn": 0.1,
    "kv_step": 0.1,
    "kv_turn": 0.1,
    "square_chip_step": 3.3,
    "query_back": 0.1,
    "kv_chip_step": 0.1,
    "token_grad_1": 0.1,
    "latent_end": 0.1,
    "square_end": 0.1,
    "update": 7.0,
}


class Order:
    def __init__(self, where):
        self.where = where
        self.last = []

    def __call__(
        self, kernel, args, outs, scratch=(), name=None, grid=(), in_specs=None, out_specs=None, after=(), onto=None
    ):
        n = len(args)
        waits = self.last + list(after)
        if onto is not None:
            waits = [onto] + waits

        def body(where, *refs):
            kernel(where, *refs[:n], *refs[n + len(waits) :])

        if grid:
            room = 20 << 20
        else:
            held = [x for x, spec in zip(args, in_specs or [VMEM] * n) if spec is not ANY]
            held += [x for x, spec in zip(outs, out_specs or [VMEM] * len(outs)) if spec is not ANY]
            held += [x for x in scratch if "semaphore" not in str(x.dtype) and "dma" not in str(x.dtype)]
            room = sum(math.prod(x.shape) * jnp.dtype(x.dtype).itemsize for x in held) * 5 // 4 + (10 << 20)
        results = pl.pallas_call(
            body,
            out_shape=outs,
            grid=grid,
            in_specs=[SMEM] + (in_specs or [VMEM] * n) + [ANY] * len(waits),
            out_specs=out_specs or [VMEM] * len(outs),
            scratch_shapes=list(scratch),
            compiler_params=pltpu.CompilerParams(vmem_limit_bytes=min(room, 58 << 20)),
            cost_estimate=pl.CostEstimate(
                flops=int(spent.get(name, 2.0) * 1e9), bytes_accessed=0, transcendentals=0
            ),
            name=name,
            input_output_aliases={} if onto is None else {1 + n: 0},
        )(self.where, *args, *waits)
        self.last = [results[-1]]
        return results

    def tree(self, terms, name):
        def kernel(where, *refs):
            refs[-1][...] = tree_sum([x[...].astype(f32) for x in refs[:-1]]).astype(bf16)

        return self(kernel, terms, [like(terms[0].shape, bf16)], name=name)[0]

    def add(self, terms, block, count, name):
        shape = terms[0].shape[1:]
        parts = shape[0] if len(shape) == 3 else 1
        terms = [x.reshape((x.shape[0], parts) + shape[-2:]) for x in terms]

        def kernel(where, *refs):
            out = refs[-1]
            acc = refs[0][...].astype(f32)
            for x in refs[1:-1]:
                acc = acc + x[...].astype(f32)
            out[...] = acc.astype(bf16)

        size = (1, 1) + shape[-2:]
        (out,) = self(
            kernel,
            terms,
            [like((count, parts) + shape[-2:], bf16)],
            name=name,
            grid=(count, parts),
            in_specs=[pl.BlockSpec(size, lambda i, m: (block * count + i, m, 0, 0))] * len(terms),
            out_specs=[pl.BlockSpec(size, lambda i, m: (i, m, 0, 0))],
        )
        return out.reshape((count,) + shape)


def like(shape, dtype):
    return jax.ShapeDtypeStruct(tuple(shape), dtype)


class Halving:
    def __init__(self, go, top, low, bits, swap, name):
        self.go, self.top, self.terms, self.bits, self.swap, self.name = go, top, low, bits, swap, name

    def start(self):
        i = self.bits - 1
        sending = self.top[0] if len(self.top) == 1 else self.go.add(self.top, 0, 1 << i, self.name + "_top")
        self.terms = self.terms + [self.swap(sending, i)]
        self.at = i

    def step(self):
        n = 1 << (self.at - 1)
        sending = self.go.add(self.terms, 1, n, self.name + "_step")
        self.at -= 1
        self.terms = self.terms + [self.swap(sending, self.at)]


class Slots:
    def __init__(self, L, go, slots, name, *before):
        self.L, self.go, self.name = L, go, name
        self.slots = [[x] for x in slots]
        self.early = []
        if L.paired:
            came = L.swap_step(after(slots[3], *before) if before else slots[3], 1)
            self.slots[1] += [came, L.swap_seq(slots[2], 2)]
            self.early = [came]
            self.steps = [1]
        else:
            for r in range(L.H // 2, L.H):
                self.slots[r - L.H // 2].append(L.swap_step(slots[r], L.hb - 1))
            self.steps = list(reversed(range(1, L.H // 2)))

    def hold(self, *others):
        for r in self.steps[:1]:
            self.slots[r] = after(self.slots[r], *others)

    def step(self):
        r, self.steps = self.steps[0], self.steps[1:]
        i = r.bit_length() - 1
        sending = self.go.add(self.slots[r], 0, 1, self.name + "_step")
        self.slots[r - (1 << i)].append(self.L.swap_step(sending, i))

    @property
    def terms(self):
        while self.steps:
            self.step()
        return self.slots[0]


def lat_kernel(where, latents, lat_params, out):
    unit, _ = unit_norm(latents[...])
    out[...] = (unit * lat_params[0:1, :] + lat_params[1:2, :]).astype(bf16)


def kv_weight_kernel(H, where, kv, mine, other):
    at = Place(where, H)
    mine[...] = kv[at.core].astype(bf16)
    other[...] = kv[1 - at.core].astype(bf16)


def first_weight_kernel(where, weight, out):
    out[...] = weight[0].astype(bf16)


def other_weight_kernel(H, where, weight, mine, other):
    at = Place(where, H)
    n = mine.shape[1]
    mine[0] = weight[0, rows_at(at.core, n), :].astype(bf16)
    other[0] = weight[0, rows_at(1 - at.core, n), :].astype(bf16)


def query_kernel(H, where, *refs):
    near, (w0, lat_all, query) = refs[:H], refs[H:]
    at = Place(where, H)
    n = near[0].shape[0]
    for m, x in enumerate(near):
        lat_all[rows_at(at.j ^ m, n), :] = x[...]
    query[...] = dot(w0[...], lat_all[...], 1, 1).astype(bf16)


def token_kernel(where, inputs, mask, in_params, out, turned):
    masked = jnp.where(mask[...] > 0, in_params[2:3, :], inputs[...])
    unit, _ = unit_norm(masked)
    low = (unit * in_params[0:1, :] + in_params[1:2, :]).astype(bf16)
    out[...] = low
    turned[...] = low.T


def started(copies):
    for copy in copies:
        copy.start()
    return copies


def waited(copies):
    for copy in copies:
        copy.wait()


def kv_kernel(H, where, in_turned, *refs):
    halves, (kv, weights, sems) = refs[: 2 * H], refs[2 * H :]
    at = Place(where, H)
    wide = halves[0].shape[0]
    d_lat = wide * H
    copies = started(
        [
            pltpu.make_async_copy(halves[i], weights.at[which, rows_at(block, wide), :], sems.at[i])
            for i, (block, which) in enumerate(at.halves())
        ]
    )
    waited(copies)
    for which in range(2):
        kv[which] = dot(weights[which], in_turned[...], 1, 0).astype(bf16)


def kv_turned_kernel(where, kv_all, out):
    out[0] = kv_all[0].T


def three_way(x, lane):
    a = x.astype(bf16).astype(f32)
    b = (x - a).astype(bf16).astype(f32)
    part = (lane // HEADS) % 3
    return jnp.where(part == 0, a, jnp.where(part == 1, b, x - a - b)).astype(bf16)


def three_sum(x):
    return x + pltpu.roll(x, SIDE - HEADS, 1) + pltpu.roll(x, SIDE - 2 * HEADS, 1)


def attention_kernel(H, where, *refs):
    near, kv, query = refs[:H], refs[H], refs[H + 1]
    packs, (mix, packed) = refs[H + 2 : -2], refs[-2:]
    at = Place(where, H)
    n = near[0].shape[0]
    for m, x in enumerate(near):
        query[rows_at(at.j ^ m, n), :] = x[...]
    d_lat, nlat = query.shape
    lane = lax.broadcasted_iota(jnp.int32, (nlat, SIDE), 1)
    logs = jnp.zeros((nlat, SIDE), f32)
    for h in range(HEADS):
        span = slice(h * HEAD, (h + 1) * HEAD)
        scores = dot(query[span, :], kv[0, span, :], 0, 0)
        peak = jnp.max(scores, -1, keepdims=True)
        weight = jnp.exp2((scores - peak) * score_two)
        total = jnp.sum(weight, -1, keepdims=True)
        probs = (weight * (1.0 / total)).astype(bf16)
        mix[span, :] = dot(kv[1, span, :], probs, 1, 1)
        log_part = peak * score_two + jnp.log2(total)
        logs = jnp.where((lane % HEADS == h) & (lane < 3 * HEADS), log_part, logs)
    packed[:, :d_lat] = mix[...].T.astype(bf16)
    packed[:, d_lat:] = three_way(logs, lane)
    lat_rows = nlat // H
    for m, out in enumerate(packs):
        out[...] = packed[rows_at(at.j ^ m, lat_rows), :]


def head_lanes(shape):
    return lax.broadcasted_iota(jnp.int32, shape, 1) // HEAD


def wide_dot(x, weights, slot, across):
    n = weights.shape[1]
    step = 256 if n % 256 == 0 else n
    parts = []
    for i in range(n // step):
        span = slice(i * step, (i + 1) * step)
        parts.append(dot(x, weights[slot, span, :], 1, 1) if across else dot(x, weights[slot, :, span], 1, 0))
    return jnp.concatenate(parts, 1)


def latent_kernel(H, parts, where, *refs):
    seqs = H // parts
    got, refs = refs[:H], refs[H:]
    latents, out_grad, lat_params, refs = refs[0], refs[1], refs[2], refs[3:]
    pieces, refs = refs[: 2 * H], refs[2 * H :]
    (latents_out, acts, small, res_mine, res_send), refs = refs[:5], refs[5:]
    attended, up_grad, hidden, branch_grad, mid_low, grad_y = (acts.at[i] for i in range(6))
    backs, (weights, sems, gathered, att, packed, res) = refs[:H], refs[H:]
    at = Place(where, H)
    lat_rows, d_lat = latents.shape
    half_wide = pieces[0].shape[1]
    copies = []
    for m in range(3):
        group = []
        for i, (block, half) in enumerate(at.halves()):
            group.append(
                pltpu.make_async_copy(
                    pieces[i].at[m],
                    weights.at[m, rows_at(block * 2 + half, half_wide), :],
                    sems.at[m, i],
                )
            )
            group[-1].start()
        copies.append(group)

    def arrived(m):
        for copy in copies[m]:
            copy.wait()

    for m in range(H):
        gathered[at.j ^ m] = got[m][...]
    heads = head_lanes((lat_rows, d_lat))
    log_totals = []
    for b in range(seqs):
        logs = [three_sum(gathered[b * parts + p, :, d_lat:].astype(f32)) for p in range(parts)]
        peak = logs[0]
        for x in logs[1:]:
            peak = jnp.maximum(peak, x)
        log_total = peak + jnp.log2(sum(jnp.exp2(x - peak) for x in logs))
        log_totals.append(log_total)
        mixed = jnp.zeros((lat_rows, d_lat), f32)
        for p in range(parts):
            share = jnp.exp2(logs[p] - log_total)
            spread = jnp.zeros((lat_rows, d_lat), f32)
            for h in range(HEADS):
                spread = jnp.where(heads == h, share[:, h : h + 1], spread)
            mixed = mixed + spread * gathered[b * parts + p, :, :d_lat].astype(f32)
        att[b * lat_rows : (b + 1) * lat_rows, :] = mixed
    attended[...] = att[...].astype(bf16)
    grad_y[...] = jnp.concatenate([out_grad[b] for b in range(seqs)], 0).astype(bf16)

    arrived(0)
    branch = wide_dot(attended[...], weights, 0, False)
    residual = jnp.concatenate([latents[...]] * seqs, 0) + branch
    unit, inverse = unit_norm(residual)
    mid_low[...] = (unit * lat_params[2:3, :] + lat_params[3:4, :]).astype(bf16)
    arrived(1)
    up_proj = wide_dot(mid_low[...], weights, 1, True)
    below = 0.5 + 0.5 * lax.erf(up_proj * math.sqrt(0.5))
    hidden[...] = (up_proj * below).astype(bf16)
    slope = below + up_proj * jnp.exp(-0.5 * up_proj * up_proj) * (1.0 / math.sqrt(2.0 * math.pi))
    arrived(2)
    latents_out[...] = residual + wide_dot(hidden[...], weights, 2, False)
    up_grad[...] = (wide_dot(grad_y[...], weights, 2, True) * slope).astype(bf16)
    grad_mid = wide_dot(up_grad[...], weights, 1, False)
    small[0:1, :] = jnp.sum(grad_mid * unit, 0, keepdims=True)
    small[1:2, :] = jnp.sum(grad_mid, 0, keepdims=True)
    grad_residual = jnp.concatenate([out_grad[b] for b in range(seqs)], 0) + norm_back(
        grad_mid, unit, inverse, lat_params[2:3, :]
    )
    branch_grad[...] = grad_residual.astype(bf16)
    folded = grad_residual[0:lat_rows]
    for b in range(1, seqs):
        folded = folded + grad_residual[b * lat_rows : (b + 1) * lat_rows]
    res[...] = folded.astype(bf16)
    res_mine[...] = res[rows_at(at.core, lat_rows // 2), :]
    res_send[...] = res[rows_at(1 - at.core, lat_rows // 2), :]
    grad_att = wide_dot(branch_grad[...], weights, 0, True).astype(bf16)
    along = grad_att.astype(f32) * att[...]
    heads = head_lanes((seqs * lat_rows, d_lat))
    lane = lax.broadcasted_iota(jnp.int32, (lat_rows, SIDE), 1)
    inner = []
    for h in range(HEADS):
        lo, hi = h * HEAD // 128 * 128, -(-(h + 1) * HEAD // 128) * 128
        inner.append(jnp.sum(jnp.where(heads[:, lo:hi] == h, along[:, lo:hi], 0.0), -1, keepdims=True))
    for b in range(seqs):
        t = log_totals[b]
        side = jnp.where(lane < HEADS, t, jnp.where(lane < 2 * HEADS, pltpu.roll(t, HEADS, 1), pltpu.roll(t, 2 * HEADS, 1)))
        for h in range(HEADS):
            own = (lane % HEADS == h) & (lane >= 3 * HEADS)
            side = jnp.where(own, inner[h][b * lat_rows : (b + 1) * lat_rows], side)
        side = jnp.where(lane < 6 * HEADS, side, 0.0)
        packed[b, :, :d_lat] = grad_att[b * lat_rows : (b + 1) * lat_rows]
        packed[b, :, d_lat:] = three_way(side, lane)
    for m, out in enumerate(backs):
        out[...] = packed[(at.j ^ m) // parts]


def square_grad_kernel(H, where, acts, others, *refs):
    outs, (turned, rights) = refs[:-2], refs[-2:]
    at = Place(where, H)
    rows = acts.shape[1]
    for m in range(3):
        turned[m, :, 0:rows] = acts[m].T
        turned[m, :, rows:] = others[m].T
        rights[m, 0:rows, :] = acts[3 + m]
        rights[m, rows:, :] = others[3 + m]
    half_wide = outs[0].shape[2]
    for r in range(H):
        at_row = rows_at(at.block(r, at.core) * 2 + at.core, half_wide)
        for m in range(3):
            block = dot(turned[m, at_row, :], rights[m], 1, 0).astype(bf16)
            if len(outs) == H and outs[2].shape[1] == 3:
                outs[r][0, m] = block
            elif r < 2:
                outs[r][0, m] = block
            elif r == 3:
                outs[2][0, m] = block
            elif m == 2:
                outs[2][0, 3] = block
            else:
                outs[3][0, m] = block


def square_step_kernel(where, own, came, over, out):
    for m in range(3):
        acc = own[0, m].astype(f32) + came[0, m].astype(f32)
        if m < over.shape[1]:
            acc = acc + over[0, m].astype(f32)
        out[0, m] = acc.astype(bf16)


def attention_back_kernel(H, where, query, *refs):
    backs, refs = refs[:H], refs[H:]
    kv, mine, send, q_keep, q_send, packed, turned, grad_q, grad_kv = refs
    at = Place(where, H)
    d_lat, nlat = query.shape
    lat_rows = nlat // H
    for m in range(H):
        packed[rows_at(at.j ^ m, lat_rows), :] = backs[m][...]
    turned[...] = packed[:, :d_lat].T
    side = three_sum(packed[:, d_lat:].astype(f32))
    for h in range(HEADS):
        span = slice(h * HEAD, (h + 1) * HEAD)
        scores = dot(query[span, :], kv[0, span, :], 0, 0)
        probs = jnp.exp2(scores * score_two - side[:, h : h + 1])
        grad_kv[1, span, :] = dot(turned[span, :], probs.astype(bf16), 1, 0).astype(bf16)
        grad_probs = dot(turned[span, :], kv[1, span, :], 0, 0)
        grad_scores = (probs * (grad_probs - side[:, 3 * HEADS + h : 3 * HEADS + h + 1])).astype(bf16)
        grad_q[span, :] = (dot(kv[0, span, :], grad_scores, 1, 1) * score_scale).astype(bf16)
        grad_kv[0, span, :] = (dot(query[span, :], grad_scores, 1, 0) * score_scale).astype(bf16)
    n = q_keep.shape[1]
    for m in range(H):
        block = (at.j ^ m) * 2
        q_keep[m] = grad_q[rows_at(block + at.core, n), :]
        q_send[m] = grad_q[rows_at(block + 1 - at.core, n), :]
    mine[...] = grad_kv[at.core]
    send[...] = grad_kv[1 - at.core]


def query_core_kernel(where, keep, got, *outs):
    for m, out in enumerate(outs):
        out[...] = (keep[m].astype(f32) + got[m].astype(f32)).astype(bf16)


def slots_out(at, core, whole, top, low):
    n = top.shape[1]
    per = whole.shape[0] // (at.H * n)
    for r in range(at.H):
        out = low if r < at.H // 2 else top
        block = at.block(r, core)
        out[r % (at.H // 2)] = whole[rows_at(block * 2 + core if per == 2 else block, n), :]


def kv_grad_kernel(H, where, mine, got, in_low, in_other, *refs):
    at = Place(where, H)
    outs, whole = refs[:H], refs[H]
    whole[...] = (dot(mine[...], in_low[...], 1, 0) + dot(got[...], in_other[...], 1, 0)).astype(bf16)
    for r, out in enumerate(outs):
        out[0] = whole[rows_at(at.block(r, at.core), out.shape[1]), :]


def token_grad_kernel(where, inputs, mask, in_params, mine, send, weights, inputs_grad, small):
    core = where[0] & 1
    upstream = (dot(weights[core], mine[...], 1, 0) + dot(weights[1 - core], send[...], 1, 0)).T
    masked_row = mask[...] > 0
    unit, inverse = unit_norm(jnp.where(masked_row, in_params[2:3, :], inputs[...]))
    grad = norm_back(upstream, unit, inverse, in_params[0:1, :])
    inputs_grad[...] = jnp.where(masked_row, 0.0, grad)

    @pl.when(pl.program_id(0) == 0)
    def _():
        small[...] = jnp.zeros_like(small)

    for r, term in enumerate((upstream * unit, upstream, jnp.where(masked_row, grad, 0.0))):
        small[0, r : r + 1, :] += jnp.sum(term, 0, keepdims=True)


def turn(where, total, turned, top, low):
    turned[...] = total[...].T.astype(bf16)
    chip = where[0] >> 1
    half, rows, lanes = top.shape
    for r in range(2 * half):
        out = low if r < half else top
        out[r % half] = turned[rows_at(chip ^ flip(r, half.bit_length()), rows), 0:lanes]


def square_turn_kernel(where, *refs):
    terms, (lat_mine, lat_other, top, low, total, turned) = refs[:-6], refs[-6:]
    half = terms[0].shape[2]
    for m in range(3):
        acc = terms[0][0, m].astype(f32)
        for x in terms[1:]:
            if x.shape[1] == 3:
                acc = acc + x[0, m].astype(f32)
            elif m == 2:
                acc = acc + x[0, 3].astype(f32)
        total[m * half : (m + 1) * half, :] = acc
    n = lat_mine.shape[0]
    total[3 * half : 3 * half + n, :] = lat_mine[...].astype(f32) + lat_other[...].astype(f32)
    if 3 * half + n < total.shape[0]:
        total[3 * half + n :, :] = jnp.zeros((total.shape[0] - 3 * half - n, total.shape[1]), f32)
    turn(where, total, turned, top, low)


def kv_turn_kernel(where, *refs):
    terms, (top, low, total, turned) = refs[:-4], refs[-4:]
    acc = terms[0][0].astype(f32)
    for x in terms[1:]:
        acc = acc + x[0].astype(f32)
    total[...] = acc
    turn(where, total, turned, top, low)


def first_blocks(terms):
    return [pl.BlockSpec((1,) + x.shape[1:], lambda i, z=(0,) * x.ndim: z) for x in terms]


def whole_blocks(arrays):
    return [pl.BlockSpec(x.shape, lambda i, z=(0,) * len(x.shape): z) for x in arrays]


def squares(x):
    return jnp.sum(jnp.sum(x * x, 0, keepdims=True), 1, keepdims=True)


def square_end_kernel(where, *refs):
    terms, (extra, wq_squares, mine, other, total_squares, total) = refs[:-6], refs[-6:]
    core = where[0] & 1
    acc = terms[0][0].astype(f32)
    for x in terms[1:]:
        acc = acc + x[0].astype(f32)
    total[...] = acc
    lanes = extra.shape[1]
    total[:, acc.shape[1] - lanes :] += extra[...]
    total_squares[...] = squares(total[...]) + wq_squares[...]
    n = mine.shape[0]
    mine[...] = total[rows_at(core, n), :]
    other[...] = total[rows_at(1 - core, n), :].astype(bf16)


def kv_end_kernel(where, *refs):
    terms, refs = refs[:-9], refs[-9:]
    sq_squares, lat_small, mid_small, in_a, in_b, mine, other, sums, total = refs
    core = where[0] & 1
    acc = terms[0][0].astype(f32)
    for x in terms[1:]:
        acc = acc + x[0].astype(f32)
    total[...] = acc
    n = mine.shape[0]
    mine[...] = total[rows_at(core, n), :]
    other[...] = total[rows_at(1 - core, n), :].astype(bf16)
    sums[...] = jnp.zeros_like(sums)
    sums[0:2, :] = lat_small[...]
    sums[2:4, :] = mid_small[...]
    sums[4:7, 0 : in_a.shape[2]] = in_a[0] + in_b[0]
    sums[7:8, :] = jnp.broadcast_to(squares(acc) + sq_squares[...], (1, sums.shape[1]))


def latent_end_kernel(H, where, *refs):
    terms, (latents, lat_params, extra, small, turned) = refs[:H], refs[H:]
    low = tree_sum([x[...].astype(f32) for x in terms])
    unit, inverse = unit_norm(latents[...])
    once = jnp.where(where[0] == 0, 1.0, 0.0)
    small[0:1, :] = jnp.sum(low * unit, 0, keepdims=True) * once
    small[1:2, :] = jnp.sum(low, 0, keepdims=True) * once
    turned[...] = norm_back(low, unit, inverse, lat_params[0:1, :]).T
    both = turned[rows_at(where[0] >> 1, extra.shape[0]), :]
    n = extra.shape[1]
    extra[...] = jnp.where((where[0] & 1) == 0, both[:, 0:n], both[:, n:])


def update_kernel(where, sums, *refs):
    square, kv, refs = refs[:3], refs[3:6], refs[6:]
    rest, (norm_out, sq_new, sq_moments, kv_new, kv_moments), refs = refs[:7], refs[7:12], refs[12:]
    outs, (sq_held, kv_held, sems) = refs[:8], refs[8:]
    small = sums[0:7, :]
    norm = jnp.sqrt(jnp.sum(jnp.sum(small * small, 1, keepdims=True), 0, keepdims=True) + sums[7:8, 0:1])
    factor = jnp.minimum(1.0, clip_limit / (norm + 1e-06))
    copies = []
    for (weight, state, gradient), held, targets in (
        (square, sq_held, (sq_new, sq_moments)),
        (kv, kv_held, (kv_new, kv_moments)),
    ):
        for m in range(weight.shape[0]):
            results = adam_step(weight[m], state[0, m], state[1, m], state[2, m], gradient[m] * factor)
            for i in range(4):
                held[i, m] = results[i]
                target = targets[i // 2].at[i % 2, m]
                copies.append(pltpu.make_async_copy(held.at[i, m], target, sems.at[len(copies)]))
                copies[-1].start()
    latents, latents_state, lat_grad, lat_params, lat_state, in_params, in_state = rest
    (latents_new, latents_moments, lat_new, lat_moments, in_new, in_moments, lat_clipped, in_clipped) = outs
    norm_out[...] = norm
    latents_new[0], latents_new[1], latents_moments[0], latents_moments[1] = adam_step(
        latents[...], latents_state[0], latents_state[1], latents_state[2], lat_grad[...] * factor
    )
    lat_clipped[...] = sums[0:4, :] * factor
    lat_new[0], lat_new[1], lat_moments[0], lat_moments[1] = adam_step(
        lat_params[...], lat_state[0], lat_state[1], lat_state[2], lat_clipped[...]
    )
    in_clipped[...] = sums[4:7, 0 : in_params.shape[1]] * factor
    results = adam_step(in_params[...], in_state[0], in_state[1], in_state[2], in_clipped[...])
    for i in range(3):
        row = slice(i, i + 1)
        in_new[i, 0:1], in_new[i, 1:2], in_moments[i, 0:1], in_moments[i, 1:2] = (x[row] for x in results)
    for copy in copies:
        copy.wait()


def query_back_kernel(H, where, lat_all, w0, mine, other, wq, wq_squares, *refs):
    outs, (grad_q, whole, term) = refs[:H], refs[H:]
    at = Place(where, H)
    half_wide = mine.shape[0]
    grad_q[rows_at(at.core, half_wide), :] = mine[...]
    grad_q[rows_at(1 - at.core, half_wide), :] = other[...]
    term[...] = dot(grad_q[...], w0[...], 0, 0).astype(bf16)
    for m, out in enumerate(outs):
        out[...] = term[rows_at(at.j ^ m, out.shape[0]), :]
    whole[...] = dot(lat_all[...], grad_q[...], 0, 1)
    wq[...] = whole[rows_at(at.s, wq.shape[0]), :]
    wq_squares[...] = squares(wq[...])


def finish_kernel(where, wq, sq_mine, sq_other, kv_mine, kv_other, square_grad, kv_grad, lat_grad):
    core = where[0] & 1
    half = wq.shape[1] // 2
    mine, other = sq_mine[...], sq_other[...].astype(f32)
    low, high = jnp.where(core == 0, mine, other), jnp.where(core == 0, other, mine)
    square_grad[0] = wq[...]
    for m in range(3):
        square_grad[1 + m, :, 0:half] = low[:, m * half : (m + 1) * half]
        square_grad[1 + m, :, half:] = high[:, m * half : (m + 1) * half]
    kv_grad[core] = kv_mine[...]
    kv_grad[1 - core] = kv_other[...].astype(f32)
    n = lat_grad.shape[0] // 2
    ends = slice(3 * half, 3 * half + n)
    lat_grad[...] = jnp.concatenate([low[:, ends], high[:, ends]], 1).T


def on_device(
    inputs,
    mask_flags,
    out_grad,
    square,
    square_state,
    kv_weights,
    kv_state,
    latents,
    latents_state,
    in_params,
    in_state,
    lat_params,
    lat_state,
):
    L = Links()
    S, H = L.S, L.H
    parity = (L.s >> 1) & 1 if L.paired else 0 * L.s
    go = Order(jnp.stack([L.s, L.j, parity]).astype(jnp.int32))
    rows, d_in = inputs.shape
    parts = SEQ_LEN // rows
    seqs = H // parts
    lat_rows, d_lat = latents.shape
    nlat = lat_rows * H
    wide = square.shape[2]
    half_wide = wide // 2
    d_part, in_part = d_lat // S, d_in // S
    chips = S // 2
    mine_rows = seqs * lat_rows

    def low(*shape):
        return like(shape, bf16)

    def full(*shape):
        return like(shape, f32)

    square_t, kv_t = jnp.swapaxes(square, 1, 2), jnp.swapaxes(kv_weights, 1, 2)
    (lat_low,) = go(lat_kernel, [latents, lat_params], [low(lat_rows, d_lat)], name="lat_norm")
    kv_pair = go(fix(kv_weight_kernel, H), [kv_t], [low(wide, d_in)] * 2, name="kv_weight")
    kv_first = L.first(kv_pair[0])
    lat_near = L.near(lat_low)
    (w0,) = go(
        first_weight_kernel,
        [square_t],
        [low(wide, d_lat)],
        name="first_weight",
        grid=(1,),
        in_specs=[pl.BlockSpec((1, wide, d_lat), lambda i: (0, 0, 0))],
        out_specs=[pl.BlockSpec((wide, d_lat), lambda i: (0, 0))],
    )
    lat_near = [lat_low] + lat_near
    lat_all, query_mine = go(
        fix(query_kernel, H), [*lat_near, w0], [low(nlat, d_lat), low(wide, nlat)], name="query"
    )
    query_near = [query_mine] + L.near(query_mine)
    mask = mask_flags.reshape(rows, 1)
    step = min(rows, 256)
    in_low, in_turned = go(
        token_kernel,
        [inputs, mask, in_params],
        [low(rows, d_in), low(d_in, rows)],
        name="token_norm",
        grid=(rows // step,),
        in_specs=[
            pl.BlockSpec((step, d_in), lambda i: (i, 0)),
            pl.BlockSpec((step, 1), lambda i: (i, 0)),
            pl.BlockSpec(in_params.shape, lambda i: (0, 0)),
        ],
        out_specs=[pl.BlockSpec((step, d_in), lambda i: (i, 0)), pl.BlockSpec((d_in, step), lambda i: (0, i))],
    )
    kv_first = after(kv_first, query_mine)
    kv_mine = [kv_pair[0]] + L.spread(kv_first)
    kv_halves = kv_mine + [kv_pair[1]] + [L.swap_core(x) for x in kv_mine[1:]]
    sq_mine, sq_other = go(
        fix(other_weight_kernel, H),
        [square_t],
        [low(3, half_wide, d_lat)] * 2,
        name="other_weights",
        grid=(3,),
        in_specs=[pl.BlockSpec((1, wide, d_lat), lambda i: (1 + i, 0, 0))],
        out_specs=[pl.BlockSpec((1, half_wide, d_lat), lambda i: (i, 0, 0))] * 2,
    )
    sq_sent = after(sq_mine, *kv_mine[1:], *query_near)
    sq_first = L.first(sq_sent)

    kv, kv_all = go(
        fix(kv_kernel, H),
        [in_turned, *kv_halves],
        [low(2, d_lat, rows), low(2, d_lat, d_in)],
        [pltpu.SemaphoreType.DMA((2 * H,))],
        name="kv",
        in_specs=[VMEM] + [ANY] * (2 * H),
        after=[sq_sent],
    )
    sq_first = after(sq_first, kv)
    sq_rest = L.spread(sq_first)
    sq_early = [L.swap_core(sq_rest[0])] if L.paired else []
    query, *packs = go(
        fix(attention_kernel, H),
        [*query_near, kv],
        [low(d_lat, nlat)] + [low(lat_rows, d_lat + SIDE)] * H,
        [
            pltpu.VMEM((d_lat, nlat), f32),
            pltpu.VMEM((nlat, d_lat + SIDE), bf16),
        ],
        name="attention",
        after=sq_early,
    )
    got = [packs[0]] + [L.swap_hid(packs[m], m) for m in range(1, H)]
    here = after(L.s, *packs)
    sq_old = lax.dynamic_slice_in_dim(square, here * d_part, d_part, 1)
    kv_old = lax.dynamic_slice_in_dim(kv_weights, here * in_part, in_part, 1)
    lat_old = lax.dynamic_slice_in_dim(latents, here * d_part, d_part, 1)
    (kv_turned,) = go(
        kv_turned_kernel,
        [kv_all],
        [low(2, d_in, d_lat)],
        name="kv_turned",
        grid=(2,),
        in_specs=[pl.BlockSpec((1, d_lat, d_in), lambda i: (i, 0, 0))],
        out_specs=[pl.BlockSpec((1, d_in, d_lat), lambda i: (i, 0, 0))],
        after=[sq_old, kv_old, lat_old],
    )
    if L.paired:
        one, two, three = sq_rest
        three = after(three, *got, kv_turned)
        three_other = L.swap_core(three)
        two = after(two, three_other)
        sq_halves = [sq_mine, one, two, three, sq_other, *sq_early, L.swap_core(two), three_other]
    else:
        sq_rest = after(sq_rest, *got, kv_turned)
        sq_halves = [sq_mine] + sq_rest + [sq_other] + [L.swap_core(x) for x in sq_rest]

    latents_out, acts, mid_small, res_mine, res_send, *backs = go(
        fix(latent_kernel, H, parts),
        [*got, latents, out_grad, lat_params, *sq_halves],
        [full(mine_rows, d_lat), low(6, mine_rows, d_lat), full(2, d_lat)]
        + [low(lat_rows // 2, d_lat)] * 2
        + [low(lat_rows, d_lat + SIDE)] * H,
        [
            pltpu.VMEM((3, d_lat, d_lat), bf16),
            pltpu.SemaphoreType.DMA((3, 2 * H)),
            pltpu.VMEM((H, lat_rows, d_lat + SIDE), bf16),
            pltpu.VMEM((mine_rows, d_lat), f32),
            pltpu.VMEM((seqs, lat_rows, d_lat + SIDE), bf16),
            pltpu.VMEM((lat_rows, d_lat), bf16),
        ],
        name="latent",
        in_specs=[VMEM] * (H + 3) + [ANY] * (2 * H),
    )
    back = [backs[0]] + [L.swap_hid(backs[m], m) for m in range(1, H)]

    sq_slots = go(
        fix(square_grad_kernel, H),
        [acts, L.swap_core(acts)],
        [low(1, x, half_wide, d_lat) for x in ((3, 3, 4, 2) if L.paired else (3,) * H)],
        [pltpu.VMEM((3, d_lat, 2 * mine_rows), bf16), pltpu.VMEM((3, 2 * mine_rows, d_lat), bf16)],
        name="square_grad",
    )
    if L.paired:
        sq = Slots(L, go, [sq_slots[0], sq_slots[1], sq_slots[3], sq_slots[2]], "square")
        sq.slots[0].append(sq.early[0])
    else:
        sq = Slots(L, go, sq_slots, "square")
    res_other = L.swap_core(res_send)
    in_other = L.swap_core(after(in_low, sq_slots[0], res_other))

    gkv_mine, gkv_send, gq_keep, gq_send = go(
        fix(attention_back_kernel, H),
        [query, *back, kv],
        [low(d_lat, rows)] * 2 + [low(H, half_wide, nlat)] * 2,
        [
            pltpu.VMEM((nlat, d_lat + SIDE), bf16),
            pltpu.VMEM((d_lat, nlat), bf16),
            pltpu.VMEM((d_lat, nlat), bf16),
            pltpu.VMEM((2, d_lat, rows), bf16),
        ],
        name="attention_back",
        after=[res_other],
    )
    gkv_got = L.swap_core(after(gkv_send, *sq.early))
    gq_got = L.swap_core(gq_send)

    in_sums = []
    inputs_grad = None
    block = min(rows // 2, 256)

    def token_grad():
        nonlocal inputs_grad
        first = len(in_sums) * (rows // 2 // block)
        inputs_grad, sums = go(
            token_grad_kernel,
            [inputs, mask, in_params, gkv_mine, gkv_send, kv_turned],
            [full(rows, d_in), full(1, 3, d_in)],
            name="token_grad_%d" % len(in_sums),
            grid=(rows // 2 // block,),
            in_specs=[
                pl.BlockSpec((block, d_in), lambda g: (first + g, 0)),
                pl.BlockSpec((block, 1), lambda g: (first + g, 0)),
                pl.BlockSpec(in_params.shape, lambda g: (0, 0)),
                pl.BlockSpec((d_lat, block), lambda g: (0, first + g)),
                pl.BlockSpec((d_lat, block), lambda g: (0, first + g)),
                pl.BlockSpec(kv_turned.shape, lambda g: (0, 0, 0)),
            ],
            out_specs=[
                pl.BlockSpec((block, d_in), lambda g: (first + g, 0)),
                pl.BlockSpec((1, 3, d_in), lambda g: (0, 0, 0)),
            ],
            onto=inputs_grad,
        )
        in_sums.append(sums)

    gq_all = go(query_core_kernel, [gq_keep, gq_got], [low(half_wide, nlat)] * H, name="query_core", after=[in_other])
    gq_near = [L.swap_hid(gq_all[m], m) for m in range(1, H)]
    token_grad()
    sq.hold(*gq_near)
    if L.paired:
        (sending,) = go(square_step_kernel, sq.slots[1], [low(1, 3, half_wide, d_lat)], name="square_step")
        sq.slots[0].append(L.swap_step(sending, 0))
        sq.steps = []
    else:
        sq.step()
    gq_mine = go.tree([gq_all[0]] + gq_near, "query_hid")
    gq_chips = L.near_chips(gq_mine)
    kv_slots = go(
        fix(kv_grad_kernel, H),
        [gkv_mine, gkv_got, in_low, in_other],
        [low(1, wide, d_in)] * H,
        [pltpu.VMEM((d_lat, d_in), bf16)],
        name="kv_grad",
    )
    gq_mine = go.tree([gq_mine] + gq_chips, "query_chips")
    gq_other = L.swap_core(gq_mine)
    sq.terms[-1] = after(sq.terms[-1], gq_mine)
    kv_sums = Slots(L, go, kv_slots, "kv", sq.terms[-1])

    lanes = 3 * half_wide + lat_rows // 2
    padded = -(-lanes // 128) * 128

    def turn_to_chips(kernel, terms, extra, n, lanes, padded, name):
        d = terms[0].shape[-1]
        out = [low(chips // 2, n, lanes)] * 2
        return go(
            kernel,
            [*terms, *extra],
            out,
            [pltpu.VMEM((padded, d), f32), pltpu.VMEM((d, padded), bf16)],
            name=name,
            grid=(1,),
            in_specs=first_blocks(terms) + whole_blocks(extra),
            out_specs=whole_blocks(out),
        )

    n = L.sb - 1

    def chip_step(x, i):
        return L.swap_seq(x, 2 << (n - 1 - i))

    def end(kernel, terms, extra, n, lanes, more, name, after=()):
        outs = [full(n, lanes), low(n, lanes)] + more
        return go(
            kernel,
            [*terms, *extra],
            outs,
            [pltpu.VMEM((2 * n, lanes), f32)],
            name=name,
            grid=(1,),
            in_specs=first_blocks(terms) + whole_blocks(extra),
            out_specs=whole_blocks(outs),
            after=after,
        )

    sq_top, sq_low = turn_to_chips(
        square_turn_kernel, sq.terms, [res_mine, res_other], 2 * d_part, lanes, padded, "square_turn"
    )
    sq_chips = Halving(go, [sq_top], [sq_low], n, chip_step, "square_chip")
    sq_chips.start()
    kv_sums.step()
    token_grad()
    kv_top, kv_low = turn_to_chips(kv_turn_kernel, kv_sums.terms, [], 2 * in_part, wide, wide, "kv_turn")
    kv_chips = Halving(go, [kv_top], [kv_low], n, chip_step, "kv_chip")
    kv_chips.start()
    sq_chips.step()
    wq_part, wq_squares, *lat_blocks = go(
        fix(query_back_kernel, H),
        [lat_all, w0, gq_mine, gq_other],
        [full(d_part, wide), full(1, 1)] + [low(lat_rows, d_lat)] * H,
        [pltpu.VMEM((wide, nlat), bf16), pltpu.VMEM((d_lat, wide), f32), pltpu.VMEM((nlat, d_lat), bf16)],
        name="query_back",
    )
    lat_near = [L.swap_hid(lat_blocks[m], m) for m in range(1, H)]
    kv_chips.step()
    lat_extra, lat_small = go(
        fix(latent_end_kernel, H),
        [lat_blocks[0], *lat_near, latents, lat_params],
        [full(2 * d_part, lat_rows // 2), full(2, d_lat)],
        [pltpu.VMEM((d_lat, lat_rows), f32)],
        name="latent_end",
    )
    for _ in range(n - 2):
        sq_chips.step()
        kv_chips.step()
    sq_mine, sq_send, sq_squares = end(
        square_end_kernel,
        sq_chips.terms,
        [lat_extra, wq_squares],
        d_part,
        lanes,
        [full(1, 1)],
        "square_end",
    )
    sq_other = L.swap_core(sq_send)
    kv_mine, kv_send, sums = end(
        kv_end_kernel,
        kv_chips.terms,
        [sq_squares, lat_small, mid_small, *in_sums],
        in_part,
        wide,
        [full(8, d_lat)],
        "kv_end",
    )
    kv_other = L.swap_core(kv_send)

    square_grad, kv_grad, lat_grad = go(
        finish_kernel,
        [wq_part, sq_mine, sq_other, kv_mine, kv_other],
        [full(4, d_part, wide), full(2, in_part, wide), full(lat_rows, d_part)],
        name="finish",
    )
    sums = L.sum_all(sums, square_grad)
    pair = [full(3, 2, d_in)] * 2
    rest = [lat_old, latents_state, lat_grad, lat_params, lat_state, in_params, in_state]
    outs = [full(2, *lat_old.shape)] * 2 + [full(2, *lat_params.shape)] * 2 + pair
    outs += [full(*lat_params.shape), full(*in_params.shape)]
    results = go(
        update_kernel,
        [sums, sq_old, square_state, square_grad, kv_old, kv_state, kv_grad, *rest],
        [full(1, 1)] + [full(2, *sq_old.shape)] * 2 + [full(2, *kv_old.shape)] * 2 + outs,
        [
            pltpu.VMEM((4,) + sq_old.shape, f32),
            pltpu.VMEM((4,) + kv_old.shape, f32),
            pltpu.SemaphoreType.DMA((4 * (sq_old.shape[0] + kv_old.shape[0]),)),
        ],
        name="update",
        out_specs=[VMEM] + [ANY] * 4 + [VMEM] * len(outs),
    )
    (grad_norm, square_new, square_moments, kv_new, kv_moments, latents_new, latents_moments) = results[:7]
    (lat_new, lat_moments, in_new, in_moments, lat_clipped, in_clipped) = results[7:]
    grad_norm = grad_norm[0, 0]
    in_new, in_moments = jnp.swapaxes(in_new, 0, 1), jnp.swapaxes(in_moments, 0, 1)
    return (
        latents_out.reshape(seqs, lat_rows, d_lat),
        inputs_grad,
        grad_norm,
        square_new,
        square_moments,
        kv_new,
        kv_moments,
        latents_new,
        latents_moments,
        in_new,
        in_moments,
        lat_new,
        lat_moments,
        in_clipped,
        lat_clipped,
    )


def solution(mesh):
    return jax.shard_map(
        on_device,
        mesh=mesh,
        in_specs=(
            P(("seq", "hid"), None),
            P(("seq", "hid")),
            P("seq", "hid", None),
            P(None, None, "hid"),
            P(None, None, "seq", "hid"),
            P(None, None, "hid"),
            P(None, None, "seq", "hid"),
            P("hid", None),
            P(None, "hid", "seq"),
            P(),
            P(),
            P(),
            P(),
        ),
        out_specs=(
            P("seq", "hid", None),
            P(("seq", "hid"), None),
            P(),
            P(None, None, "seq", "hid"),
            P(None, None, "seq", "hid"),
            P(None, None, "seq", "hid"),
            P(None, None, "seq", "hid"),
            P(None, "hid", "seq"),
            P(None, "hid", "seq"),
            P(),
            P(),
            P(),
            P(),
            P(),
            P(),
        ),
        check_vma=False,
    )
```
